32 devices in a mesh: groups: 2 (over y), space: 4 (over z), chan: 2 (over x), pipe: 2 (over core).
Axes of the slice: x: 2, y: 2, z: 4, core: 2. Of those that a mesh axis runs over, the one named last changes fastest.
Arguments:
- grid_latent: bfloat16 [32768, 512], P(('groups', 'space', 'pipe')), parts along dimension 0, may hold values from -6 to 6
- g2m_face: int32 [32768, 1], P(('groups', 'space', 'pipe')), parts along dimension 0, may hold values from 0 to 3; in each aligned block of 2048 rows (0 to 2047, 2048 to 4095, ...) at most 1024 rows name the same one
- g2m_node: int32 [32768], P(('groups', 'space', 'pipe')), parts along dimension 0, may hold values from 0 to 511
- mesh_latent: bfloat16 [4096, 512], P(('groups', 'space'), 'chan'), parts along dimension 0, may hold values from -6 to 6
- mesh_links: int32 [4096, 6], P(('groups', 'space'), 'pipe'), parts along dimension 0, may hold values from 0 to 2047, as said below
- w_enc: bfloat16 [512, 512], replicated, may hold values from -0.25 to 0.25
- w_send: bfloat16 [2, 512, 512], replicated, may hold values from -0.25 to 0.25
- w_recv: bfloat16 [2, 512, 512], replicated, may hold values from -0.25 to 0.25
- w_node: bfloat16 [2, 512, 512], replicated, may hold values from -0.25 to 0.25
- w_dec: bfloat16 [512, 512], replicated, may hold values from -0.25 to 0.25
- cotangent: bfloat16 [32768, 512], P(('groups', 'space', 'pipe'), 'chan'), parts along dimension 0, may hold values from -6 to 6
Outputs:
- mixed: bfloat16 [32768, 512], P(('groups', 'space', 'pipe'), 'chan'), parts along dimension 0
- grad_grid: bfloat16 [32768, 512], P(('groups', 'space', 'pipe'), 'chan'), parts along dimension 0
- grad_mesh: float32 [4096, 512], P(('groups', 'space'), 'chan'), parts along dimension 0
- grad_w_enc: float32 [1024, 512], P('groups', 'chan'), parts along dimension 0
- grad_w_send: float32 [4, 512, 512], P('groups', None, 'chan'), parts along dimension 0
- grad_w_recv: float32 [4, 512, 512], P('groups', None, 'chan'), parts along dimension 0
- grad_w_node: float32 [4, 512, 512], P('groups', None, 'chan'), parts along dimension 0
- grad_w_dec: float32 [1024, 512], P('groups', 'chan'), parts along dimension 0
The draws below stay inside these ranges and needn't reach their ends.
There are 2 independent parts, one for each index of `groups`. The reference program is written for one: setup_inputs(seed, part) draws one part's arguments, and reference() takes and returns one part's arrays. A program takes and returns all parts, laid end to end along the dimension named above; an argument that names none is the same for every part. Nothing has to cross between parts.
Inputs may be any that keep to these rules, and one draw needn't show every extreme that they name: `g2m_face`: in each aligned block of 2048 rows (the rows of one device) no face block is named by more than 1024 rows, and in some such block a face block is named by exactly 1024 rows. `mesh_links`: each entry names a mesh node in the row's own block of 512 rows or in one of the two blocks beside it, the first and the last block counting as beside each other.
All inputs are finite; a program needn't handle non-finite values.
Results may differ from the reference program's by a relative error of at most 0.014.
Values may be sent and summed in bfloat16 or wider, within the bound.
No kernel may reach another device: no remote copies, remote signals or barrier semaphores. Data moves between devices by JAX's collectives and lax.ppermute only.
A program may use at most 128 MiB of HBM per device.

```python
import math
import jax
import jax.numpy as jnp
import numpy as np
from jax import lax

WIDTH = 512
GRID_DEV = 2048
MESH_DEV = 512
NBRS = 6
LAYERS = 2
CAP = 1024
GRID = 16384
MESH = 2048
N_SPACE = 4
N_PIPE = 2


def draw_mesh_links(key, part):
    key = jax.random.fold_in(key, 7)
    key_step, key_row = jax.random.split(key)
    block_count = MESH // MESH_DEV
    own_block = jnp.arange(MESH, dtype=jnp.int32) // MESH_DEV
    block_step = jax.random.randint(key_step, (MESH, NBRS), -1, 2, dtype=jnp.int32)
    local_row = jax.random.randint(key_row, (MESH, NBRS), 0, MESH_DEV, dtype=jnp.int32)
    return (own_block[:, None] + block_step) % block_count * MESH_DEV + local_row


def with_ends(entries, stream_key, smallest, top_value):
    index_at = [jax.random.randint(jax.random.fold_in(stream_key, axis), (), 0, length) for axis, length in enumerate(entries.shape)]
    widest = entries.shape.index(max(entries.shape))
    neighbour = index_at[:widest] + [(index_at[widest] + 1) % entries.shape[widest]] + index_at[widest + 1:]
    return entries.at[tuple(index_at)].set(smallest).at[tuple(neighbour)].set(top_value)


def block_levels(stream_key, extent, pieces, smallest, high):
    factor_of = 1.0
    for dim, parts in pieces:
        draws = jax.random.uniform(jax.random.fold_in(jax.random.fold_in(stream_key, 6), dim), (parts,), jnp.float32, smallest / len(pieces), high / len(pieces))
        factor_of = factor_of * jnp.repeat(jnp.exp(draws), extent[dim] // parts).reshape((-1,) + (1,) * (len(extent) - 1 - dim))
    return factor_of


def deal_out(stream_key, own, number, rows, number_of, top, most, slope):
    order = jax.random.permutation(stream_key, number_of)
    heavy_load, ordinary = shares(number_of, rows * top, most, slope, True), shares(number_of, rows * top, most, slope, False)
    places = jnp.arange(number_of)

    def named(sizes, offset_by):
        used = int((sizes > 0).sum())
        fixed = max(1, used // 4)
        passed = fixed + (places - fixed + offset_by * (used - fixed)) % max(1, number_of - fixed)
        return jnp.zeros((number_of,), jnp.int32).at[order[jnp.where(places < fixed, places, passed)]].set(jnp.asarray(sizes, jnp.int32))

    sizes = jnp.where(number % 4 == 0, named(heavy_load, number // 4), named(ordinary, number - number // 4 - 1))
    mixed = jax.random.permutation(jax.random.fold_in(own, 3), number_of)
    source_of, receiver = mixed[0:number_of // 2 * 2:2], mixed[1:number_of // 2 * 2:2]
    room = jnp.minimum(sizes[source_of] - 1, most - sizes[receiver]) // 2
    room = jnp.where((source_of == order[0]) | (receiver == order[0]) | (sizes[receiver] == 0), 0, jnp.maximum(room, 0))
    passed = jax.random.randint(jax.random.fold_in(own, 4), (number_of // 2,), 0, 1 << 20) % (room + 1)
    sizes = sizes.at[source_of].add(-passed).at[receiver].add(passed)
    members = jnp.searchsorted(jnp.cumsum(sizes), jnp.arange(rows * top), side="right").astype(jnp.int32)
    listing = members.reshape(top, rows).T
    listing = listing[jax.random.permutation(jax.random.fold_in(own, 1), rows)]
    offset_by = jax.random.randint(jax.random.fold_in(own, 2), (rows, 1), 0, top)
    return jnp.take_along_axis(listing, (jnp.arange(top)[None, :] + offset_by) % top, axis=1)


def shares(number_of, total, bound, slope, full):
    weights = [(1 << 20) // math.isqrt(grade ** slope) + 1 for grade in range(1, number_of + 1)]
    largest = bound if full else min(bound, max(-(-total // number_of), total * weights[0] // sum(weights)))
    least = 1 if total - largest >= number_of - 1 else 0
    holding, rest = [largest] + [least] * (number_of - 1), total - largest - least * (number_of - 1)
    while rest > 0:
        candidates = [i for i in range(1, number_of) if holding[i] < largest] or [i for i in range(1, number_of) if holding[i] < bound]
        whole, budget = sum([weights[i] for i in candidates]), rest
        for i in candidates:
            extra = min(bound - holding[i], max(1, budget * weights[i] // whole), rest)
            holding[i] = holding[i] + extra
            rest = rest - extra
    return np.array(holding)


def normal_values(key, extent, spread, reach, cuts=(), kind=jnp.bfloat16):
    drawn = jax.random.normal(key, extent, jnp.float32) * spread
    if len(cuts) > 0:
        drawn = block_levels(key, extent, cuts, -0.22, 0.18) * drawn
    return jnp.clip(drawn, min=-reach, max=reach).astype(kind)


def setup_inputs(seed: int = 0, part: int = 0) -> dict:
    key_list = jax.random.split(jax.random.key(seed), 12)
    part_splits = jax.random.split(jax.random.fold_in(key_list[11], part), 12)
    grid_latent = normal_values(part_splits[0], (GRID, WIDTH), 1.0, 6.0, ((0, 8),))
    g2m_face_keys = jax.random.split(jax.random.fold_in(part_splits[1], 1), GRID // GRID_DEV)
    g2m_face_turns = jax.random.permutation(jax.random.fold_in(part_splits[1], 3), GRID // GRID_DEV)
    g2m_face = jax.vmap(lambda own, number: deal_out(jax.random.fold_in(part_splits[1], 2), own, number, GRID_DEV, N_SPACE, 1, CAP, 2))(g2m_face_keys, g2m_face_turns).reshape((GRID, 1))
    g2m_node = with_ends(jax.random.randint(part_splits[2], (GRID,), 0, MESH_DEV), jax.random.fold_in(part_splits[2], 1), 0, MESH_DEV - 1).astype(jnp.int32)
    mesh_latent = normal_values(part_splits[3], (MESH, WIDTH), 1.0, 6.0, ((0, 4), (1, 2)))
    mesh_links = draw_mesh_links(jax.random.fold_in(jax.random.fold_in(key_list[11], part), 71), part)
    w_enc = normal_values(key_list[5], (WIDTH, WIDTH), WIDTH ** -0.5, 0.25)
    w_send = normal_values(key_list[6], (LAYERS, WIDTH, WIDTH), WIDTH ** -0.5, 0.25)
    w_recv = normal_values(key_list[7], (LAYERS, WIDTH, WIDTH), WIDTH ** -0.5, 0.25)
    w_node = normal_values(key_list[8], (LAYERS, WIDTH, WIDTH), WIDTH ** -0.5, 0.25)
    w_dec = normal_values(key_list[9], (WIDTH, WIDTH), WIDTH ** -0.5, 0.25)
    cotangent = normal_values(part_splits[10], (GRID, WIDTH), 1.0, 6.0, ((0, 8), (1, 2)))
    return {"grid_latent": grid_latent, "g2m_face": g2m_face, "g2m_node": g2m_node, "mesh_latent": mesh_latent, "mesh_links": mesh_links, "w_enc": w_enc, "w_send": w_send, "w_recv": w_recv, "w_node": w_node, "w_dec": w_dec, "cotangent": cotangent}


def silu_slope(values):
    sigmoid_v = jax.nn.sigmoid(values)
    return sigmoid_v * (1.0 + values * (1.0 - sigmoid_v))


def dot_plain(left, right):
    return jnp.dot(left, right, preferred_element_type=jnp.float32)


def dot_back(left, right):
    return lax.dot_general(left, right, (((1,), (1,)), ((), ())), preferred_element_type=jnp.float32)


def dot_left(left, right):
    return lax.dot_general(left, right, (((0,), (0,)), ((), ())), preferred_element_type=jnp.float32)


def reference(grid_latent, g2m_face, g2m_node, mesh_latent, mesh_links, w_enc, w_send, w_recv, w_node, w_dec, cotangent):
    target = (g2m_face[:, 0] * MESH_DEV + g2m_node).astype(jnp.int32)
    mix_scale = (MESH_DEV / (GRID_DEV * N_PIPE)) ** 0.5
    node_count = MESH_DEV * N_SPACE
    z_enc = dot_plain(grid_latent, w_enc)
    enc_out = jax.nn.silu(z_enc).astype(jnp.bfloat16)
    agg_first = jax.ops.segment_sum(enc_out.astype(jnp.float32), target, node_count)
    mesh_state = mesh_latent.astype(jnp.float32) + mix_scale * agg_first
    stored = []
    for step_index in range(LAYERS):
        state_bf = mesh_state.astype(jnp.bfloat16)
        send_p = dot_plain(state_bf, w_send[step_index]).astype(jnp.bfloat16)
        recv_p = dot_plain(state_bf, w_recv[step_index])
        pre_edge = send_p[mesh_links].astype(jnp.float32) + recv_p[:, None, :]
        agg_b = (jnp.sum(jax.nn.silu(pre_edge), axis=1) / NBRS).astype(jnp.bfloat16)
        mesh_state = mesh_state + dot_plain(agg_b, w_node[step_index])
        stored.append((state_bf, pre_edge, agg_b))
    last_b = mesh_state.astype(jnp.bfloat16)
    z_dec = dot_plain(last_b, w_dec)
    dec_out = jax.nn.silu(z_dec).astype(jnp.bfloat16)
    mixed = (grid_latent.astype(jnp.float32) + dec_out[target].astype(jnp.float32)).astype(jnp.bfloat16)

    cot_full = cotangent.astype(jnp.float32)
    back_dec = jax.ops.segment_sum(cot_full, target, node_count)
    dec_grad = (back_dec * silu_slope(z_dec)).astype(jnp.bfloat16)
    grad_w_dec = dot_left(last_b, dec_grad)
    grad_state = dot_back(dec_grad, w_dec)
    send_list = [None] * LAYERS
    recv_list = [None] * LAYERS
    node_list = [None] * LAYERS
    for step_index in reversed(range(LAYERS)):
        state_bf, pre_edge, agg_b = stored[step_index]
        grad_b = grad_state.astype(jnp.bfloat16)
        node_list[step_index] = dot_left(agg_b, grad_b)
        back_agg = dot_back(grad_b, w_node[step_index])
        back_pre = (back_agg / NBRS)[:, None, :] * silu_slope(pre_edge)
        recv_grad = jnp.sum(back_pre, axis=1).astype(jnp.bfloat16)
        send_grad = jax.ops.segment_sum(back_pre.reshape(-1, WIDTH), mesh_links.reshape(-1), node_count).astype(jnp.bfloat16)
        send_list[step_index] = dot_left(state_bf, send_grad)
        recv_list[step_index] = dot_left(state_bf, recv_grad)
        grad_state = grad_state + dot_back(send_grad, w_send[step_index]) + dot_back(recv_grad, w_recv[step_index])
    grad_mesh = grad_state
    enc_back = (mix_scale * grad_state).astype(jnp.bfloat16)
    enc_grad = (enc_back[target].astype(jnp.float32) * silu_slope(z_enc)).astype(jnp.bfloat16)
    grad_w_enc = dot_left(grid_latent, enc_grad)
    grad_grid = (cot_full + dot_back(enc_grad, w_enc)).astype(jnp.bfloat16)
    return (mixed, grad_grid, grad_mesh, grad_w_enc, jnp.stack(send_list), jnp.stack(recv_list), jnp.stack(node_list), grad_w_dec)
```

```python
import functools

import jax
import jax.numpy as jnp
from jax import lax
from jax.experimental import pallas as pl
from jax.experimental.pallas import tpu as pltpu
from jax.sharding import PartitionSpec as P

F32, BF16 = jnp.float32, jnp.bfloat16
FACE_AXES = ("chan", "pipe")


def shifted(block, axis, distance):
    count = lax.axis_size(axis)
    return lax.ppermute(block, axis, [((i + distance) % count, i) for i in range(count)])


def dot_plain(left, right):
    return jnp.dot(left, right, preferred_element_type=F32)


def dot_back(left, right):
    return lax.dot_general(left, right, (((1,), (1,)), ((), ())), preferred_element_type=F32)


def dot_left(left, right):
    return lax.dot_general(left, right, (((0,), (0,)), ((), ())), preferred_element_type=F32)


def slope_of(values, sigmoid_v):
    return sigmoid_v * (1.0 + values * (1.0 - sigmoid_v))


def one_hot(rows, ids):
    return jnp.where(rows == ids, 1.0, 0.0).astype(BF16)


def pick(values, index, width):
    out = values[:, :width]
    for j in range(1, values.shape[1] // width):
        out = jnp.where(index == j, values[:, j * width : (j + 1) * width], out)
    return out


def widen(parts):
    return jnp.concatenate([parts[j] for j in range(parts.shape[0])], axis=1)


def whole(shape):
    return pl.BlockSpec(shape, lambda i, sr: (0,) * len(shape))


def layer_of(shape, layer):
    return pl.BlockSpec((None,) + shape[1:], lambda i, sr: (layer, 0, 0))


def run(body, scalars, args, outs, scratch=(), flops=0, specs=None):
    specs = specs or {}
    return pl.pallas_call(
        body,
        out_shape=[jax.ShapeDtypeStruct(s, d) for s, d in outs],
        grid_spec=pltpu.PrefetchScalarGridSpec(
            num_scalar_prefetch=1,
            grid=(1,),
            in_specs=[specs.get(i, whole(a.shape)) for i, a in enumerate(args)],
            out_specs=[whole(s) for s, _ in outs],
            scratch_shapes=list(scratch),
        ),
        compiler_params=pltpu.CompilerParams(vmem_limit_bytes=56 * 1024 * 1024),
        cost_estimate=pl.CostEstimate(flops=flops, bytes_accessed=0, transcendentals=0),
    )(scalars, *args)


def rows_at(index, size):
    return pl.ds(pl.multiple_of(index * size, size), size)


def sum_by_node(sr, target, values, keep, give):
    mesh_all, width = keep.shape
    grid_rows = values.shape[0]
    size = 256

    def step(i, carry):
        ids = lax.broadcasted_iota(jnp.int32, (size, grid_rows), 0) + i * size
        total = dot_plain(one_hot(ids, target[...]), values[...])
        low, high = total[:, :width], total[:, width:]
        first = sr[1] == 0
        keep[rows_at(i, size), :] = jnp.where(first, low, high).astype(BF16)
        give[rows_at(i, size), :] = jnp.where(first, high, low).astype(BF16)
        return carry

    lax.fori_loop(0, mesh_all // size, step, 0)


def encode_body(sr, x, w, target, keep, give, enc):
    size = 512

    def step(i, carry):
        z = dot_plain(x[rows_at(i, size), :], w[...])
        enc[rows_at(i, size), :] = (z * jax.nn.sigmoid(z)).astype(BF16)
        return carry

    lax.fori_loop(0, x.shape[0] // size, step, 0)
    sum_by_node(sr, target, enc, keep, give)


def project(sr, state_b, w_send, w_recv, send_p, recv_p):
    width = send_p.shape[1]
    send_p[...] = dot_plain(state_b, pick(w_send[...], sr[2], width)).astype(BF16)
    recv_p[...] = dot_plain(state_b, pick(w_recv[...], sr[2], width))


def first_body(sr, parts, w_send, w_recv, state_b, send_p, recv_p):
    wide = widen(parts)
    state_b[...] = wide
    project(sr, wide, w_send, w_recv, send_p, recv_p)


def next_body(sr, agg, state, w_node, w_send, w_recv, agg_wide, new_state, state_b, send_p, recv_p):
    wide = widen(agg)
    agg_wide[...] = wide
    total = state[...].astype(F32) + dot_plain(wide, w_node[...])
    new_state[...] = total
    narrow = total.astype(BF16)
    state_b[...] = narrow
    project(sr, narrow, w_send, w_recv, send_p, recv_p)


def edge_body(sr, below, own, above, recv_p, spot, agg, slope, halo):
    mesh_rows = own.shape[0]
    halo[:mesh_rows, :] = below[...]
    halo[mesh_rows : 2 * mesh_rows, :] = own[...]
    halo[2 * mesh_rows :, :] = above[...]
    ids = lax.broadcasted_iota(jnp.int32, (mesh_rows, 3 * mesh_rows), 1)
    count = slope.shape[0]
    total = jnp.zeros(agg.shape, F32)
    for k in range(count):
        pre = dot_plain(one_hot(ids, spot[:, k : k + 1]), halo[...]) + recv_p[...]
        sigmoid_v = jax.nn.sigmoid(pre)
        total = total + pre * sigmoid_v
        slope[k] = slope_of(pre, sigmoid_v)
    agg[...] = (total / count).astype(BF16)


def edge_back(sr, grad_b, w_node, slope, spot, recv_grad, below, own, above, back):
    mesh_rows, width = recv_grad.shape
    count = slope.shape[0]
    w_rows = w_node[rows_at(sr[2], width), :]
    back_agg = dot_back(grad_b, w_rows) / count
    total = jnp.zeros(recv_grad.shape, F32)
    for k in range(count):
        term = back_agg * slope[k]
        total = total + term
        back[k * mesh_rows : (k + 1) * mesh_rows, :] = term.astype(BF16)
    recv_grad[...] = total.astype(BF16)
    size = 256
    ids = lax.broadcasted_iota(jnp.int32, (size, count * mesh_rows), 0)
    for place, out in enumerate((below, own, above)):
        for half in range(mesh_rows // size):
            first = place * mesh_rows + half * size
            spread = dot_plain(one_hot(ids + first, spot[...]), back[...])
            out[half * size : (half + 1) * size, :] = spread.astype(out.dtype)


def turn_body(
    sr, agg, state, w_node, w_dec, back_dec, slope, spot,
    agg_wide, last_b, dec_part, dec_grad, grad, grad_b, recv_grad, below, own, above, back,
):
    wide = widen(agg)
    agg_wide[...] = wide
    last = (state[...] + dot_plain(wide, w_node[...])).astype(BF16)
    last_b[...] = last
    z_dec = dot_plain(last, w_dec[...])
    sigmoid_v = jax.nn.sigmoid(z_dec)
    dec_part[...] = pick(z_dec * sigmoid_v, sr[2], dec_part.shape[1]).astype(BF16)
    back_wide = widen(back_dec).astype(F32)
    down = (back_wide * slope_of(z_dec, sigmoid_v)).astype(BF16)
    dec_grad[...] = down
    total = dot_back(down, w_dec[...])
    grad[...] = total
    narrow = total.astype(BF16)
    grad_b[...] = narrow
    edge_back(sr, narrow, w_node, slope, spot, recv_grad, below, own, above, back)


def through(grad, send_wide, recv_wide, w_send, w_recv):
    return grad[...] + dot_back(send_wide, w_send[...]) + dot_back(recv_wide, w_recv[...])


def back_body(
    sr, grad, send_parts, recv_parts, w_send, w_recv, w_node, slope, spot,
    send_out, recv_out, new_grad, grad_b, recv_grad, below, own, above, back,
):
    send_wide, recv_wide = widen(send_parts), widen(recv_parts)
    send_out[...] = send_wide
    recv_out[...] = recv_wide
    total = through(grad, send_wide, recv_wide, w_send, w_recv)
    new_grad[...] = total
    narrow = total.astype(BF16)
    grad_b[...] = narrow
    edge_back(sr, narrow, w_node, slope, spot, recv_grad, below, own, above, back)


def last_body(mix_scale, sr, grad, send_parts, recv_parts, w_send, w_recv, send_out, recv_out, grad_mesh, enc_part):
    send_wide, recv_wide = widen(send_parts), widen(recv_parts)
    send_out[...] = send_wide
    recv_out[...] = recv_wide
    total = through(grad, send_wide, recv_wide, w_send, w_recv)
    grad_mesh[...] = pick(total, sr[0], grad_mesh.shape[1])
    enc_part[...] = (mix_scale * pick(total, sr[2], enc_part.shape[1])).astype(BF16)


def two_halves(sr, mine, other):
    first = sr[1] == 0
    return (
        jnp.where(first, mine[...], other[...]),
        jnp.where(first, other[...], mine[...]),
    )


def fill_table(sr, table, column, mine, other):
    low, high = two_halves(sr, mine, other)
    width = low.shape[1]
    table[:, column : column + width] = low
    table[:, column + width : column + 2 * width] = high


def mixed_body(sr, x, target, mine, other, mixed, table):
    fill_table(sr, table, 0, mine, other)
    size = 256

    def step(i, carry):
        at = rows_at(i, size)
        ids = lax.broadcasted_iota(jnp.int32, (size, table.shape[0]), 1)
        got = dot_plain(one_hot(ids, target[at, :]), table[...])
        mixed[at, :] = (x[at, :].astype(F32) + got).astype(BF16)
        return carry

    lax.fori_loop(0, x.shape[0] // size, step, 0)


def enc_own_body(sr, x, w, target, mine, other, enc_grad, grad_keep, grad_give, table, total):
    fill_table(sr, table, 0, mine, other)
    size = 256
    total[...] = jnp.zeros(total.shape, F32)

    def step(i, carry):
        at = rows_at(i, size)
        ids = lax.broadcasted_iota(jnp.int32, (size, table.shape[0]), 1)
        got = dot_plain(one_hot(ids, target[at, :]), table[...])
        z = dot_plain(x[at, :], w[...])
        down = (got * slope_of(z, jax.nn.sigmoid(z))).astype(BF16)
        enc_grad[at, :] = down
        total[...] += dot_left(x[at, :], down)
        return carry

    lax.fori_loop(0, x.shape[0] // size, step, 0)
    half = grad_keep.shape[0]
    grad_keep[...] = total[rows_at(sr[1], half), :]
    grad_give[...] = total[rows_at(1 - sr[1], half), :].astype(BF16)


def enc_other_body(count, sr, x, target, cotangent, enc_grad, w_own, w_own_rows, *rest):
    w_cols, w_rows = rest[:count], rest[count : 2 * count]
    mine, other = rest[2 * count : 3 * count], rest[3 * count : 4 * count]
    grad_grid, table = rest[4 * count :]
    narrow = cotangent.shape[1]
    for j in range(count):
        fill_table(sr, table, j * narrow, mine[j], other[j])
    size = 256

    def step(i, carry):
        at = rows_at(i, size)
        ids = lax.broadcasted_iota(jnp.int32, (size, table.shape[0]), 1)
        got = dot_plain(one_hot(ids, target[at, :]), table[...])
        total = cotangent[at, :].astype(F32) + dot_back(enc_grad[at, :], w_own_rows[...])
        for j in range(count):
            z = dot_plain(x[at, :], w_cols[j][...])
            part = got[:, j * narrow : (j + 1) * narrow]
            down = (part * slope_of(z, jax.nn.sigmoid(z))).astype(BF16)
            total = total + dot_back(down, w_rows[j][...])
        grad_grid[at, :] = total.astype(BF16)
        return carry

    lax.fori_loop(0, x.shape[0] // size, step, 0)


def weight_body(pairs, sr, *refs):
    outs = refs[2 * pairs :]
    for i in range(pairs):
        left, right, out = refs[2 * i], refs[2 * i + 1], outs[i]
        rows, columns = out.shape
        out[...] = dot_left(pick(left[...], sr[1], rows), pick(right[...], sr[0], columns))


def per_device(
    grid_latent, g2m_face, g2m_node, mesh_latent, mesh_links,
    w_enc, w_send, w_recv, w_node, w_dec, cotangent,
):
    face_count = lax.axis_size("space")
    pipe_count = lax.axis_size("pipe")
    chan_count = lax.axis_size("chan")
    grid_rows, wide = grid_latent.shape
    mesh_rows, narrow = mesh_latent.shape
    part = narrow // pipe_count
    mesh_all = face_count * mesh_rows
    mix_scale = (mesh_rows / (grid_rows * pipe_count)) ** 0.5
    nbrs = mesh_links.shape[1] * pipe_count
    chan, pipe, face = (lax.axis_index(a) for a in ("chan", "pipe", "space"))
    scalars = jnp.stack(
        [chan, pipe, chan * pipe_count + pipe]
        + [(chan + j) % chan_count for j in range(1, chan_count)]
    ).astype(jnp.int32)

    target = ((g2m_face[:, 0] - face) % face_count) * mesh_rows + g2m_node
    target_row = target.reshape(1, grid_rows)
    target_col = target.reshape(grid_rows, 1)

    links = lax.all_gather(mesh_links, "pipe", axis=1, tiled=True)
    offset = (links // mesh_rows - face) % face_count
    local = links % mesh_rows
    spot = jnp.where(
        offset == 0, mesh_rows + local, jnp.where(offset == 1, 2 * mesh_rows + local, local)
    )
    spot_row = spot.T.reshape(1, nbrs * mesh_rows)

    def columns_at(place):
        return pl.BlockSpec((wide, narrow), lambda i, sr: (0, sr[place]))

    def to_owner(keep, give):
        mixed_sum = keep.astype(F32) + shifted(give, "pipe", 1).astype(F32)
        blocks = mixed_sum.astype(BF16).reshape(face_count, mesh_rows, part)
        total = blocks[0].astype(F32)
        for k in range(1, face_count):
            total = total + shifted(blocks[k], "space", -k).astype(F32)
        return total

    def face_wide(block):
        return lax.all_gather(block, FACE_AXES)

    def from_owners(block):
        parts = [block] + [shifted(block, "space", k) for k in range(1, face_count)]
        return jnp.concatenate(parts, axis=0)

    sums = [((mesh_all, part), BF16)] * 2
    sum_flops = 2 * mesh_all * grid_rows * narrow
    keep, give = run(
        encode_body, scalars, (grid_latent, w_enc, target_row), sums,
        scratch=[pltpu.VMEM((grid_rows, narrow), BF16)],
        flops=sum_flops + 2 * grid_rows * wide * narrow, specs={1: columns_at(0)},
    )
    mesh_part = lax.dynamic_slice_in_dim(mesh_latent, pipe * part, part, 1)
    state_part = mesh_part.astype(F32) + mix_scale * to_owner(keep, give)
    parts = face_wide(state_part.astype(BF16))

    keep, give = run(sum_by_node, scalars, (target_row, cotangent), sums, flops=sum_flops)
    back_dec = face_wide(to_owner(keep, give).astype(BF16))

    block = (mesh_rows, part)
    full = (mesh_rows, wide)
    edge_flops = 6 * mesh_rows * mesh_rows * nbrs * part
    layer_specs = lambda first, layer: {
        first: layer_of(w_send.shape, layer), first + 1: layer_of(w_recv.shape, layer)
    }

    def edges(send_p, recv_p):
        return run(
            edge_body, scalars,
            (shifted(send_p, "space", -1), send_p, shifted(send_p, "space", 1), recv_p, spot),
            [(block, BF16), ((nbrs,) + block, F32)],
            scratch=[pltpu.VMEM((3 * mesh_rows, part), BF16)], flops=edge_flops,
        )

    state_0, send_p, recv_p = run(
        first_body, scalars, (parts, w_send, w_recv),
        [(full, BF16), (block, BF16), (block, F32)], specs=layer_specs(1, 0),
        flops=4 * mesh_rows * wide * part,
    )
    agg, slope_0 = edges(send_p, recv_p)
    agg_0, state, state_1, send_p, recv_p = run(
        next_body, scalars, (face_wide(agg), state_0, w_node, w_send, w_recv),
        [(full, BF16), (full, F32), (full, BF16), (block, BF16), (block, F32)],
        specs={2: layer_of(w_node.shape, 0), **layer_specs(3, 1)},
        flops=2 * mesh_rows * wide * wide,
    )
    agg, slope_1 = edges(send_p, recv_p)
    back_outs = [(full, F32), (full, BF16), (block, BF16), (block, BF16), (block, F32), (block, BF16)]
    back_scratch = [pltpu.VMEM((nbrs * mesh_rows, part), BF16)]
    agg_1, last_b, dec_part, dec_grad, grad, grad_b, recv_grad, below, own, above = run(
        turn_body, scalars,
        (face_wide(agg), state, w_node, w_dec, back_dec, slope_1, spot_row),
        [(full, BF16), (full, BF16), (block, BF16), (full, BF16)] + back_outs,
        specs={2: layer_of(w_node.shape, 1)}, scratch=back_scratch,
        flops=edge_flops + 6 * mesh_rows * wide * wide,
    )

    def weights(*pairs):
        shape = (wide // pipe_count, narrow)
        return run(
            functools.partial(weight_body, len(pairs)), scalars,
            [a for pair in pairs for a in pair], [(shape, F32)] * len(pairs),
            flops=2 * mesh_rows * shape[0] * shape[1] * len(pairs),
        )

    def senders(below, own, above):
        return (
            own
            + shifted(below, "space", 1).astype(F32)
            + shifted(above, "space", -1).astype(F32)
        ).astype(BF16)

    grads_a = lax.psum(weights((last_b, dec_grad), (agg_1, grad_b)), "space")
    recv_parts = face_wide(recv_grad)
    send_parts = face_wide(senders(below, own, above))
    send_1, recv_1, grad, grad_b, recv_grad, below, own, above = run(
        back_body, scalars,
        (grad, send_parts, recv_parts, w_send, w_recv, w_node, slope_0, spot_row),
        [(full, BF16), (full, BF16)] + back_outs,
        specs={**layer_specs(3, 1), 5: layer_of(w_node.shape, 0)}, scratch=back_scratch,
        flops=edge_flops + 4 * mesh_rows * wide * wide,
    )
    grads_b = lax.psum(weights((state_1, send_1), (state_1, recv_1), (agg_0, grad_b)), "space")
    recv_parts = face_wide(recv_grad)
    send_parts = face_wide(senders(below, own, above))
    send_0, recv_0, grad_mesh, enc_part = run(
        functools.partial(last_body, mix_scale), scalars,
        (grad, send_parts, recv_parts, w_send, w_recv),
        [(full, BF16), (full, BF16), ((mesh_rows, narrow), F32), (block, BF16)],
        specs=layer_specs(3, 0), flops=4 * mesh_rows * wide * wide,
    )
    grads_c = lax.psum(weights((state_0, send_0), (state_0, recv_0)), "space")

    table = pltpu.VMEM((mesh_all, narrow), BF16)
    dec_mine = from_owners(dec_part)
    mixed, = run(
        mixed_body, scalars, (grid_latent, target_col, dec_mine, shifted(dec_mine, "pipe", 1)),
        [((grid_rows, narrow), BF16)], scratch=[table], flops=sum_flops,
        specs={0: pl.BlockSpec((grid_rows, narrow), lambda i, sr: (0, sr[0]))},
    )
    enc_mine = from_owners(enc_part)
    half = (wide // pipe_count, narrow)
    enc_grad, grad_keep, grad_give = run(
        enc_own_body, scalars,
        (grid_latent, w_enc, target_col, enc_mine, shifted(enc_mine, "pipe", 1)),
        [((grid_rows, narrow), BF16), (half, F32), (half, BF16)],
        scratch=[table, pltpu.VMEM((wide, narrow), F32)],
        flops=sum_flops + 4 * grid_rows * wide * narrow, specs={1: columns_at(0)},
    )
    half_sum = (grad_keep + shifted(grad_give, "pipe", 1).astype(F32)).astype(BF16)
    total = half_sum.astype(F32)
    for k in range(1, face_count):
        total = total + shifted(half_sum, "space", k).astype(F32)
    grad_w_enc = lax.all_gather(total, "pipe", axis=0, tiled=True)

    others = chan_count - 1
    other_mine = [shifted(enc_mine, "chan", j) for j in range(1, chan_count)]
    other_sib = [shifted(block_j, "pipe", 1) for block_j in other_mine]
    corner = lambda place: pl.BlockSpec((narrow, narrow), lambda i, sr: (sr[0], sr[place]))
    specs = {4: columns_at(0), 5: corner(0)}
    for j in range(others):
        specs[6 + j] = columns_at(3 + j)
        specs[6 + others + j] = corner(3 + j)
    grad_grid, = run(
        functools.partial(enc_other_body, others), scalars,
        (grid_latent, target_col, cotangent, enc_grad, w_enc, w_enc)
        + (w_enc,) * (2 * others) + tuple(other_mine) + tuple(other_sib),
        [((grid_rows, narrow), BF16)], specs=specs,
        scratch=[pltpu.VMEM((mesh_all, narrow * others), BF16)],
        flops=(sum_flops + 4 * grid_rows * wide * narrow) * others,
    )

    def rows_of(*blocks):
        return lax.all_gather(jnp.stack(blocks), "pipe", axis=1, tiled=True)

    grad_w_dec = lax.all_gather(grads_a[0], "pipe", axis=0, tiled=True)
    return (
        mixed,
        grad_grid,
        grad_mesh,
        grad_w_enc,
        rows_of(grads_c[0], grads_b[0]),
        rows_of(grads_c[1], grads_b[1]),
        rows_of(grads_b[2], grads_a[1]),
        grad_w_dec,
    )


def solution(mesh):
    nodes = ("groups", "space", "pipe")
    in_specs = (
        P(nodes, None), P(nodes, None), P(nodes), P(("groups", "space"), "chan"),
        P(("groups", "space"), "pipe"), P(), P(), P(), P(), P(), P(nodes, "chan"),
    )
    out_specs = (
        P(nodes, "chan"), P(nodes, "chan"), P(("groups", "space"), "chan"), P("groups", "chan"),
        P("groups", None, "chan"), P("groups", None, "chan"), P("groups", None, "chan"),
        P("groups", "chan"),
    )
    return jax.shard_map(
        per_device, mesh=mesh, in_specs=in_specs, out_specs=out_specs, check_vma=False
    )
```

```python
import functools

import jax
import jax.numpy as jnp
from jax import lax
from jax.experimental import pallas as pl
from jax.experimental.pallas import tpu as pltpu
from jax.sharding import PartitionSpec as P

F32, BF16 = jnp.float32, jnp.bfloat16
FACE_AXES = ("chan", "pipe")


def shifted(block, axis, distance):
    count = lax.axis_size(axis)
    return lax.ppermute(block, axis, [((i + distance) % count, i) for i in range(count)])


def dot_plain(left, right):
    return jnp.dot(left, right, preferred_element_type=F32)


def dot_back(left, right):
    return lax.dot_general(left, right, (((1,), (1,)), ((), ())), preferred_element_type=F32)


def dot_left(left, right):
    return lax.dot_general(left, right, (((0,), (0,)), ((), ())), preferred_element_type=F32)


def slope_of(values, sigmoid_v):
    return sigmoid_v * (1.0 + values * (1.0 - sigmoid_v))


def one_hot(rows, ids):
    return jnp.where(rows == ids, 1.0, 0.0).astype(BF16)


def pick(values, index, width):
    out = values[:, :width]
    for j in range(1, values.shape[1] // width):
        out = jnp.where(index == j, values[:, j * width : (j + 1) * width], out)
    return out


def widen(parts):
    return jnp.concatenate([parts[j] for j in range(parts.shape[0])], axis=1)


def some_of(parts, index, count):
    return jnp.concatenate([parts[index * count + j] for j in range(count)], axis=1)


def whole(shape):
    return pl.BlockSpec(shape, lambda i, sr: (0,) * len(shape))


def layer_of(shape, layer):
    return pl.BlockSpec((None,) + shape[1:], lambda i, sr: (layer, 0, 0))


def run(body, scalars, args, outs, scratch=(), flops=0, specs=None):
    specs = specs or {}
    return pl.pallas_call(
        body,
        out_shape=[jax.ShapeDtypeStruct(s, d) for s, d in outs],
        grid_spec=pltpu.PrefetchScalarGridSpec(
            num_scalar_prefetch=1,
            grid=(1,),
            in_specs=[specs.get(i, whole(a.shape)) for i, a in enumerate(args)],
            out_specs=[whole(s) for s, _ in outs],
            scratch_shapes=list(scratch),
        ),
        compiler_params=pltpu.CompilerParams(vmem_limit_bytes=56 * 1024 * 1024),
        cost_estimate=pl.CostEstimate(flops=flops, bytes_accessed=0, transcendentals=0),
    )(scalars, *args)


def rows_at(index, size):
    return pl.ds(pl.multiple_of(index * size, size), size)


def sum_by_node(sr, target, values, keep, give):
    mesh_all, width = keep.shape
    grid_rows = values.shape[0]
    size = 512

    def step(i, carry):
        ids = lax.broadcasted_iota(jnp.int32, (size, grid_rows), 0) + i * size
        total = dot_plain(one_hot(ids, target[...]), values[...])
        low, high = total[:, :width], total[:, width:]
        first = sr[1] == 0
        keep[rows_at(i, size), :] = jnp.where(first, low, high).astype(BF16)
        give[rows_at(i, size), :] = jnp.where(first, high, low).astype(BF16)
        return carry

    lax.fori_loop(0, mesh_all // size, step, 0)


def encode_body(sr, x, w, target, keep, give, enc):
    size = 512

    def step(i, carry):
        z = dot_plain(x[rows_at(i, size), :], w[...])
        enc[rows_at(i, size), :] = (z * jax.nn.sigmoid(z)).astype(BF16)
        return carry

    lax.fori_loop(0, x.shape[0] // size, step, 0)
    sum_by_node(sr, target, enc, keep, give)


def project(sr, state_b, w_send, w_recv, send_p, recv_p):
    width = send_p.shape[1]
    send_p[...] = dot_plain(state_b, own_columns(sr, w_send, width)).astype(BF16)
    recv_p[...] = dot_plain(state_b, own_columns(sr, w_recv, width))


def own_columns(sr, w, width):
    return w[...] if w.shape[1] == width else pick(w[...], sr[2], width)


def first_body(sr, parts, w_send, w_recv, send_p, recv_p):
    project(sr, widen(parts), w_send, w_recv, send_p, recv_p)


def next_body(sr, agg, state, w_node, w_send, w_recv, new_state, send_p, recv_p):
    total = widen(state).astype(F32) + dot_plain(widen(agg), w_node[...])
    new_state[...] = total
    project(sr, total.astype(BF16), w_send, w_recv, send_p, recv_p)


def edge_body(sr, below, own, above, recv_p, spot, agg, slope, halo):
    mesh_rows, width = own.shape
    middle, half = mesh_rows // 2, 3 * mesh_rows // 2
    halo[:mesh_rows, :width] = below[...]
    halo[mesh_rows:, :width] = own[:middle, :]
    halo[:middle, width:] = own[middle:, :]
    halo[middle:, width:] = above[...]
    ids = lax.broadcasted_iota(jnp.int32, (mesh_rows, half), 1)
    count = slope.shape[0]
    total = jnp.zeros(agg.shape, F32)
    for k in range(count):
        place = spot[:, k : k + 1]
        right = place >= half
        both = dot_plain(one_hot(ids, jnp.where(right, place - half, place)), halo[...])
        pre = jnp.where(right, both[:, width:], both[:, :width]) + recv_p[...]
        sigmoid_v = jax.nn.sigmoid(pre)
        total = total + pre * sigmoid_v
        slope[k] = slope_of(pre, sigmoid_v).astype(BF16)
    agg[...] = (total / count).astype(BF16)


def edge_back(sr, grad_b, w_node, slope, spot, spot_row, recv_grad, below, own, above, back):
    mesh_rows, width = recv_grad.shape
    middle, half = mesh_rows // 2, 3 * mesh_rows // 2
    count = slope.shape[0]
    back_agg = dot_back(grad_b, w_node[rows_at(sr[2], width), :]) / count
    total = jnp.zeros(recv_grad.shape, F32)
    for k in range(count):
        term = back_agg * slope[k].astype(F32)
        total = total + term
        right = spot[:, k : k + 1] >= half
        rows = slice(k * mesh_rows, (k + 1) * mesh_rows)
        back[rows, :width] = jnp.where(right, 0.0, term).astype(BF16)
        back[rows, width:] = jnp.where(right, term, 0.0).astype(BF16)
    recv_grad[...] = total.astype(BF16)
    place = spot_row[...]
    place = jnp.where(place >= half, place - half, place)
    ids = lax.broadcasted_iota(jnp.int32, (half, count * mesh_rows), 0)
    spread = dot_plain(one_hot(ids, place), back[...])
    below[...] = spread[:mesh_rows, :width].astype(BF16)
    own[:middle, :] = spread[mesh_rows:, :width]
    own[middle:, :] = spread[:middle, width:]
    above[...] = spread[middle:, width:].astype(BF16)


def turn_body(
    sr, agg, state, w_node, w_dec, back_dec, slope, spot, spot_row,
    last_b, dec_part, dec_grad, grad, recv_grad, below, own, above, back,
):
    last = (state[...] + dot_plain(widen(agg), w_node[...])).astype(BF16)
    last_b[...] = last
    z_dec = dot_plain(last, w_dec[...])
    sigmoid_v = jax.nn.sigmoid(z_dec)
    dec_part[...] = pick(z_dec * sigmoid_v, sr[2], dec_part.shape[1]).astype(BF16)
    down = (widen(back_dec).astype(F32) * slope_of(z_dec, sigmoid_v)).astype(BF16)
    dec_grad[...] = down
    total = dot_back(down, w_dec[...])
    grad[...] = total
    edge_back(sr, total.astype(BF16), w_node, slope, spot, spot_row, recv_grad, below, own, above, back)


def through(grad, send_parts, recv_parts, w_send, w_recv):
    return (
        grad[...]
        + dot_back(widen(send_parts), w_send[...])
        + dot_back(widen(recv_parts), w_recv[...])
    )


def back_body(
    sr, grad, send_parts, recv_parts, w_send, w_recv, w_node, slope, spot, spot_row,
    new_grad, recv_grad, below, own, above, back,
):
    total = through(grad, send_parts, recv_parts, w_send, w_recv)
    new_grad[...] = total
    edge_back(sr, total.astype(BF16), w_node, slope, spot, spot_row, recv_grad, below, own, above, back)


def last_body(mix_scale, sr, grad, send_parts, recv_parts, w_send, w_recv, grad_mesh, enc_part, enc_all):
    total = through(grad, send_parts, recv_parts, w_send, w_recv)
    grad_mesh[...] = pick(total, sr[0], grad_mesh.shape[1])
    scaled = (mix_scale * total).astype(BF16)
    enc_part[...] = pick(scaled, sr[2], enc_part.shape[1])
    enc_all[...] = scaled


def put_pair(sr, table, row, column, mine, other):
    first = sr[1] == 0
    rows, width = mine.shape
    at = slice(row, row + rows)
    table[at, column : column + width] = jnp.where(first, mine[...], other[...])
    table[at, column + width : column + 2 * width] = jnp.where(first, other[...], mine[...])


def node_values(target, at, table):
    ids = lax.broadcasted_iota(jnp.int32, (table.shape[0], at.size), 0)
    return dot_left(one_hot(ids, target[:, at]), table[...])


def mixed_body(sr, x, x_own, w, target, mine, other, mixed, slope, table):
    put_pair(sr, table, 0, 0, mine, other)
    size = 512

    def step(i, carry):
        at = rows_at(i, size)
        got = node_values(target, at, table)
        mixed[at, :] = (x_own[at, :].astype(F32) + got).astype(BF16)
        z = dot_plain(x[at, :], w[...])
        slope[at, :] = slope_of(z, jax.nn.sigmoid(z)).astype(BF16)
        return carry

    lax.fori_loop(0, x.shape[0] // size, step, 0)


def enc_own_body(count, sr, x, target, slope, *rest):
    mine, other = rest[:count], rest[count : 2 * count]
    enc_grad, grad_keep, grad_give, table, total = rest[2 * count :]
    mesh_rows = mine[0].shape[0]
    for k in range(count):
        put_pair(sr, table, k * mesh_rows, 0, mine[k], other[k])
    size = 512
    total[...] = jnp.zeros(total.shape, F32)

    def step(i, carry):
        at = rows_at(i, size)
        down = (node_values(target, at, table) * slope[at, :].astype(F32)).astype(BF16)
        enc_grad[at, :] = down
        total[...] += dot_left(x[at, :], down)
        return carry

    lax.fori_loop(0, x.shape[0] // size, step, 0)
    half = grad_keep.shape[0]
    grad_keep[...] = total[rows_at(sr[1], half), :]
    grad_give[...] = total[rows_at(1 - sr[1], half), :].astype(BF16)


def enc_other_body(faces, count, sr, target, cotangent, enc_grad, w_own_rows, enc_all, *rest):
    slopes, w_rows = rest[:count], rest[count : 2 * count]
    blocks = rest[2 * count : -2]
    grad_grid, table = rest[-2:]
    grid_rows, narrow = cotangent.shape
    width, mesh_rows = narrow // 2, enc_all.shape[0]
    for j in range(count):
        own = pick(enc_all[...], sr[4 + j], narrow)
        table[:mesh_rows, j * narrow : (j + 1) * narrow] = own
        for k in range(1, faces):
            mine, other = blocks[2 * (j * (faces - 1) + k - 1) :][:2]
            put_pair(sr, table, k * mesh_rows, j * narrow, mine, other)
    size = 512

    def step(i, carry):
        at = rows_at(i, size)
        got = node_values(target, at, table)
        total = cotangent[at, :].astype(F32) + dot_back(enc_grad[at, :], w_own_rows[...])
        for j in range(count):
            part = got[:, j * narrow : (j + 1) * narrow]
            down = (part * slopes[j][at, :].astype(F32)).astype(BF16)
            total = total + dot_back(down, w_rows[j][...])
        grad_grid[at, :] = total.astype(BF16)
        return carry

    lax.fori_loop(0, grid_rows // size, step, 0)


def weight_body(kinds, sr, *refs):
    out = refs[-1]
    rows = out.shape[0] // len(kinds)
    narrow = out.shape[1]

    def half_of(ref, index, width):
        if len(ref.shape) == 3:
            return some_of(ref, index, width // ref.shape[2])
        return pick(ref[...].astype(BF16), index, width)

    for i, (left, right) in enumerate(kinds):
        product = dot_left(half_of(refs[left], sr[1], rows), half_of(refs[right], sr[0], narrow))
        out[i * rows : (i + 1) * rows, :] = product.astype(BF16)


def write_body(places, sr, *refs):
    count = len(places)
    outs = refs[2 * count :]
    for i, items in enumerate(places):
        mine, other = refs[i], refs[count + i]
        rows = mine.shape[0] // len(items)
        for j, (out, layer) in enumerate(items):
            ref = outs[out] if layer is None else outs[out].at[layer]
            at = slice(j * rows, (j + 1) * rows)
            ref[rows_at(sr[1], rows), :] = mine[at, :].astype(F32)
            ref[rows_at(1 - sr[1], rows), :] = other[at, :].astype(F32)


def per_device(
    grid_latent, g2m_face, g2m_node, mesh_latent, mesh_links,
    w_enc, w_send, w_recv, w_node, w_dec, cotangent,
):
    face_count = lax.axis_size("space")
    pipe_count = lax.axis_size("pipe")
    chan_count = lax.axis_size("chan")
    grid_rows, wide = grid_latent.shape
    mesh_rows, narrow = mesh_latent.shape
    part = narrow // pipe_count
    mesh_all = face_count * mesh_rows
    others = chan_count - 1
    mix_scale = (mesh_rows / (grid_rows * pipe_count)) ** 0.5
    nbrs = mesh_links.shape[1] * pipe_count
    chan, pipe, face = (lax.axis_index(a) for a in ("chan", "pipe", "space"))
    scalars = jnp.stack(
        [chan, pipe, chan * pipe_count + pipe, face]
        + [(chan + j) % chan_count for j in range(1, chan_count)]
    ).astype(jnp.int32)
    target = ((g2m_face[:, 0] - face) % face_count) * mesh_rows + g2m_node
    target = target.reshape(1, grid_rows)

    def columns_at(place):
        return pl.BlockSpec((wide, narrow), lambda i, sr: (0, sr[place]))

    def both_cores(keep, give):
        total = keep.astype(F32) + shifted(give, "pipe", 1).astype(F32)
        return list(total.astype(BF16).reshape(face_count, mesh_rows, part))

    def to_owner(blocks):
        total = blocks[0].astype(F32)
        for k in range(1, face_count):
            total = total + shifted(blocks[k], "space", -k).astype(F32)
        return total

    def face_wide(block):
        return lax.all_gather(block, FACE_AXES)

    def from_owners(block):
        return [block] + [shifted(block, "space", k) for k in range(1, face_count)]

    sums = [((mesh_all, part), BF16)] * 2
    sum_flops = 2 * mesh_all * grid_rows * narrow
    keep, give = run(
        encode_body, scalars, (grid_latent, w_enc, target), sums,
        scratch=[pltpu.VMEM((grid_rows, narrow), BF16)],
        flops=sum_flops + 2 * grid_rows * wide * narrow, specs={1: columns_at(0)},
    )
    blocks, cotangent_late, links = lax.optimization_barrier(
        (both_cores(keep, give), cotangent, mesh_links)
    )
    mesh_part = lax.dynamic_slice_in_dim(mesh_latent, pipe * part, part, 1)
    state_part = mesh_part.astype(F32) + mix_scale * to_owner(blocks)
    state_0 = face_wide(state_part.astype(BF16))

    links = jnp.concatenate([links, shifted(links, "pipe", 1)], axis=1)
    offset = (links // mesh_rows - face) % face_count
    local = links % mesh_rows
    spot = jnp.where(
        offset == 0, mesh_rows + local, jnp.where(offset == 1, 2 * mesh_rows + local, local)
    )
    spot_row = spot.T.reshape(1, nbrs * mesh_rows)

    keep, give = run(sum_by_node, scalars, (target, cotangent_late), sums, flops=sum_flops)
    back_blocks = both_cores(keep, give)

    block = (mesh_rows, part)
    full = (mesh_rows, wide)
    edge_flops = 6 * mesh_rows * mesh_rows * nbrs * part

    def own_part(layer):
        if part % 128:
            return layer_of(w_send.shape, layer)
        return pl.BlockSpec((None, wide, part), lambda i, sr: (layer, 0, sr[2]))

    def neighbours(send_p):
        return shifted(send_p, "space", -1), shifted(send_p, "space", 1)

    def edges(send_p, recv_p, below, above):
        return run(
            edge_body, scalars, (below, send_p, above, recv_p, spot),
            [(block, BF16), ((nbrs,) + block, BF16)],
            scratch=[pltpu.VMEM((3 * mesh_rows // 2, 2 * part), BF16)], flops=edge_flops,
        )

    send_p, recv_p = run(
        first_body, scalars, (state_0, w_send, w_recv), [(block, BF16), (block, F32)],
        specs={1: own_part(0), 2: own_part(0)}, flops=4 * mesh_rows * wide * part,
    )
    below, above, back_blocks = lax.optimization_barrier((*neighbours(send_p), back_blocks))
    agg, slope_0 = edges(send_p, recv_p, below, above)
    agg_0 = face_wide(agg)
    state_1, send_p, recv_p = run(
        next_body, scalars, (agg_0, state_0, w_node, w_send, w_recv),
        [(full, F32), (block, BF16), (block, F32)],
        specs={2: layer_of(w_node.shape, 0), 3: own_part(1), 4: own_part(1)},
        flops=2 * mesh_rows * wide * wide,
    )
    back_dec = face_wide(to_owner(back_blocks).astype(BF16))
    agg, slope_1 = edges(send_p, recv_p, *neighbours(send_p))
    agg_1 = face_wide(agg)
    back_outs = [(full, F32), (block, BF16), (block, BF16), (block, F32), (block, BF16)]
    back_scratch = [pltpu.VMEM((nbrs * mesh_rows, 2 * part), BF16)]
    last_b, dec_part, dec_grad, grad_2, recv_grad, below, own, above = run(
        turn_body, scalars,
        (agg_1, state_1, w_node, w_dec, back_dec, slope_1, spot, spot_row),
        [(full, BF16), (block, BF16), (full, BF16)] + back_outs,
        specs={2: layer_of(w_node.shape, 1)}, scratch=back_scratch,
        flops=edge_flops + 6 * mesh_rows * wide * wide,
    )

    half = wide // pipe_count

    def weights(args, kinds):
        return run(
            functools.partial(weight_body, kinds), scalars, args,
            [((half * len(kinds), narrow), BF16)],
            flops=2 * mesh_rows * half * narrow * len(kinds),
        )[0]

    def senders(below, own, above):
        return (own + below.astype(F32) + above.astype(F32)).astype(BF16)

    sums_a = weights((last_b, dec_grad, agg_1, grad_2), ((0, 1), (2, 3)))
    recv_1 = face_wide(recv_grad)
    below, above = shifted(below, "space", 1), shifted(above, "space", -1)
    below, above, dec_part = lax.optimization_barrier((below, above, dec_part))
    send_1 = face_wide(senders(below, own, above))
    layer_specs = lambda first, layer: {
        first: layer_of(w_send.shape, layer), first + 1: layer_of(w_recv.shape, layer)
    }
    grad_1, recv_grad, below, own, above = run(
        back_body, scalars,
        (grad_2, send_1, recv_1, w_send, w_recv, w_node, slope_0, spot, spot_row), back_outs,
        specs={**layer_specs(3, 1), 5: layer_of(w_node.shape, 0)}, scratch=back_scratch,
        flops=edge_flops + 4 * mesh_rows * wide * wide,
    )
    sums_b = weights((state_1, send_1, recv_1, agg_0, grad_1), ((0, 1), (0, 2), (3, 4)))
    recv_0 = face_wide(recv_grad)
    below, above = shifted(below, "space", 1), shifted(above, "space", -1)
    send_0 = face_wide(senders(below, own, above))
    grad_mesh, enc_part, enc_all = run(
        functools.partial(last_body, mix_scale), scalars,
        (grad_1, send_0, recv_0, w_send, w_recv),
        [((mesh_rows, narrow), F32), (block, BF16), (full, BF16)],
        specs=layer_specs(3, 0), flops=4 * mesh_rows * wide * wide,
    )
    sums_c = weights((state_0, send_0, recv_0), ((0, 1), (0, 2)))

    dec_mine = jnp.concatenate(from_owners(dec_part), axis=0)
    mixed, slope_enc = run(
        mixed_body, scalars,
        (grid_latent, grid_latent, w_enc, target, dec_mine, shifted(dec_mine, "pipe", 1)),
        [((grid_rows, narrow), BF16), ((grid_rows, wide), BF16)],
        scratch=[pltpu.VMEM((mesh_all, narrow), BF16)],
        flops=sum_flops + 2 * grid_rows * wide * wide,
        specs={1: pl.BlockSpec((grid_rows, narrow), lambda i, sr: (0, sr[0]))},
    )
    enc_mine = from_owners(enc_part)
    enc_other = [shifted(piece, "pipe", 1) for piece in enc_mine]
    grid_columns = lambda place: pl.BlockSpec((grid_rows, narrow), lambda i, sr: (0, sr[place]))
    enc_grad, grad_keep, grad_give = run(
        functools.partial(enc_own_body, face_count), scalars,
        (grid_latent, target, slope_enc, *enc_mine, *enc_other),
        [((grid_rows, narrow), BF16), ((half, narrow), F32), ((half, narrow), BF16)],
        scratch=[pltpu.VMEM((mesh_all, narrow), BF16), pltpu.VMEM((wide, narrow), F32)],
        flops=sum_flops + 2 * grid_rows * wide * narrow, specs={2: grid_columns(0)},
    )
    half_sum = (grad_keep + shifted(grad_give, "pipe", 1).astype(F32)).astype(BF16)
    total = half_sum.astype(F32)
    for k in range(1, face_count):
        total = total + shifted(half_sum, "space", k).astype(F32)
    grad_w_enc = lax.all_gather(total, "pipe", axis=0, tiled=True)

    pieces = []
    for j in range(1, chan_count):
        for k in range(1, face_count):
            piece = shifted(enc_mine[k], "chan", j)
            pieces += [piece, shifted(piece, "pipe", 1)]
    corner = lambda place: pl.BlockSpec((narrow, narrow), lambda i, sr: (sr[0], sr[place]))
    specs = {3: corner(0)}
    for j in range(others):
        specs[5 + j] = grid_columns(4 + j)
        specs[5 + others + j] = corner(4 + j)
    grad_grid, = run(
        functools.partial(enc_other_body, face_count, others), scalars,
        (target, cotangent, enc_grad, w_enc, enc_all)
        + (slope_enc,) * others + (w_enc,) * others + tuple(pieces),
        [((grid_rows, narrow), BF16)], specs=specs,
        scratch=[pltpu.VMEM((mesh_all, narrow * others), BF16)],
        flops=(sum_flops + 4 * grid_rows * narrow * narrow) * others,
    )

    sums_all = lax.psum((sums_a, sums_b, sums_c), "space")
    layers = w_send.shape[0]
    layer_shape = ((layers, wide, narrow), F32)
    grad_w_send, grad_w_recv, grad_w_node, grad_w_dec = run(
        functools.partial(
            write_body, (((3, None), (2, 1)), ((0, 1), (1, 1), (2, 0)), ((0, 0), (1, 0)))
        ),
        scalars, (*sums_all, *(shifted(a, "pipe", 1) for a in sums_all)),
        [layer_shape] * 3 + [((wide, narrow), F32)],
    )
    return (
        mixed,
        grad_grid,
        grad_mesh,
        grad_w_enc,
        grad_w_send,
        grad_w_recv,
        grad_w_node,
        grad_w_dec,
    )


def solution(mesh):
    nodes = ("groups", "space", "pipe")
    in_specs = (
        P(nodes, None), P(nodes, None), P(nodes), P(("groups", "space"), "chan"),
        P(("groups", "space"), "pipe"), P(), P(), P(), P(), P(), P(nodes, "chan"),
    )
    out_specs = (
        P(nodes, "chan"), P(nodes, "chan"), P(("groups", "space"), "chan"), P("groups", "chan"),
        P("groups", None, "chan"), P("groups", None, "chan"), P("groups", None, "chan"),
        P("groups", "chan"),
    )
    return jax.shard_map(
        per_device, mesh=mesh, in_specs=in_specs, out_specs=out_specs, check_vma=False
    )
```

```python
import functools

import jax
import jax.numpy as jnp
from jax import lax
from jax.experimental import pallas as pl
from jax.experimental.pallas import tpu as pltpu
from jax.sharding import PartitionSpec as P

F32, BF16 = jnp.float32, jnp.bfloat16
FACE_AXES = ("chan", "pipe")


def shifted(block, axis, distance):
    count = lax.axis_size(axis)
    return lax.ppermute(block, axis, [((i + distance) % count, i) for i in range(count)])


def dot_plain(left, right):
    return jnp.dot(left, right, preferred_element_type=F32)


def dot_back(left, right):
    return lax.dot_general(left, right, (((1,), (1,)), ((), ())), preferred_element_type=F32)


def dot_left(left, right):
    return lax.dot_general(left, right, (((0,), (0,)), ((), ())), preferred_element_type=F32)


def slope_of(values, sigmoid_v):
    return sigmoid_v * (1.0 + values * (1.0 - sigmoid_v))


def one_hot(rows, ids):
    return jnp.where(rows == ids, 1.0, 0.0).astype(BF16)


def pick(values, index, width):
    out = values[:, :width]
    for j in range(1, values.shape[1] // width):
        out = jnp.where(index == j, values[:, j * width : (j + 1) * width], out)
    return out


def in_order(first, mine, other):
    return jnp.where(first, mine, other), jnp.where(first, other, mine)


def widen(parts):
    chan, first = lax.axis_index("chan"), lax.axis_index("pipe") == 0
    count = len(parts) // 2
    pairs = [
        jnp.concatenate(in_order(first, parts[2 * j][...], parts[2 * j + 1][...]), axis=1)
        for j in range(count)
    ]
    out = []
    for place in range(count):
        block = pairs[0]
        for j in range(1, count):
            block = jnp.where(lax.rem(chan + j, count) == place, pairs[j], block)
        out.append(block)
    return jnp.concatenate(out, axis=1)


def own_quarter():
    return lax.axis_index("chan") * lax.axis_size("pipe") + lax.axis_index("pipe")


def run(body, args, outs, scratch=(), flops=0, vmem=17, hbm=()):
    args = [pltpu.with_memory_space_constraint(a, pltpu.VMEM) for a in args]
    return pl.pallas_call(
        body,
        out_shape=[
            jax.ShapeDtypeStruct(s, d) if i in hbm else pltpu.VMEM(s, d)
            for i, (s, d) in enumerate(outs)
        ],
        in_specs=[pl.BlockSpec(memory_space=pltpu.VMEM)] * len(args),
        out_specs=[pl.BlockSpec(memory_space=pltpu.VMEM)] * len(outs),
        scratch_shapes=list(scratch),
        compiler_params=pltpu.CompilerParams(vmem_limit_bytes=vmem * 1024 * 1024),
        cost_estimate=pl.CostEstimate(flops=flops, bytes_accessed=0, transcendentals=0),
    )(*args)


def rows_at(index, size):
    return pl.ds(pl.multiple_of(index * size, size), size)


def table_rows(mesh_rows, face_ids, node_ids):
    count = lax.axis_size("space")
    turned = face_ids - lax.axis_index("space")
    return jnp.where(turned < 0, turned + count, turned) * mesh_rows + node_ids


def sum_by_node(mesh_rows, face_ids, node_ids, values, keep, give):
    mesh_all, width = keep.shape
    grid_rows = values.shape[0]
    size = 512
    first = lax.axis_index("pipe") == 0
    target = table_rows(mesh_rows, face_ids[...], node_ids[...])

    def step(i, carry):
        ids = lax.broadcasted_iota(jnp.int32, (size, grid_rows), 0) + i * size
        total = dot_plain(one_hot(ids, target), values[...])
        mine, other = in_order(first, total[:, :width], total[:, width:])
        keep[rows_at(i, size), :] = mine.astype(BF16)
        give[rows_at(i, size), :] = other.astype(BF16)
        return carry

    lax.fori_loop(0, mesh_all // size, step, 0)


def encode_body(mesh_rows, x, w, face_ids, node_ids, keep, give, enc):
    size = 512
    columns = pick(w[...], lax.axis_index("chan"), enc.shape[1])

    def step(i, carry):
        z = dot_plain(x[rows_at(i, size), :], columns)
        enc[rows_at(i, size), :] = (z * jax.nn.sigmoid(z)).astype(BF16)
        return carry

    lax.fori_loop(0, x.shape[0] // size, step, 0)
    sum_by_node(mesh_rows, face_ids, node_ids, enc, keep, give)


def join_body(keep, got, *outs):
    rows = outs[0].shape[0]
    for k, out in enumerate(outs):
        at = slice(k * rows, (k + 1) * rows)
        out[...] = (keep[at, :].astype(F32) + got[at, :].astype(F32)).astype(BF16)


def add_all(parts):
    total = parts[0][...].astype(F32)
    for ref in parts[1:]:
        total = total + ref[...].astype(F32)
    return total


def add_body(*refs):
    refs[-1][...] = add_all(refs[:-1]).astype(refs[-1].dtype)


def state_body(mix_scale, mesh, *refs):
    own = pick(mesh[...], lax.axis_index("pipe"), refs[-1].shape[1]).astype(F32)
    refs[-1][...] = (own + mix_scale * add_all(refs[:-1])).astype(BF16)


def project(layer, state_b, w_send, w_recv, send_p, recv_p):
    width, quarter = send_p.shape[1], own_quarter()
    send_p[...] = dot_plain(state_b, pick(w_send[layer], quarter, width)).astype(BF16)
    recv_p[...] = dot_plain(state_b, pick(w_recv[layer], quarter, width))


def first_body(w_send, w_recv, *refs):
    state_0, send_p, recv_p = refs[-3:]
    wide = widen(refs[:-3])
    state_0[...] = wide
    project(0, wide, w_send, w_recv, send_p, recv_p)


def next_body(state, w_node, w_send, w_recv, *refs):
    agg_wide, new_state, send_p, recv_p = refs[-4:]
    wide = widen(refs[:-4])
    agg_wide[...] = wide
    total = state[...].astype(F32) + dot_plain(wide, w_node[0])
    new_state[...] = total
    project(1, total.astype(BF16), w_send, w_recv, send_p, recv_p)


def edge_body(below, own, above, recv_p, spot, agg, slope, halo):
    mesh_rows, width = own.shape
    middle, half = mesh_rows // 2, 3 * mesh_rows // 2
    halo[:mesh_rows, :width] = below[...]
    halo[mesh_rows:, :width] = own[:middle, :]
    halo[:middle, width:] = own[middle:, :]
    halo[middle:, width:] = above[...]
    ids = lax.broadcasted_iota(jnp.int32, (mesh_rows, half), 1)
    count = slope.shape[0]
    total = jnp.zeros(agg.shape, F32)
    for k in range(count):
        place = spot[:, k : k + 1]
        right = place >= half
        both = dot_plain(one_hot(ids, jnp.where(right, place - half, place)), halo[...])
        pre = jnp.where(right, both[:, width:], both[:, :width]) + recv_p[...]
        sigmoid_v = jax.nn.sigmoid(pre)
        total = total + pre * sigmoid_v
        slope[k] = slope_of(pre, sigmoid_v).astype(BF16)
    agg[...] = (total / count).astype(BF16)


def edge_back(grad_b, w_node, slope, spot, spot_row, recv_grad, below, own, above, back):
    mesh_rows, width = recv_grad.shape
    middle, half = mesh_rows // 2, 3 * mesh_rows // 2
    count = slope.shape[0]
    back_agg = dot_back(grad_b, w_node[rows_at(own_quarter(), width), :]) / count
    total = jnp.zeros(recv_grad.shape, F32)
    for k in range(count):
        term = back_agg * slope[k].astype(F32)
        total = total + term
        right = spot[:, k : k + 1] >= half
        rows = slice(k * mesh_rows, (k + 1) * mesh_rows)
        back[rows, :width] = jnp.where(right, 0.0, term).astype(BF16)
        back[rows, width:] = jnp.where(right, term, 0.0).astype(BF16)
    recv_grad[...] = total.astype(BF16)
    place = spot_row[...]
    place = jnp.where(place >= half, place - half, place)
    ids = lax.broadcasted_iota(jnp.int32, (half, count * mesh_rows), 0)
    spread = dot_plain(one_hot(ids, place), back[...])
    below[...] = spread[:mesh_rows, :width].astype(BF16)
    own[:middle, :] = spread[mesh_rows:, :width]
    own[middle:, :] = spread[:middle, width:]
    above[...] = spread[middle:, width:].astype(BF16)


def turn_body(count, state, w_node, w_dec, slope, spot, spot_row, *refs):
    agg, back_dec = refs[:count], refs[count : 2 * count]
    agg_wide, last_b, dec_part, dec_grad, grad = refs[2 * count : 2 * count + 5]
    wide = widen(agg)
    agg_wide[...] = wide
    last = (state[...] + dot_plain(wide, w_node[1])).astype(BF16)
    last_b[...] = last
    z_dec = dot_plain(last, w_dec[...])
    sigmoid_v = jax.nn.sigmoid(z_dec)
    dec_part[...] = pick(z_dec * sigmoid_v, own_quarter(), dec_part.shape[1]).astype(BF16)
    down = (widen(back_dec).astype(F32) * slope_of(z_dec, sigmoid_v)).astype(BF16)
    dec_grad[...] = down
    total = dot_back(down, w_dec[...])
    grad[...] = total
    edge_back(total.astype(BF16), w_node.at[1], slope, spot, spot_row, *refs[2 * count + 5 :])


def through(layer, grad, w_send, w_recv, send_parts, recv_parts, send_wide, recv_wide):
    send, recv = widen(send_parts), widen(recv_parts)
    send_wide[...] = send
    recv_wide[...] = recv
    return grad[...] + dot_back(send, w_send[layer]) + dot_back(recv, w_recv[layer])


def back_body(count, grad, w_send, w_recv, w_node, slope, spot, spot_row, *refs):
    send_parts, recv_parts = refs[:count], refs[count : 2 * count]
    send_wide, recv_wide, new_grad = refs[2 * count : 2 * count + 3]
    total = through(1, grad, w_send, w_recv, send_parts, recv_parts, send_wide, recv_wide)
    new_grad[...] = total
    edge_back(total.astype(BF16), w_node.at[0], slope, spot, spot_row, *refs[2 * count + 3 :])


def last_body(count, mix_scale, grad, w_send, w_recv, *refs):
    send_parts, recv_parts = refs[:count], refs[count : 2 * count]
    send_wide, recv_wide, grad_mesh, enc_part, enc_all = refs[2 * count :]
    total = through(0, grad, w_send, w_recv, send_parts, recv_parts, send_wide, recv_wide)
    grad_mesh[...] = pick(total, lax.axis_index("chan"), grad_mesh.shape[1])
    scaled = (mix_scale * total).astype(BF16)
    enc_part[...] = pick(scaled, own_quarter(), enc_part.shape[1])
    enc_all[...] = scaled


def put_pair(table, row, column, mine, other):
    rows, width = mine.shape
    low, high = in_order(lax.axis_index("pipe") == 0, mine[...], other[...])
    table[row : row + rows, column : column + width] = low
    table[row : row + rows, column + width : column + 2 * width] = high


def node_values(target, at, table):
    ids = lax.broadcasted_iota(jnp.int32, (table.shape[0], at.size), 0)
    return dot_left(one_hot(ids, target[:, at]), table[...])


def mixed_body(count, x, w, face_ids, node_ids, *refs):
    mine, other = refs[:count], refs[count : 2 * count]
    mixed, slope, table, target = refs[2 * count :]
    mesh_rows = mine[0].shape[0]
    for k in range(count):
        put_pair(table, k * mesh_rows, 0, mine[k], other[k])
    target[...] = table_rows(mesh_rows, face_ids[...], node_ids[...])
    size = 512
    chan = lax.axis_index("chan")

    def step(i, carry):
        at = rows_at(i, size)
        got = node_values(target, at, table)
        rows = x[at, :]
        mixed[at, :] = (pick(rows, chan, mixed.shape[1]).astype(F32) + got).astype(BF16)
        z = dot_plain(rows, w[...])
        slope[at, :] = slope_of(z, jax.nn.sigmoid(z)).astype(BF16)
        return carry

    lax.fori_loop(0, x.shape[0] // size, step, 0)


def enc_own_body(count, x, face_ids, node_ids, slope, *refs):
    mine, other = refs[:count], refs[count : 2 * count]
    enc_grad, grad_keep, grad_give, table, target, total = refs[2 * count :]
    mesh_rows = mine[0].shape[0]
    for k in range(count):
        put_pair(table, k * mesh_rows, 0, mine[k], other[k])
    target[...] = table_rows(mesh_rows, face_ids[...], node_ids[...])
    size = 512
    chan, pipe = lax.axis_index("chan"), lax.axis_index("pipe")
    total[...] = jnp.zeros(total.shape, F32)

    def step(i, carry):
        at = rows_at(i, size)
        own = pick(slope[at, :], chan, enc_grad.shape[1]).astype(F32)
        down = (node_values(target, at, table) * own).astype(BF16)
        enc_grad[at, :] = down
        total[...] += dot_left(x[at, :], down)
        return carry

    lax.fori_loop(0, x.shape[0] // size, step, 0)
    half = grad_keep.shape[0]
    grad_keep[...] = total[rows_at(pipe, half), :]
    grad_give[...] = total[rows_at(1 - pipe, half), :].astype(BF16)


def enc_other_body(faces, count, face_ids, node_ids, cotangent, enc_grad, enc_all, slope, w, *refs):
    blocks = refs[:-3]
    grad_grid, table, target = refs[-3:]
    grid_rows, narrow = cotangent.shape
    mesh_rows = enc_all.shape[0]
    chan = lax.axis_index("chan")
    for j in range(count):
        other = lax.rem(chan + 1 + j, count + 1)
        columns = slice(j * narrow, (j + 1) * narrow)
        table[:mesh_rows, columns] = pick(enc_all[...], other, narrow)
        for k in range(1, faces):
            mine, sibling = blocks[2 * (j * (faces - 1) + k - 1) :][:2]
            put_pair(table, k * mesh_rows, j * narrow, mine, sibling)
    target[...] = table_rows(mesh_rows, face_ids[...], node_ids[...])
    size = 512
    w_rows = w[rows_at(chan, narrow), :]
    own_block = pick(w_rows, chan, narrow)

    def step(i, carry):
        at = rows_at(i, size)
        got = node_values(target, at, table)
        total = cotangent[at, :].astype(F32) + dot_back(enc_grad[at, :], own_block)
        for j in range(count):
            other = lax.rem(chan + 1 + j, count + 1)
            part = got[:, j * narrow : (j + 1) * narrow]
            down = (part * pick(slope[at, :], other, narrow).astype(F32)).astype(BF16)
            total = total + dot_back(down, pick(w_rows, other, narrow))
        grad_grid[at, :] = total.astype(BF16)
        return carry

    lax.fori_loop(0, grid_rows // size, step, 0)


def weight_body(kinds, count, *refs):
    outs, table = refs[-count - 1 : -1], refs[-1]
    rows = table.shape[0] // len(kinds)
    narrow = table.shape[1]
    chan, pipe, face = (lax.axis_index(a) for a in ("chan", "pipe", "space"))
    for i, (left, right) in enumerate(kinds):
        one = pick(refs[left][...].astype(BF16), pipe, rows)
        two = pick(refs[right][...].astype(BF16), chan, narrow)
        table[i * rows : (i + 1) * rows, :] = dot_left(one, two).astype(BF16)
    size = outs[0].shape[0]
    for k, out in enumerate(outs):
        out[...] = table[rows_at(lax.rem(face + k, count), size), :]


def write_body(places, count, *refs):
    groups = len(places)
    outs, table = refs[2 * groups * count : -1], refs[-1]
    pipe, face = lax.axis_index("pipe"), lax.axis_index("space")
    for side in range(2):
        for i, items in enumerate(places):
            pieces = refs[(side * groups + i) * count :][:count]
            size = pieces[0].shape[0]
            for k in range(count):
                table[rows_at(lax.rem(face + k, count), size), :] = pieces[k][...]
            rows = size * count // len(items)
            half = pipe if side == 0 else 1 - pipe
            for j, (out, layer) in enumerate(items):
                ref = outs[out] if layer is None else outs[out].at[layer]
                ref[rows_at(half, rows), :] = table[j * rows : (j + 1) * rows, :].astype(F32)


def halves_body(mine, other, out):
    rows = mine.shape[0]
    pipe = lax.axis_index("pipe")
    out[rows_at(pipe, rows), :] = mine[...]
    out[rows_at(1 - pipe, rows), :] = other[...]


def per_device(
    grid_latent, g2m_face, g2m_node, mesh_latent, mesh_links,
    w_enc, w_send, w_recv, w_node, w_dec, cotangent,
):
    tie = lax.optimization_barrier
    faces = lax.axis_size("space")
    pipe_count = lax.axis_size("pipe")
    chan_count = lax.axis_size("chan")
    grid_rows, wide = grid_latent.shape
    mesh_rows, narrow = mesh_latent.shape
    part = narrow // pipe_count
    mesh_all = faces * mesh_rows
    mix_scale = (mesh_rows / (grid_rows * pipe_count)) ** 0.5
    nbrs = mesh_links.shape[1] * pipe_count
    face = lax.axis_index("space")
    ids = (g2m_face.reshape(1, grid_rows), g2m_node.reshape(1, grid_rows))
    grid_vmem = 14 + mesh_all // 512

    def on(body, *fixed):
        return functools.partial(body, *fixed)

    def over_faces(blocks, step):
        return [shifted(b, "space", step * k) for k, b in enumerate(blocks) if k > 0]

    def face_parts(block):
        out = []
        for j in range(chan_count):
            mine = shifted(block, "chan", j) if j else block
            out += [mine, shifted(mine, "pipe", 1)]
        return out

    def add(parts, kind=BF16):
        return run(add_body, parts, [(parts[0].shape, kind)])[0]

    block = (mesh_rows, part)
    full = (mesh_rows, wide)
    half = wide // pipe_count
    sums = [((mesh_all, part), BF16)] * 2
    sum_flops = 2 * mesh_all * grid_rows * narrow
    edge_flops = 6 * mesh_rows * mesh_rows * nbrs * part
    parts_count = 2 * chan_count

    def join(keep, give):
        return run(join_body, (keep, shifted(give, "pipe", 1)), [(block, BF16)] * faces)

    keep, give = run(
        on(encode_body, mesh_rows), (grid_latent, w_enc, *ids), sums,
        scratch=[pltpu.VMEM((grid_rows, narrow), BF16)],
        flops=sum_flops + 2 * grid_rows * wide * narrow, vmem=grid_vmem,
    )
    *blocks, cotangent_late, links = tie((*join(keep, give), cotangent, mesh_links))
    state_part, = run(
        on(state_body, mix_scale), (mesh_latent, blocks[0], *over_faces(blocks, -1)),
        [(block, BF16)],
    )

    links = jnp.concatenate([links, shifted(links, "pipe", 1)], axis=1)
    offset = (links // mesh_rows - face) % faces
    local = links % mesh_rows
    spot = jnp.where(
        offset == 0, mesh_rows + local, jnp.where(offset == 1, 2 * mesh_rows + local, local)
    )
    spot_row = spot.T.reshape(1, nbrs * mesh_rows)
    keep, give = run(
        on(sum_by_node, mesh_rows), (*ids, cotangent_late), sums, flops=sum_flops, vmem=grid_vmem
    )
    keep, give, spot, spot_row, state_part = tie((keep, give, spot, spot_row, state_part))

    def edges(send_p, recv_p, below, above):
        return run(
            edge_body, (below, send_p, above, recv_p, spot),
            [(block, BF16), ((nbrs,) + block, BF16)],
            scratch=[pltpu.VMEM((3 * mesh_rows // 2, 2 * part), BF16)], flops=edge_flops,
        )

    def neighbours(send_p):
        return shifted(send_p, "space", -1), shifted(send_p, "space", 1)

    state_0, send_p, recv_p = run(
        first_body, (w_send, w_recv, *face_parts(state_part)),
        [(full, BF16), (block, BF16), (block, F32)], flops=4 * mesh_rows * wide * part,
    )
    below, above, *back_blocks = tie((*neighbours(send_p), *join(keep, give)))
    back_got = over_faces(back_blocks, -1)
    agg, slope_0 = edges(send_p, recv_p, below, above)
    agg_0, state_1, send_p, recv_p = run(
        next_body, (state_0, w_node, w_send, w_recv, *face_parts(agg)),
        [(full, BF16), (full, F32), (block, BF16), (block, F32)],
        flops=2 * mesh_rows * wide * wide,
    )
    send_p, *back_got = tie((send_p, *back_got))
    below, above = neighbours(send_p)
    back_parts = face_parts(add([back_blocks[0], *back_got]))
    below, above, *back_parts = tie((below, above, *back_parts))
    agg, slope_1 = edges(send_p, recv_p, below, above)
    back_outs = [(full, F32), (block, BF16), (block, BF16), (block, F32), (block, BF16)]
    back_scratch = [pltpu.VMEM((nbrs * mesh_rows, 2 * part), BF16)]
    agg_1, last_b, dec_part, dec_grad, grad_2, recv_grad, below, own, above = run(
        on(turn_body, parts_count),
        (state_1, w_node, w_dec, slope_1, spot, spot_row, *face_parts(agg), *back_parts),
        [(full, BF16), (full, BF16), (block, BF16), (full, BF16)] + back_outs,
        scratch=back_scratch, flops=edge_flops + 6 * mesh_rows * wide * wide,
    )

    def weights(args, kinds):
        rows = half * len(kinds)
        return run(
            on(weight_body, kinds, faces), args, [((rows // faces, narrow), BF16)] * faces,
            scratch=[pltpu.VMEM((rows, narrow), BF16)], flops=2 * mesh_rows * rows * narrow,
        )

    def from_owners(piece):
        return [piece] + [shifted(piece, "space", k) for k in range(1, faces)]

    recv_parts = face_parts(recv_grad)
    pieces_a = weights((last_b, dec_grad, agg_1, grad_2), ((0, 1), (2, 3)))
    below, above = shifted(below, "space", 1), shifted(above, "space", -1)
    below, above, dec_part, *rest = tie((below, above, dec_part, *pieces_a, *recv_parts))
    pieces_a, recv_parts = rest[:faces], rest[faces:]
    got_a = over_faces(pieces_a, -1)
    dec_mine = from_owners(dec_part)
    outs = run(
        on(back_body, parts_count),
        (grad_2, w_send, w_recv, w_node, slope_0, spot, spot_row)
        + (*face_parts(add([own, below, above])), *recv_parts),
        [(full, BF16), (full, BF16)] + back_outs,
        scratch=back_scratch, flops=edge_flops + 4 * mesh_rows * wide * wide,
    )
    outs = tie((*outs, *got_a, *dec_mine[1:]))
    send_1, recv_1, grad_1, recv_grad, below, own, above = outs[:7]
    got_a, dec_mine = outs[7 : 6 + faces], [dec_mine[0], *outs[6 + faces :]]

    recv_parts = face_parts(recv_grad)
    pieces_b = weights((state_1, send_1, recv_1, agg_0, grad_1), ((0, 1), (0, 2), (3, 4)))
    sum_a = add([pieces_a[0], *got_a])
    below, above = shifted(below, "space", 1), shifted(above, "space", -1)
    below, above, sum_a, *rest = tie((below, above, sum_a, *pieces_b, *recv_parts))
    pieces_b, recv_parts = rest[:faces], rest[faces:]
    all_a = from_owners(sum_a)
    got_b = over_faces(pieces_b, -1)
    outs = run(
        on(last_body, parts_count, mix_scale),
        (grad_1, w_send, w_recv, *face_parts(add([own, below, above])), *recv_parts),
        [(full, BF16), (full, BF16), ((mesh_rows, narrow), F32), (block, BF16), (full, BF16)],
        flops=4 * mesh_rows * wide * wide,
    )
    outs = tie((*outs, *all_a[1:], *got_b))
    send_0, recv_0, grad_mesh, enc_part, enc_all = outs[:5]
    all_a, got_b = [all_a[0], *outs[5 : 4 + faces]], outs[4 + faces :]

    enc_mine = from_owners(enc_part)
    pieces_c = weights((state_0, send_0, recv_0), ((0, 1), (0, 2)))
    sum_b = add([pieces_b[0], *got_b])
    table = [pltpu.VMEM((mesh_all, narrow), BF16), pltpu.VMEM((1, grid_rows), jnp.int32)]
    mixed, slope_enc = run(
        on(mixed_body, faces),
        (grid_latent, w_enc, *ids, *dec_mine, *(shifted(b, "pipe", 1) for b in dec_mine)),
        [((grid_rows, narrow), BF16), ((grid_rows, wide), BF16)], scratch=table,
        flops=sum_flops + 2 * grid_rows * wide * wide, vmem=grid_vmem,
    )
    outs = tie((*enc_mine[1:], slope_enc, sum_b, *pieces_c))
    enc_mine = [enc_mine[0], *outs[: faces - 1]]
    slope_enc, sum_b, *pieces_c = outs[faces - 1 :]
    got_c = over_faces(pieces_c, -1)
    all_b = from_owners(sum_b)
    enc_grad, grad_keep, grad_give = run(
        on(enc_own_body, faces),
        (grid_latent, *ids, slope_enc, *enc_mine, *(shifted(b, "pipe", 1) for b in enc_mine)),
        [((grid_rows, narrow), BF16), ((half, narrow), F32), ((half, narrow), BF16)],
        scratch=table + [pltpu.VMEM((wide, narrow), F32)],
        flops=sum_flops + 2 * grid_rows * wide * narrow, vmem=grid_vmem,
    )
    outs = tie((enc_grad, grad_keep, grad_give, *got_c))
    enc_grad, grad_keep, grad_give, *got_c = outs
    half_sum, = run(
        add_body, (grad_keep, shifted(grad_give, "pipe", 1)), [((half, narrow), BF16)]
    )
    total = add(from_owners(half_sum), F32)
    grad_w_enc, = run(
        halves_body, (total, shifted(total, "pipe", 1)), [((wide, narrow), F32)], hbm=(0,)
    )
    all_c = from_owners(add([pieces_c[0], *got_c]))

    pieces = []
    for j in range(1, chan_count):
        for k in range(1, faces):
            piece = shifted(enc_mine[k], "chan", j)
            pieces += [piece, shifted(piece, "pipe", 1)]
    others = chan_count - 1
    grad_grid, = run(
        on(enc_other_body, faces, others),
        (*ids, cotangent, enc_grad, enc_all, slope_enc, w_enc, *pieces),
        [((grid_rows, narrow), BF16)],
        scratch=[pltpu.VMEM((mesh_all, narrow * others), BF16), table[1]],
        flops=(sum_flops + 4 * grid_rows * narrow * narrow) * others, vmem=grid_vmem + 4, hbm=(0,),
    )
    groups = (*all_a, *all_b, *all_c)
    layer_shape = ((w_send.shape[0], wide, narrow), F32)
    places = (((3, None), (2, 1)), ((0, 1), (1, 1), (2, 0)), ((0, 0), (1, 0)))
    grad_w_send, grad_w_recv, grad_w_node, grad_w_dec = run(
        on(write_body, places, faces), (*groups, *(shifted(b, "pipe", 1) for b in groups)),
        [layer_shape] * 3 + [((wide, narrow), F32)], hbm=(0, 1, 2, 3),
        scratch=[pltpu.VMEM((3 * half, narrow), BF16)],
    )
    return (
        mixed,
        grad_grid,
        grad_mesh,
        grad_w_enc,
        grad_w_send,
        grad_w_recv,
        grad_w_node,
        grad_w_dec,
    )


def solution(mesh):
    nodes = ("groups", "space", "pipe")
    in_specs = (
        P(nodes, None), P(nodes, None), P(nodes), P(("groups", "space"), "chan"),
        P(("groups", "space"), "pipe"), P(), P(), P(), P(), P(), P(nodes, "chan"),
    )
    out_specs = (
        P(nodes, "chan"), P(nodes, "chan"), P(("groups", "space"), "chan"), P("groups", "chan"),
        P("groups", None, "chan"), P("groups", None, "chan"), P("groups", None, "chan"),
        P("groups", "chan"),
    )
    return jax.shard_map(
        per_device, mesh=mesh, in_specs=in_specs, out_specs=out_specs, check_vma=False
    )
```

```python
import functools

import jax
import jax.numpy as jnp
from jax import lax
from jax.experimental import pallas as pl
from jax.experimental.pallas import tpu as pltpu
from jax.sharding import PartitionSpec as P

F32, BF16 = jnp.float32, jnp.bfloat16
FACE_AXES = ("chan", "pipe")


def shifted(block, axis, distance):
    count = lax.axis_size(axis)
    return lax.ppermute(block, axis, [((i + distance) % count, i) for i in range(count)])


def dot_plain(left, right):
    return jnp.dot(left, right, preferred_element_type=F32)


def dot_back(left, right):
    return lax.dot_general(left, right, (((1,), (1,)), ((), ())), preferred_element_type=F32)


def dot_left(left, right):
    return lax.dot_general(left, right, (((0,), (0,)), ((), ())), preferred_element_type=F32)


def slope_of(values, sigmoid_v):
    return sigmoid_v * (1.0 + values * (1.0 - sigmoid_v))


def one_hot(rows, ids):
    return jnp.where(rows == ids, 1.0, 0.0).astype(BF16)


def pick(values, index, width):
    out = values[:, :width]
    for j in range(1, values.shape[1] // width):
        out = jnp.where(index == j, values[:, j * width : (j + 1) * width], out)
    return out


def in_order(first, mine, other):
    return jnp.where(first, mine, other), jnp.where(first, other, mine)


def widen(parts):
    chan, first = lax.axis_index("chan"), lax.axis_index("pipe") == 0
    count = len(parts) // 2
    pairs = [
        jnp.concatenate(in_order(first, parts[2 * j][...], parts[2 * j + 1][...]), axis=1)
        for j in range(count)
    ]
    out = []
    for place in range(count):
        block = pairs[0]
        for j in range(1, count):
            block = jnp.where(lax.rem(chan + j, count) == place, pairs[j], block)
        out.append(block)
    return jnp.concatenate(out, axis=1)


def own_quarter():
    return lax.axis_index("chan") * lax.axis_size("pipe") + lax.axis_index("pipe")


def run(body, args, outs, scratch=(), flops=0, vmem=17, hbm=(), loads=()):
    args = [
        pltpu.with_memory_space_constraint(a, pltpu.HBM if i in loads else pltpu.VMEM)
        for i, a in enumerate(args)
    ]
    return pl.pallas_call(
        body,
        out_shape=[
            jax.ShapeDtypeStruct(s, d) if i in hbm else pltpu.VMEM(s, d)
            for i, (s, d) in enumerate(outs)
        ],
        in_specs=[pl.BlockSpec(memory_space=pltpu.VMEM)] * len(args),
        out_specs=[pl.BlockSpec(memory_space=pltpu.VMEM)] * len(outs),
        scratch_shapes=list(scratch),
        compiler_params=pltpu.CompilerParams(vmem_limit_bytes=vmem * 1024 * 1024),
        cost_estimate=pl.CostEstimate(flops=flops, bytes_accessed=0, transcendentals=0),
    )(*args)


def rows_at(index, size):
    return pl.ds(pl.multiple_of(index * size, size), size)


def table_rows(mesh_rows, face_ids, node_ids):
    count = lax.axis_size("space")
    turned = face_ids - lax.axis_index("space")
    return jnp.where(turned < 0, turned + count, turned) * mesh_rows + node_ids


def sum_by_node(mesh_rows, face_ids, node_ids, values, keep, give):
    mesh_all, width = keep.shape
    grid_rows = values.shape[0]
    size = 512
    first = lax.axis_index("pipe") == 0
    target = table_rows(mesh_rows, face_ids[...], node_ids[...])

    def step(i, carry):
        ids = lax.broadcasted_iota(jnp.int32, (size, grid_rows), 0) + i * size
        total = dot_plain(one_hot(ids, target), values[...])
        mine, other = in_order(first, total[:, :width], total[:, width:])
        keep[rows_at(i, size), :] = mine.astype(BF16)
        give[rows_at(i, size), :] = other.astype(BF16)
        return carry

    lax.fori_loop(0, mesh_all // size, step, 0)


def encode_body(mesh_rows, x, w, face_ids, node_ids, keep, give, enc):
    size = 512
    columns = pick(w[...], lax.axis_index("chan"), enc.shape[1])

    def step(i, carry):
        z = dot_plain(x[rows_at(i, size), :], columns)
        enc[rows_at(i, size), :] = (z * jax.nn.sigmoid(z)).astype(BF16)
        return carry

    lax.fori_loop(0, x.shape[0] // size, step, 0)
    sum_by_node(mesh_rows, face_ids, node_ids, enc, keep, give)


def join_body(keep, got, *outs):
    rows = outs[0].shape[0]
    for k, out in enumerate(outs):
        at = slice(k * rows, (k + 1) * rows)
        out[...] = (keep[at, :].astype(F32) + got[at, :].astype(F32)).astype(BF16)


def add_all(parts):
    total = parts[0][...].astype(F32)
    for ref in parts[1:]:
        total = total + ref[...].astype(F32)
    return total


def add_body(*refs):
    refs[-1][...] = add_all(refs[:-1]).astype(refs[-1].dtype)


def state_body(mix_scale, mesh, *refs):
    own = pick(mesh[...], lax.axis_index("pipe"), refs[-1].shape[1]).astype(F32)
    refs[-1][...] = (own + mix_scale * add_all(refs[:-1])).astype(BF16)


def project(layer, state_b, w_send, w_recv, send_p, recv_p):
    width, quarter = send_p.shape[1], own_quarter()
    send_p[...] = dot_plain(state_b, pick(w_send[layer], quarter, width)).astype(BF16)
    recv_p[...] = dot_plain(state_b, pick(w_recv[layer], quarter, width))


def first_body(w_send, w_recv, *refs):
    state_0, send_p, recv_p = refs[-3:]
    wide = widen(refs[:-3])
    state_0[...] = wide
    project(0, wide, w_send, w_recv, send_p, recv_p)


def next_body(state, w_node, w_send, w_recv, *refs):
    agg_wide, new_state, send_p, recv_p = refs[-4:]
    wide = widen(refs[:-4])
    agg_wide[...] = wide
    total = state[...].astype(F32) + dot_plain(wide, w_node[0])
    new_state[...] = total
    project(1, total.astype(BF16), w_send, w_recv, send_p, recv_p)


def spot_body(mine, other, spot, spot_row):
    count, mesh_rows = mine.shape
    faces = lax.axis_size("space")
    spare = jnp.zeros((spot.shape[1] - 2 * count, mesh_rows), jnp.int32)
    links = jnp.concatenate([mine[...], other[...], spare], axis=0)
    owner = lax.div(links, mesh_rows)
    local = links - owner * mesh_rows
    step = owner - lax.axis_index("space")
    step = jnp.where(step < 0, step + faces, step)
    place = jnp.where(step == 0, mesh_rows, jnp.where(step == 1, 2 * mesh_rows, 0)) + local
    spot[...] = place.T
    for k in range(2 * count):
        spot_row[:, k * mesh_rows : (k + 1) * mesh_rows] = place[k : k + 1, :]


def stack_body(*refs):
    rows = refs[0].shape[0]
    for k, ref in enumerate(refs[:-1]):
        refs[-1][k * rows : (k + 1) * rows, :] = ref[...]


def pick_body(values, out):
    out[...] = pick(values[...], lax.axis_index("chan"), out.shape[1])


def edge_body(below, own, above, recv_p, spot, agg, slope, halo):
    mesh_rows, width = own.shape
    middle, half = mesh_rows // 2, 3 * mesh_rows // 2
    halo[:mesh_rows, :width] = below[...]
    halo[mesh_rows:, :width] = own[:middle, :]
    halo[:middle, width:] = own[middle:, :]
    halo[middle:, width:] = above[...]
    ids = lax.broadcasted_iota(jnp.int32, (mesh_rows, half), 1)
    count = slope.shape[0]
    total = jnp.zeros(agg.shape, F32)
    for k in range(count):
        place = spot[:, k : k + 1]
        right = place >= half
        both = dot_plain(one_hot(ids, jnp.where(right, place - half, place)), halo[...])
        pre = jnp.where(right, both[:, width:], both[:, :width]) + recv_p[...]
        sigmoid_v = jax.nn.sigmoid(pre)
        total = total + pre * sigmoid_v
        slope[k] = slope_of(pre, sigmoid_v).astype(BF16)
    agg[...] = (total / count).astype(BF16)


def edge_back(grad_b, w_node, slope, spot, spot_row, recv_grad, below, own, above, back):
    mesh_rows, width = recv_grad.shape
    middle, half = mesh_rows // 2, 3 * mesh_rows // 2
    count = slope.shape[0]
    back_agg = dot_back(grad_b, w_node[rows_at(own_quarter(), width), :]) / count
    total = jnp.zeros(recv_grad.shape, F32)
    for k in range(count):
        term = back_agg * slope[k].astype(F32)
        total = total + term
        right = spot[:, k : k + 1] >= half
        rows = slice(k * mesh_rows, (k + 1) * mesh_rows)
        back[rows, :width] = jnp.where(right, 0.0, term).astype(BF16)
        back[rows, width:] = jnp.where(right, term, 0.0).astype(BF16)
    recv_grad[...] = total.astype(BF16)
    place = spot_row[...]
    place = jnp.where(place >= half, place - half, place)
    ids = lax.broadcasted_iota(jnp.int32, (half, count * mesh_rows), 0)
    spread = dot_plain(one_hot(ids, place), back[...])
    below[...] = spread[:mesh_rows, :width].astype(BF16)
    own[:middle, :] = spread[mesh_rows:, :width]
    own[middle:, :] = spread[:middle, width:]
    above[...] = spread[middle:, width:].astype(BF16)


def turn_body(count, state, w_node, w_dec, slope, spot, spot_row, *refs):
    agg, back_dec = refs[:count], refs[count : 2 * count]
    agg_wide, last_b, dec_part, dec_grad, grad = refs[2 * count : 2 * count + 5]
    wide = widen(agg)
    agg_wide[...] = wide
    last = (state[...] + dot_plain(wide, w_node[1])).astype(BF16)
    last_b[...] = last
    z_dec = dot_plain(last, w_dec[...])
    sigmoid_v = jax.nn.sigmoid(z_dec)
    dec_part[...] = pick(z_dec * sigmoid_v, own_quarter(), dec_part.shape[1]).astype(BF16)
    down = (widen(back_dec).astype(F32) * slope_of(z_dec, sigmoid_v)).astype(BF16)
    dec_grad[...] = down
    total = dot_back(down, w_dec[...])
    grad[...] = total
    edge_back(total.astype(BF16), w_node.at[1], slope, spot, spot_row, *refs[2 * count + 5 :])


def through(layer, grad, w_send, w_recv, send_parts, recv_parts, send_wide, recv_wide):
    send, recv = widen(send_parts), widen(recv_parts)
    send_wide[...] = send
    recv_wide[...] = recv
    return grad[...] + dot_back(send, w_send[layer]) + dot_back(recv, w_recv[layer])


def back_body(count, grad, w_send, w_recv, w_node, slope, spot, spot_row, *refs):
    send_parts, recv_parts = refs[:count], refs[count : 2 * count]
    send_wide, recv_wide, new_grad = refs[2 * count : 2 * count + 3]
    total = through(1, grad, w_send, w_recv, send_parts, recv_parts, send_wide, recv_wide)
    new_grad[...] = total
    edge_back(total.astype(BF16), w_node.at[0], slope, spot, spot_row, *refs[2 * count + 3 :])


def last_body(count, mix_scale, grad_1, w_send, w_recv, *refs):
    send_parts, recv_parts = refs[:count], refs[count : 2 * count]
    send_wide, recv_wide, grad, enc_part, enc_all = refs[2 * count :]
    total = through(0, grad_1, w_send, w_recv, send_parts, recv_parts, send_wide, recv_wide)
    grad[...] = total
    scaled = (mix_scale * total).astype(BF16)
    enc_part[...] = pick(scaled, own_quarter(), enc_part.shape[1])
    enc_all[...] = scaled


def put_pair(table, row, column, mine, other):
    rows, width = mine.shape
    low, high = in_order(lax.axis_index("pipe") == 0, mine[...], other[...])
    table[row : row + rows, column : column + width] = low
    table[row : row + rows, column + width : column + 2 * width] = high


def node_values(target, at, table):
    ids = lax.broadcasted_iota(jnp.int32, (table.shape[0], at.size), 0)
    return dot_left(one_hot(ids, target[:, at]), table[...])


def mixed_body(x, w, face_ids, node_ids, mine, other, mixed, slope, table, target):
    put_pair(table, 0, 0, mine, other)
    mesh_rows = mine.shape[0] // lax.axis_size("space")
    target[...] = table_rows(mesh_rows, face_ids[...], node_ids[...])
    size = 512
    chan = lax.axis_index("chan")

    def step(i, carry):
        at = rows_at(i, size)
        got = node_values(target, at, table)
        rows = x[at, :]
        mixed[at, :] = (pick(rows, chan, mixed.shape[1]).astype(F32) + got).astype(BF16)
        z = dot_plain(rows, w[...])
        slope[at, :] = slope_of(z, jax.nn.sigmoid(z)).astype(BF16)
        return carry

    lax.fori_loop(0, x.shape[0] // size, step, 0)


def enc_own_body(
    x, face_ids, node_ids, slope, enc_all, mine, other,
    enc_grad, grad_keep, grad_give, table, target, total,
):
    mesh_rows = enc_all.shape[0]
    chan, pipe = lax.axis_index("chan"), lax.axis_index("pipe")
    table[:mesh_rows, :] = pick(enc_all[...], chan, table.shape[1])
    put_pair(table, mesh_rows, 0, mine, other)
    target[...] = table_rows(mesh_rows, face_ids[...], node_ids[...])
    size = 512
    total[...] = jnp.zeros(total.shape, F32)

    def step(i, carry):
        at = rows_at(i, size)
        own = pick(slope[at, :], chan, enc_grad.shape[1]).astype(F32)
        down = (node_values(target, at, table) * own).astype(BF16)
        enc_grad[at, :] = down
        total[...] += dot_left(x[at, :], down)
        return carry

    lax.fori_loop(0, x.shape[0] // size, step, 0)
    half = grad_keep.shape[0]
    grad_keep[...] = total[rows_at(pipe, half), :]
    grad_give[...] = total[rows_at(1 - pipe, half), :].astype(BF16)


def enc_other_body(count, face_ids, node_ids, cotangent, enc_grad, enc_all, slope, w, *refs):
    blocks = refs[:-3]
    grad_grid, table, target = refs[-3:]
    grid_rows, narrow = cotangent.shape
    mesh_rows = enc_all.shape[0]
    chan = lax.axis_index("chan")
    for j in range(count):
        other = lax.rem(chan + 1 + j, count + 1)
        columns = slice(j * narrow, (j + 1) * narrow)
        table[:mesh_rows, columns] = pick(enc_all[...], other, narrow)
        put_pair(table, mesh_rows, j * narrow, blocks[2 * j], blocks[2 * j + 1])
    target[...] = table_rows(mesh_rows, face_ids[...], node_ids[...])
    size = 512
    w_rows = w[rows_at(chan, narrow), :]
    own_block = pick(w_rows, chan, narrow)

    def step(i, carry):
        at = rows_at(i, size)
        got = node_values(target, at, table)
        total = cotangent[at, :].astype(F32) + dot_back(enc_grad[at, :], own_block)
        for j in range(count):
            other = lax.rem(chan + 1 + j, count + 1)
            part = got[:, j * narrow : (j + 1) * narrow]
            down = (part * pick(slope[at, :], other, narrow).astype(F32)).astype(BF16)
            total = total + dot_back(down, pick(w_rows, other, narrow))
        grad_grid[at, :] = total.astype(BF16)
        return carry

    lax.fori_loop(0, grid_rows // size, step, 0)


def cut_by_face(table, outs):
    count, size = len(outs), outs[0].shape[0]
    face = lax.axis_index("space")
    for k, out in enumerate(outs):
        out[...] = table[rows_at(lax.rem(face + k, count), size), :].astype(out.dtype)


def weight_body(kinds, *refs):
    outs, table = refs[-1 - lax.axis_size("space") : -1], refs[-1]
    rows = table.shape[0] // len(kinds)
    chan, pipe = lax.axis_index("chan"), lax.axis_index("pipe")
    for i, (left, right) in enumerate(kinds):
        one = pick(refs[left][...].astype(BF16), pipe, rows)
        two = pick(refs[right][...].astype(BF16), chan, table.shape[1])
        table[i * rows : (i + 1) * rows, :] = dot_left(one, two).astype(BF16)
    cut_by_face(table, outs)


def cores_body(keep, got, *refs):
    refs[-1][...] = keep[...] + got[...].astype(F32)
    cut_by_face(refs[-1], refs[:-1])


def stack_all_body(*refs):
    row = 0
    for ref in refs[:-1]:
        rows = ref.shape[0]
        refs[-1][row : row + rows, :] = ref[...]
        row += rows


def write_body(places, *refs):
    count = lax.axis_size("space")
    outs, tables = refs[2 * count : -len(places)], refs[-len(places) :]
    pipe, face = lax.axis_index("pipe"), lax.axis_index("space")
    for side in range(2):
        half = pipe if side == 0 else 1 - pipe
        for k in range(count):
            piece = refs[side * count + k]
            block = lax.rem(face + k, count)
            row = 0
            for table in tables:
                size = table.shape[0] // count
                table[rows_at(block, size), :] = piece[row : row + size, :]
                row += size
        for table, items in zip(tables, places):
            rows = table.shape[0] // len(items)
            for j, (out, layer) in enumerate(items):
                to = outs[out] if layer is None else outs[out].at[layer]
                to[rows_at(half, rows), :] = table[j * rows : (j + 1) * rows, :].astype(F32)


def per_device(
    grid_latent, g2m_face, g2m_node, mesh_latent, mesh_links,
    w_enc, w_send, w_recv, w_node, w_dec, cotangent,
):
    tie = lax.optimization_barrier
    faces = lax.axis_size("space")
    pipe_count = lax.axis_size("pipe")
    chan_count = lax.axis_size("chan")
    grid_rows, wide = grid_latent.shape
    mesh_rows, narrow = mesh_latent.shape
    part = narrow // pipe_count
    mesh_all = faces * mesh_rows
    mix_scale = (mesh_rows / (grid_rows * pipe_count)) ** 0.5
    nbrs = mesh_links.shape[1] * pipe_count
    ids = (g2m_face.reshape(1, grid_rows), g2m_node.reshape(1, grid_rows))
    grid_vmem = 14 + mesh_all // 512

    def on(body, *fixed):
        return functools.partial(body, *fixed)

    def over_faces(blocks, step):
        return [shifted(b, "space", step * k) for k, b in enumerate(blocks) if k > 0]

    def face_parts(block):
        out = []
        for j in range(chan_count):
            mine = shifted(block, "chan", j) if j else block
            out += [mine, shifted(mine, "pipe", 1)]
        return out

    def add(parts, kind=BF16):
        return run(add_body, parts, [(parts[0].shape, kind)])[0]

    block = (mesh_rows, part)
    full = (mesh_rows, wide)
    half = wide // pipe_count
    sums = [((mesh_all, part), BF16)] * 2
    sum_flops = 2 * mesh_all * grid_rows * narrow
    edge_flops = 6 * mesh_rows * mesh_rows * nbrs * part
    parts_count = 2 * chan_count

    def join(keep, give):
        return run(join_body, (keep, shifted(give, "pipe", 1)), [(block, BF16)] * faces)

    def neighbours(send_p):
        return shifted(send_p, "space", -1), shifted(send_p, "space", 1)

    def stack(blocks):
        rows, columns = blocks[0].shape
        return run(stack_body, blocks, [((len(blocks) * rows, columns), blocks[0].dtype)])[0]

    keep, give = run(
        on(encode_body, mesh_rows), (grid_latent, w_enc, *ids), sums,
        scratch=[pltpu.VMEM((grid_rows, narrow), BF16)], loads=(0, 1, 2, 3),
        flops=sum_flops + 2 * grid_rows * wide * narrow, vmem=grid_vmem,
    )
    *blocks, cotangent_late, links = tie((*join(keep, give), cotangent, mesh_links.T))
    state_part, = run(
        on(state_body, mix_scale), (mesh_latent, blocks[0], *over_faces(blocks, -1)),
        [(block, BF16)],
    )
    spot, spot_row = run(
        spot_body, (links, shifted(links, "pipe", 1)),
        [((mesh_rows, 8), jnp.int32), ((1, nbrs * mesh_rows), jnp.int32)],
    )
    keep, give = run(
        on(sum_by_node, mesh_rows), (*ids, cotangent_late), sums, flops=sum_flops,
        vmem=grid_vmem, loads=(2,),
    )
    back_blocks = join(keep, give)
    *parts, spot, spot_row = tie((*face_parts(state_part), spot, spot_row))

    def edges(send_p, recv_p, below, above):
        return run(
            edge_body, (below, send_p, above, recv_p, spot),
            [(block, BF16), ((nbrs,) + block, BF16)],
            scratch=[pltpu.VMEM((3 * mesh_rows // 2, 2 * part), BF16)], flops=edge_flops,
        )

    state_0, send_p, recv_p = run(
        first_body, (w_send, w_recv, *parts),
        [(full, BF16), (block, BF16), (block, F32)], flops=4 * mesh_rows * wide * part,
    )
    below, above, *back_blocks = tie((*neighbours(send_p), *back_blocks))
    agg, slope_0 = edges(send_p, recv_p, below, above)
    agg_0, state_1, send_p, recv_p = run(
        next_body, (state_0, w_node, w_send, w_recv, *face_parts(agg)),
        [(full, BF16), (full, F32), (block, BF16), (block, F32)],
        flops=2 * mesh_rows * wide * wide,
    )
    back_own = add([back_blocks[0], *over_faces(back_blocks, -1)])
    below, above, *back_parts = tie((*neighbours(send_p), *face_parts(back_own)))
    agg, slope_1 = edges(send_p, recv_p, below, above)
    back_outs = [(full, F32), (block, BF16), (block, BF16), (block, F32), (block, BF16)]
    back_scratch = [pltpu.VMEM((nbrs * mesh_rows, 2 * part), BF16)]
    agg_1, last_b, dec_part, dec_grad, grad_2, recv_grad, below, own, above = run(
        on(turn_body, parts_count),
        (state_1, w_node, w_dec, slope_1, spot, spot_row, *face_parts(agg), *back_parts),
        [(full, BF16), (full, BF16), (block, BF16), (full, BF16)] + back_outs,
        scratch=back_scratch, flops=edge_flops + 6 * mesh_rows * wide * wide,
    )

    def weights(args, kinds):
        rows = half * len(kinds)
        pieces = run(
            on(weight_body, kinds), args, [((rows // faces, narrow), BF16)] * faces,
            scratch=[pltpu.VMEM((rows, narrow), BF16)], flops=2 * mesh_rows * rows * narrow,
        )
        return add([pieces[0], *over_faces(pieces, -1)])

    def from_owners(piece):
        return [piece] + [shifted(piece, "space", k) for k in range(1, faces)]

    recv_parts = face_parts(recv_grad)
    sums_a = weights((last_b, dec_grad, agg_1, grad_2), ((0, 1), (2, 3)))
    below, above = shifted(below, "space", 1), shifted(above, "space", -1)
    below, above, dec_part, *recv_parts = tie((below, above, dec_part, *recv_parts))
    send_parts = face_parts(add([own, below, above]))
    send_1, recv_1, grad_1, recv_grad, below, own, above = run(
        on(back_body, parts_count),
        (grad_2, w_send, w_recv, w_node, slope_0, spot, spot_row, *send_parts, *recv_parts),
        [(full, BF16), (full, BF16)] + back_outs,
        scratch=back_scratch, flops=edge_flops + 4 * mesh_rows * wide * wide,
    )

    recv_parts = face_parts(recv_grad)
    sums_b = weights((state_1, send_1, recv_1, agg_0, grad_1), ((0, 1), (0, 2), (3, 4)))
    dec_mine = stack(from_owners(dec_part))
    dec_other = shifted(dec_mine, "pipe", 1)
    below, above = shifted(below, "space", 1), shifted(above, "space", -1)
    below, above, sums_a, dec_other, *recv_parts = tie(
        (below, above, sums_a, dec_other, *recv_parts)
    )
    send_parts = face_parts(add([own, below, above]))
    send_0, recv_0, grad_0, enc_part, enc_all = run(
        on(last_body, parts_count, mix_scale), (grad_1, w_send, w_recv, *send_parts, *recv_parts),
        [(full, BF16), (full, BF16), (full, F32), (block, BF16), (full, BF16)],
        flops=4 * mesh_rows * wide * wide,
    )

    enc_got = from_owners(enc_part)[1:]
    sums_c = weights((state_0, send_0, recv_0), ((0, 1), (0, 2)))
    grad_mesh, = run(pick_body, (grad_0,), [((mesh_rows, narrow), F32)], hbm=(0,))
    table = [pltpu.VMEM((mesh_all, narrow), BF16), pltpu.VMEM((1, grid_rows), jnp.int32)]
    mixed, slope_enc = run(
        mixed_body, (grid_latent, w_enc, *ids, dec_mine, dec_other),
        [((grid_rows, narrow), BF16), ((grid_rows, wide), BF16)], scratch=table, hbm=(0,),
        flops=sum_flops + 2 * grid_rows * wide * wide, vmem=grid_vmem,
    )
    *enc_got, slope_enc, grad_mesh = tie((*enc_got, slope_enc, grad_mesh))
    enc_mine = stack(enc_got)
    enc_grad, grad_keep, grad_give = run(
        enc_own_body,
        (grid_latent, *ids, slope_enc, enc_all, enc_mine, shifted(enc_mine, "pipe", 1)),
        [((grid_rows, narrow), BF16), ((half, narrow), F32), ((half, narrow), BF16)],
        scratch=table + [pltpu.VMEM((wide, narrow), F32)],
        flops=sum_flops + 2 * grid_rows * wide * narrow, vmem=grid_vmem,
    )
    enc_grad, grad_keep, grad_give, sums_b = tie((enc_grad, grad_keep, grad_give, sums_b))
    sums_g = run(
        cores_body, (grad_keep, shifted(grad_give, "pipe", 1)),
        [((half // faces, narrow), BF16)] * faces, scratch=[pltpu.VMEM((half, narrow), F32)],
    )
    sums_g = add([sums_g[0], *over_faces(sums_g, -1)])
    sums_all = (sums_a, sums_b, sums_c, sums_g)
    reduced, = run(
        stack_all_body, sums_all, [((sum(a.shape[0] for a in sums_all), narrow), BF16)]
    )
    reduced = from_owners(reduced)
    reduced_other = [shifted(piece, "pipe", 1) for piece in reduced]
    others = chan_count - 1
    pieces = face_parts(enc_mine)[2:]
    grad_grid, = run(
        on(enc_other_body, others),
        (*ids, cotangent, enc_grad, enc_all, slope_enc, w_enc, *pieces),
        [((grid_rows, narrow), BF16)], loads=(2,),
        scratch=[pltpu.VMEM((mesh_all, narrow * others), BF16), table[1]],
        flops=(sum_flops + 4 * grid_rows * narrow * narrow) * others, vmem=grid_vmem + 4, hbm=(0,),
    )
    *reduced_other, grad_grid = tie((*reduced_other, grad_grid))
    layer_shape = ((w_send.shape[0], wide, narrow), F32)
    places = (
        ((3, None), (2, 1)), ((0, 1), (1, 1), (2, 0)), ((0, 0), (1, 0)), ((4, None),),
    )
    grad_w_send, grad_w_recv, grad_w_node, grad_w_dec, grad_w_enc = run(
        on(write_body, places), (*reduced, *reduced_other),
        [layer_shape] * 3 + [((wide, narrow), F32)] * 2, hbm=(0, 1, 2, 3, 4),
        scratch=[pltpu.VMEM((half * len(items), narrow), BF16) for items in places],
    )
    return (
        mixed,
        grad_grid,
        grad_mesh,
        grad_w_enc,
        grad_w_send,
        grad_w_recv,
        grad_w_node,
        grad_w_dec,
    )


def solution(mesh):
    nodes = ("groups", "space", "pipe")
    in_specs = (
        P(nodes, None), P(nodes, None), P(nodes), P(("groups", "space"), "chan"),
        P(("groups", "space"), "pipe"), P(), P(), P(), P(), P(), P(nodes, "chan"),
    )
    out_specs = (
        P(nodes, "chan"), P(nodes, "chan"), P(("groups", "space"), "chan"), P("groups", "chan"),
        P("groups", None, "chan"), P("groups", None, "chan"), P("groups", None, "chan"),
        P("groups", "chan"),
    )
    return jax.shard_map(
        per_device, mesh=mesh, in_specs=in_specs, out_specs=out_specs, check_vma=False
    )
```

```python
import functools

import jax
import jax.numpy as jnp
from jax import lax
from jax.experimental import pallas as pl
from jax.experimental.pallas import tpu as pltpu
from jax.sharding import PartitionSpec as P

F32, BF16 = jnp.float32, jnp.bfloat16
FACE_AXES = ("chan", "pipe")


def shifted(block, axis, distance):
    count = lax.axis_size(axis)
    return lax.ppermute(block, axis, [((i + distance) % count, i) for i in range(count)])


def dot_plain(left, right):
    return jnp.dot(left, right, preferred_element_type=F32)


def dot_back(left, right):
    return lax.dot_general(left, right, (((1,), (1,)), ((), ())), preferred_element_type=F32)


def dot_left(left, right):
    return lax.dot_general(left, right, (((0,), (0,)), ((), ())), preferred_element_type=F32)


def slope_of(values, sigmoid_v):
    return sigmoid_v * (1.0 + values * (1.0 - sigmoid_v))


def one_hot(rows, ids):
    return jnp.where(rows == ids, 1.0, 0.0).astype(BF16)


def pick(values, index, width):
    out = values[:, :width]
    for j in range(1, values.shape[1] // width):
        out = jnp.where(index == j, values[:, j * width : (j + 1) * width], out)
    return out


def in_order(first, mine, other):
    return jnp.where(first, mine, other), jnp.where(first, other, mine)


def widen(parts):
    chan, first = lax.axis_index("chan"), lax.axis_index("pipe") == 0
    count = len(parts) // 2
    pairs = [
        jnp.concatenate(in_order(first, parts[2 * j][...], parts[2 * j + 1][...]), axis=1)
        for j in range(count)
    ]
    out = []
    for place in range(count):
        block = pairs[0]
        for j in range(1, count):
            block = jnp.where(lax.rem(chan + j, count) == place, pairs[j], block)
        out.append(block)
    return jnp.concatenate(out, axis=1)


def own_quarter():
    return lax.axis_index("chan") * lax.axis_size("pipe") + lax.axis_index("pipe")


def run(body, args, outs, scratch=(), flops=0, vmem=17, hbm=(), loads=()):
    args = [
        pltpu.with_memory_space_constraint(a, pltpu.HBM if i in loads else pltpu.VMEM)
        for i, a in enumerate(args)
    ]
    return pl.pallas_call(
        body,
        out_shape=[
            jax.ShapeDtypeStruct(s, d) if i in hbm else pltpu.VMEM(s, d)
            for i, (s, d) in enumerate(outs)
        ],
        in_specs=[pl.BlockSpec(memory_space=pltpu.VMEM)] * len(args),
        out_specs=[pl.BlockSpec(memory_space=pltpu.VMEM)] * len(outs),
        scratch_shapes=list(scratch),
        compiler_params=pltpu.CompilerParams(vmem_limit_bytes=vmem * 1024 * 1024),
        cost_estimate=pl.CostEstimate(flops=flops, bytes_accessed=0, transcendentals=0),
    )(*args)


def rows_at(index, size):
    return pl.ds(pl.multiple_of(index * size, size), size)


def table_rows(mesh_rows, face_ids, node_ids):
    count = lax.axis_size("space")
    turned = face_ids - lax.axis_index("space")
    return jnp.where(turned < 0, turned + count, turned) * mesh_rows + node_ids


def sum_by_node(mesh_rows, face_ids, node_ids, values, keep, give):
    mesh_all, width = keep.shape
    grid_rows = values.shape[0]
    size = 512
    first = lax.axis_index("pipe") == 0
    target = table_rows(mesh_rows, face_ids[...], node_ids[...])

    def step(i, carry):
        ids = lax.broadcasted_iota(jnp.int32, (size, grid_rows), 0) + i * size
        total = dot_plain(one_hot(ids, target), values[...])
        mine, other = in_order(first, total[:, :width], total[:, width:])
        keep[rows_at(i, size), :] = mine.astype(BF16)
        give[rows_at(i, size), :] = other.astype(BF16)
        return carry

    lax.fori_loop(0, mesh_all // size, step, 0)


def encode_body(mesh_rows, x, w, face_ids, node_ids, keep, give, enc):
    size = 512
    columns = pick(w[...], lax.axis_index("chan"), enc.shape[1])

    def step(i, carry):
        z = dot_plain(x[rows_at(i, size), :], columns)
        enc[rows_at(i, size), :] = (z * jax.nn.sigmoid(z)).astype(BF16)
        return carry

    lax.fori_loop(0, x.shape[0] // size, step, 0)
    sum_by_node(mesh_rows, face_ids, node_ids, enc, keep, give)


def join_body(keep, got, *outs):
    rows = outs[0].shape[0]
    for k, out in enumerate(outs):
        at = slice(k * rows, (k + 1) * rows)
        out[...] = (keep[at, :].astype(F32) + got[at, :].astype(F32)).astype(BF16)


def add_all(parts):
    total = parts[0][...].astype(F32)
    for ref in parts[1:]:
        total = total + ref[...].astype(F32)
    return total


def add_body(*refs):
    refs[-1][...] = add_all(refs[:-1]).astype(refs[-1].dtype)


def state_body(mix_scale, mesh, *refs):
    own = pick(mesh[...], lax.axis_index("pipe"), refs[-1].shape[1]).astype(F32)
    refs[-1][...] = (own + mix_scale * add_all(refs[:-1])).astype(BF16)


def project(layer, state_b, w_send, w_recv, send_p, recv_p):
    width, quarter = send_p.shape[1], own_quarter()
    send_p[...] = dot_plain(state_b, pick(w_send[layer], quarter, width)).astype(BF16)
    recv_p[...] = dot_plain(state_b, pick(w_recv[layer], quarter, width))


def first_body(w_send, w_recv, *refs):
    state_0, send_p, recv_p = refs[-3:]
    wide = widen(refs[:-3])
    state_0[...] = wide
    project(0, wide, w_send, w_recv, send_p, recv_p)


def next_body(state, w_node, w_send, w_recv, *refs):
    agg_wide, new_state, send_p, recv_p = refs[-4:]
    wide = widen(refs[:-4])
    agg_wide[...] = wide
    total = state[...].astype(F32) + dot_plain(wide, w_node[0])
    new_state[...] = total
    project(1, total.astype(BF16), w_send, w_recv, send_p, recv_p)


def spot_body(mine, other, spot, spot_row):
    count, mesh_rows = mine.shape
    faces = lax.axis_size("space")
    spare = jnp.zeros((spot.shape[1] - 2 * count, mesh_rows), jnp.int32)
    links = jnp.concatenate([mine[...], other[...], spare], axis=0)
    owner = lax.div(links, mesh_rows)
    local = links - owner * mesh_rows
    step = owner - lax.axis_index("space")
    step = jnp.where(step < 0, step + faces, step)
    place = jnp.where(step == 0, mesh_rows, jnp.where(step == 1, 2 * mesh_rows, 0)) + local
    spot[...] = place.T
    for k in range(2 * count):
        spot_row[:, k * mesh_rows : (k + 1) * mesh_rows] = place[k : k + 1, :]


def stack_body(*refs):
    rows = refs[0].shape[0]
    for k, ref in enumerate(refs[:-1]):
        refs[-1][k * rows : (k + 1) * rows, :] = ref[...]


def pick_body(values, out):
    out[...] = pick(values[...], lax.axis_index("chan"), out.shape[1])


def edge_body(below, own, above, recv_p, spot, agg, slope, halo):
    mesh_rows, width = own.shape
    middle, half = mesh_rows // 2, 3 * mesh_rows // 2
    halo[:mesh_rows, :width] = below[...]
    halo[mesh_rows:, :width] = own[:middle, :]
    halo[:middle, width:] = own[middle:, :]
    halo[middle:, width:] = above[...]
    ids = lax.broadcasted_iota(jnp.int32, (mesh_rows, half), 1)
    count = slope.shape[0]
    total = jnp.zeros(agg.shape, F32)
    for k in range(count):
        place = spot[:, k : k + 1]
        right = place >= half
        both = dot_plain(one_hot(ids, jnp.where(right, place - half, place)), halo[...])
        pre = jnp.where(right, both[:, width:], both[:, :width]) + recv_p[...]
        sigmoid_v = jax.nn.sigmoid(pre)
        total = total + pre * sigmoid_v
        slope[k] = slope_of(pre, sigmoid_v).astype(BF16)
    agg[...] = (total / count).astype(BF16)


def edge_back(grad_b, w_node, slope, spot, spot_row, recv_grad, below, own, above, back):
    mesh_rows, width = recv_grad.shape
    middle, half = mesh_rows // 2, 3 * mesh_rows // 2
    count = slope.shape[0]
    back_agg = dot_back(grad_b, w_node[rows_at(own_quarter(), width), :]) / count
    total = jnp.zeros(recv_grad.shape, F32)
    for k in range(count):
        term = back_agg * slope[k].astype(F32)
        total = total + term
        right = spot[:, k : k + 1] >= half
        rows = slice(k * mesh_rows, (k + 1) * mesh_rows)
        back[rows, :width] = jnp.where(right, 0.0, term).astype(BF16)
        back[rows, width:] = jnp.where(right, term, 0.0).astype(BF16)
    recv_grad[...] = total.astype(BF16)
    place = spot_row[...]
    place = jnp.where(place >= half, place - half, place)
    ids = lax.broadcasted_iota(jnp.int32, (half, count * mesh_rows), 0)
    spread = dot_plain(one_hot(ids, place), back[...])
    below[...] = spread[:mesh_rows, :width].astype(BF16)
    own[:middle, :] = spread[mesh_rows:, :width]
    own[middle:, :] = spread[:middle, width:]
    above[...] = spread[middle:, width:].astype(BF16)


def turn_body(count, state, w_node, w_dec, slope, spot, spot_row, *refs):
    agg, back_dec = refs[:count], refs[count : 2 * count]
    agg_wide, last_b, dec_part, dec_grad, grad = refs[2 * count : 2 * count + 5]
    wide = widen(agg)
    agg_wide[...] = wide
    last = (state[...] + dot_plain(wide, w_node[1])).astype(BF16)
    last_b[...] = last
    z_dec = dot_plain(last, w_dec[...])
    sigmoid_v = jax.nn.sigmoid(z_dec)
    dec_part[...] = pick(z_dec * sigmoid_v, own_quarter(), dec_part.shape[1]).astype(BF16)
    down = (widen(back_dec).astype(F32) * slope_of(z_dec, sigmoid_v)).astype(BF16)
    dec_grad[...] = down
    total = dot_back(down, w_dec[...])
    grad[...] = total
    edge_back(total.astype(BF16), w_node.at[1], slope, spot, spot_row, *refs[2 * count + 5 :])


def through(layer, grad, w_send, w_recv, send_parts, recv_parts, send_wide, recv_wide):
    send, recv = widen(send_parts), widen(recv_parts)
    send_wide[...] = send
    recv_wide[...] = recv
    return grad[...] + dot_back(send, w_send[layer]) + dot_back(recv, w_recv[layer])


def back_body(count, grad, w_send, w_recv, w_node, slope, spot, spot_row, *refs):
    send_parts, recv_parts = refs[:count], refs[count : 2 * count]
    send_wide, recv_wide, new_grad = refs[2 * count : 2 * count + 3]
    total = through(1, grad, w_send, w_recv, send_parts, recv_parts, send_wide, recv_wide)
    new_grad[...] = total
    edge_back(total.astype(BF16), w_node.at[0], slope, spot, spot_row, *refs[2 * count + 3 :])


def last_body(count, mix_scale, grad_1, w_send, w_recv, *refs):
    send_parts, recv_parts = refs[:count], refs[count : 2 * count]
    send_wide, recv_wide, grad, enc_part, enc_all = refs[2 * count :]
    total = through(0, grad_1, w_send, w_recv, send_parts, recv_parts, send_wide, recv_wide)
    grad[...] = total
    scaled = (mix_scale * total).astype(BF16)
    enc_part[...] = pick(scaled, own_quarter(), enc_part.shape[1])
    enc_all[...] = scaled


def put_pair(table, row, column, mine, other):
    rows, width = mine.shape
    low, high = in_order(lax.axis_index("pipe") == 0, mine[...], other[...])
    table[row : row + rows, column : column + width] = low
    table[row : row + rows, column + width : column + 2 * width] = high


def node_values(target, at, table):
    ids = lax.broadcasted_iota(jnp.int32, (table.shape[0], at.size), 0)
    return dot_left(one_hot(ids, target[:, at]), table[...])


def mixed_body(x, w, face_ids, node_ids, mine, other, mixed, slope, table, target):
    put_pair(table, 0, 0, mine, other)
    mesh_rows = mine.shape[0] // lax.axis_size("space")
    target[...] = table_rows(mesh_rows, face_ids[...], node_ids[...])
    size = 512
    chan = lax.axis_index("chan")

    def step(i, carry):
        at = rows_at(i, size)
        got = node_values(target, at, table)
        rows = x[at, :]
        mixed[at, :] = (pick(rows, chan, mixed.shape[1]).astype(F32) + got).astype(BF16)
        z = dot_plain(rows, w[...])
        slope[at, :] = slope_of(z, jax.nn.sigmoid(z)).astype(BF16)
        return carry

    lax.fori_loop(0, x.shape[0] // size, step, 0)


def enc_own_body(
    x, face_ids, node_ids, slope, enc_all, mine, other,
    enc_grad, grad_keep, grad_give, table, target, total,
):
    mesh_rows = enc_all.shape[0]
    chan, pipe = lax.axis_index("chan"), lax.axis_index("pipe")
    table[:mesh_rows, :] = pick(enc_all[...], chan, table.shape[1])
    put_pair(table, mesh_rows, 0, mine, other)
    target[...] = table_rows(mesh_rows, face_ids[...], node_ids[...])
    size = 512
    total[...] = jnp.zeros(total.shape, F32)

    def step(i, carry):
        at = rows_at(i, size)
        own = pick(slope[at, :], chan, enc_grad.shape[1]).astype(F32)
        down = (node_values(target, at, table) * own).astype(BF16)
        enc_grad[at, :] = down
        total[...] += dot_left(x[at, :], down)
        return carry

    lax.fori_loop(0, x.shape[0] // size, step, 0)
    half = grad_keep.shape[0]
    grad_keep[...] = total[rows_at(pipe, half), :]
    grad_give[...] = total[rows_at(1 - pipe, half), :].astype(BF16)


def enc_other_body(count, face_ids, node_ids, cotangent, enc_grad, enc_all, slope, w, *refs):
    blocks = refs[:-3]
    grad_grid, table, target = refs[-3:]
    grid_rows, narrow = cotangent.shape
    mesh_rows = enc_all.shape[0]
    chan = lax.axis_index("chan")
    for j in range(count):
        other = lax.rem(chan + 1 + j, count + 1)
        columns = slice(j * narrow, (j + 1) * narrow)
        table[:mesh_rows, columns] = pick(enc_all[...], other, narrow)
        put_pair(table, mesh_rows, j * narrow, blocks[2 * j], blocks[2 * j + 1])
    target[...] = table_rows(mesh_rows, face_ids[...], node_ids[...])
    size = 512
    w_rows = w[rows_at(chan, narrow), :]
    own_block = pick(w_rows, chan, narrow)

    def step(i, carry):
        at = rows_at(i, size)
        got = node_values(target, at, table)
        total = cotangent[at, :].astype(F32) + dot_back(enc_grad[at, :], own_block)
        for j in range(count):
            other = lax.rem(chan + 1 + j, count + 1)
            part = got[:, j * narrow : (j + 1) * narrow]
            down = (part * pick(slope[at, :], other, narrow).astype(F32)).astype(BF16)
            total = total + dot_back(down, pick(w_rows, other, narrow))
        grad_grid[at, :] = total.astype(BF16)
        return carry

    lax.fori_loop(0, grid_rows // size, step, 0)


def cut_by_face(table, outs):
    count, size = len(outs), outs[0].shape[0]
    face = lax.axis_index("space")
    for k, out in enumerate(outs):
        out[...] = table[rows_at(lax.rem(face + k, count), size), :].astype(out.dtype)


def weight_body(kinds, *refs):
    outs, table = refs[-1 - lax.axis_size("space") : -1], refs[-1]
    rows = table.shape[0] // len(kinds)
    chan, pipe = lax.axis_index("chan"), lax.axis_index("pipe")
    for i, (left, right) in enumerate(kinds):
        one = pick(refs[left][...].astype(BF16), pipe, rows)
        two = pick(refs[right][...].astype(BF16), chan, table.shape[1])
        table[i * rows : (i + 1) * rows, :] = dot_left(one, two).astype(BF16)
    cut_by_face(table, outs)


def cores_body(keep, got, *refs):
    refs[-1][...] = keep[...] + got[...].astype(F32)
    cut_by_face(refs[-1], refs[:-1])


def stack_all_body(*refs):
    row = 0
    for ref in refs[:-1]:
        rows = ref.shape[0]
        refs[-1][row : row + rows, :] = ref[...]
        row += rows


def write_body(places, *refs):
    count = lax.axis_size("space")
    outs, tables = refs[2 * count : -len(places)], refs[-len(places) :]
    pipe, face = lax.axis_index("pipe"), lax.axis_index("space")
    for side in range(2):
        half = pipe if side == 0 else 1 - pipe
        for k in range(count):
            piece = refs[side * count + k]
            block = lax.rem(face + k, count)
            row = 0
            for table in tables:
                size = table.shape[0] // count
                table[rows_at(block, size), :] = piece[row : row + size, :]
                row += size
        for table, items in zip(tables, places):
            rows = table.shape[0] // len(items)
            for j, (out, layer) in enumerate(items):
                to = outs[out] if layer is None else outs[out].at[layer]
                to[rows_at(half, rows), :] = table[j * rows : (j + 1) * rows, :].astype(F32)


def per_device(
    grid_latent, g2m_face, g2m_node, mesh_latent, mesh_links,
    w_enc, w_send, w_recv, w_node, w_dec, cotangent,
):
    tie = lax.optimization_barrier
    faces = lax.axis_size("space")
    pipe_count = lax.axis_size("pipe")
    chan_count = lax.axis_size("chan")
    grid_rows, wide = grid_latent.shape
    mesh_rows, narrow = mesh_latent.shape
    part = narrow // pipe_count
    mesh_all = faces * mesh_rows
    mix_scale = (mesh_rows / (grid_rows * pipe_count)) ** 0.5
    nbrs = mesh_links.shape[1] * pipe_count
    ids = (g2m_face.reshape(1, grid_rows), g2m_node.reshape(1, grid_rows))
    grid_vmem = 14 + mesh_all // 512

    def on(body, *fixed):
        return functools.partial(body, *fixed)

    def over_faces(blocks, step):
        return [shifted(b, "space", step * k) for k, b in enumerate(blocks) if k > 0]

    def face_parts(block):
        out = []
        for j in range(chan_count):
            mine = shifted(block, "chan", j) if j else block
            out += [mine, shifted(mine, "pipe", 1)]
        return out

    def add(parts, kind=BF16):
        return run(add_body, parts, [(parts[0].shape, kind)])[0]

    block = (mesh_rows, part)
    full = (mesh_rows, wide)
    half = wide // pipe_count
    sums = [((mesh_all, part), BF16)] * 2
    sum_flops = 2 * mesh_all * grid_rows * narrow
    edge_flops = 6 * mesh_rows * mesh_rows * nbrs * part
    parts_count = 2 * chan_count

    near = [k for k in range(1, faces) if k in (1, faces - 1)]
    far = [k for k in range(1, faces) if k not in near]

    def join(keep, give):
        return run(join_body, (keep, shifted(give, "pipe", 1)), [(block, BF16)] * faces)

    def neighbours(send_p):
        return shifted(send_p, "space", -1), shifted(send_p, "space", 1)

    def stack(blocks):
        rows, columns = blocks[0].shape
        return run(stack_body, blocks, [((len(blocks) * rows, columns), blocks[0].dtype)])[0]

    keep, give = run(
        on(encode_body, mesh_rows), (grid_latent, w_enc, *ids), sums,
        scratch=[pltpu.VMEM((grid_rows, narrow), BF16)], loads=(0, 1, 2, 3),
        flops=sum_flops + 2 * grid_rows * wide * narrow, vmem=grid_vmem,
    )
    *blocks, cotangent_late, links = tie((*join(keep, give), cotangent, mesh_links.T))
    state_part, = run(
        on(state_body, mix_scale), (mesh_latent, blocks[0], *over_faces(blocks, -1)),
        [(block, BF16)],
    )
    spot, spot_row = run(
        spot_body, (links, shifted(links, "pipe", 1)),
        [((mesh_rows, 8), jnp.int32), ((1, nbrs * mesh_rows), jnp.int32)],
    )
    state_part, spot, spot_row = tie((state_part, spot, spot_row))
    keep, give = run(
        on(sum_by_node, mesh_rows), (*ids, cotangent_late), sums, flops=sum_flops,
        vmem=grid_vmem, loads=(2,),
    )
    back_blocks = join(keep, give)
    parts = face_parts(state_part)

    def edges(send_p, recv_p, below, above):
        return run(
            edge_body, (below, send_p, above, recv_p, spot),
            [(block, BF16), ((nbrs,) + block, BF16)],
            scratch=[pltpu.VMEM((3 * mesh_rows // 2, 2 * part), BF16)], flops=edge_flops,
        )

    state_0, send_p, recv_p = run(
        first_body, (w_send, w_recv, *parts),
        [(full, BF16), (block, BF16), (block, F32)], flops=4 * mesh_rows * wide * part,
    )
    agg, slope_0 = edges(send_p, recv_p, *neighbours(send_p))
    agg, *back_blocks = tie((agg, *back_blocks))
    back_near = [shifted(back_blocks[k], "space", -k) for k in near]
    outs = tie((*face_parts(agg), *back_near))
    agg_parts, back_near = outs[:parts_count], outs[parts_count:]
    agg_0, state_1, send_p, recv_p = run(
        next_body, (state_0, w_node, w_send, w_recv, *agg_parts),
        [(full, BF16), (full, F32), (block, BF16), (block, F32)],
        flops=2 * mesh_rows * wide * wide,
    )
    back_far = [shifted(back_blocks[k], "space", -k) for k in far]
    below, above, *back_far = tie((*neighbours(send_p), *back_far))
    agg, slope_1 = edges(send_p, recv_p, below, above)
    back_parts = face_parts(add([back_blocks[0], *back_near, *back_far]))
    back_outs = [(full, F32), (block, BF16), (block, BF16), (block, F32), (block, BF16)]
    back_scratch = [pltpu.VMEM((nbrs * mesh_rows, 2 * part), BF16)]
    agg_1, last_b, dec_part, dec_grad, grad_2, recv_grad, below, own, above = run(
        on(turn_body, parts_count),
        (state_1, w_node, w_dec, slope_1, spot, spot_row, *face_parts(agg), *back_parts),
        [(full, BF16), (full, BF16), (block, BF16), (full, BF16)] + back_outs,
        scratch=back_scratch, flops=edge_flops + 6 * mesh_rows * wide * wide,
    )

    def weights(args, kinds):
        rows = half * len(kinds)
        pieces = run(
            on(weight_body, kinds), args, [((rows // faces, narrow), BF16)] * faces,
            scratch=[pltpu.VMEM((rows, narrow), BF16)], flops=2 * mesh_rows * rows * narrow,
        )
        return add([pieces[0], *over_faces(pieces, -1)])

    def from_owners(piece):
        return [piece] + [shifted(piece, "space", k) for k in range(1, faces)]

    recv_parts = face_parts(recv_grad)
    below, above = shifted(below, "space", 1), shifted(above, "space", -1)
    below, above, dec_part, *recv_parts = tie((below, above, dec_part, *recv_parts))
    dec_near = [shifted(dec_part, "space", k) for k in near]
    outs = tie((*face_parts(add([own, below, above])), *dec_near))
    send_parts, dec_near = outs[:parts_count], outs[parts_count:]
    send_1, recv_1, grad_1, recv_grad, below, own, above = run(
        on(back_body, parts_count),
        (grad_2, w_send, w_recv, w_node, slope_0, spot, spot_row, *send_parts, *recv_parts),
        [(full, BF16), (full, BF16)] + back_outs,
        scratch=back_scratch, flops=edge_flops + 4 * mesh_rows * wide * wide,
    )

    recv_parts = face_parts(recv_grad)
    below, above = shifted(below, "space", 1), shifted(above, "space", -1)
    below, above, dec_last, *recv_parts = tie((below, above, dec_part, *recv_parts))
    dec_far = [shifted(dec_last, "space", k) for k in far]
    outs = tie((*face_parts(add([own, below, above])), *dec_far))
    send_parts, dec_far = outs[:parts_count], outs[parts_count:]
    dec_all = dict(zip(near + far, [*dec_near, *dec_far]))
    dec_mine = stack([dec_part] + [dec_all[k] for k in range(1, faces)])
    dec_other = shifted(dec_mine, "pipe", 1)
    send_0, recv_0, grad_0, enc_part, enc_all = run(
        on(last_body, parts_count, mix_scale), (grad_1, w_send, w_recv, *send_parts, *recv_parts),
        [(full, BF16), (full, BF16), (full, F32), (block, BF16), (full, BF16)],
        flops=4 * mesh_rows * wide * wide,
    )

    enc_got = from_owners(enc_part)[1:]
    sums_b = weights(
        (state_1, send_1, recv_1, agg_0, grad_1, state_0, send_0, recv_0)
        + (last_b, dec_grad, agg_1, grad_2),
        ((0, 1), (0, 2), (3, 4), (5, 6), (5, 7), (8, 9), (10, 11)),
    )
    grad_mesh, = run(pick_body, (grad_0,), [((mesh_rows, narrow), F32)], hbm=(0,))
    table = [pltpu.VMEM((mesh_all, narrow), BF16), pltpu.VMEM((1, grid_rows), jnp.int32)]
    mixed, slope_enc = run(
        mixed_body, (grid_latent, w_enc, *ids, dec_mine, dec_other),
        [((grid_rows, narrow), BF16), ((grid_rows, wide), BF16)], scratch=table, hbm=(0,),
        flops=sum_flops + 2 * grid_rows * wide * wide, vmem=grid_vmem,
    )
    *enc_got, slope_enc, grad_mesh = tie((*enc_got, slope_enc, grad_mesh))
    enc_mine = stack(enc_got)
    enc_grad, grad_keep, grad_give = run(
        enc_own_body,
        (grid_latent, *ids, slope_enc, enc_all, enc_mine, shifted(enc_mine, "pipe", 1)),
        [((grid_rows, narrow), BF16), ((half, narrow), F32), ((half, narrow), BF16)],
        scratch=table + [pltpu.VMEM((wide, narrow), F32)],
        flops=sum_flops + 2 * grid_rows * wide * narrow, vmem=grid_vmem,
    )
    sums_g = run(
        cores_body, (grad_keep, shifted(grad_give, "pipe", 1)),
        [((half // faces, narrow), BF16)] * faces, scratch=[pltpu.VMEM((half, narrow), F32)],
    )
    *sums_g, sums_b = tie((*sums_g, sums_b))
    sums_g = add([sums_g[0], *over_faces(sums_g, -1)])
    sums_all = (sums_b, sums_g)
    reduced, = run(
        stack_all_body, sums_all, [((sum(a.shape[0] for a in sums_all), narrow), BF16)]
    )
    reduced = from_owners(reduced)
    others = chan_count - 1
    pieces = face_parts(enc_mine)[2:]
    grad_grid, = run(
        on(enc_other_body, others),
        (*ids, cotangent, enc_grad, enc_all, slope_enc, w_enc, *pieces),
        [((grid_rows, narrow), BF16)], loads=(2,),
        scratch=[pltpu.VMEM((mesh_all, narrow * others), BF16), table[1]],
        flops=(sum_flops + 4 * grid_rows * narrow * narrow) * others, vmem=grid_vmem + 4, hbm=(0,),
    )
    *reduced, grad_grid = tie((*reduced, grad_grid))
    reduced_other = [shifted(piece, "pipe", 1) for piece in reduced]
    layer_shape = ((w_send.shape[0], wide, narrow), F32)
    places = (
        ((0, 1), (1, 1), (2, 0), (0, 0), (1, 0), (3, None), (2, 1)), ((4, None),),
    )
    grad_w_send, grad_w_recv, grad_w_node, grad_w_dec, grad_w_enc = run(
        on(write_body, places), (*reduced, *reduced_other),
        [layer_shape] * 3 + [((wide, narrow), F32)] * 2, hbm=(0, 1, 2, 3, 4),
        scratch=[pltpu.VMEM((half * len(items), narrow), BF16) for items in places],
    )
    return (
        mixed,
        grad_grid,
        grad_mesh,
        grad_w_enc,
        grad_w_send,
        grad_w_recv,
        grad_w_node,
        grad_w_dec,
    )


def solution(mesh):
    nodes = ("groups", "space", "pipe")
    in_specs = (
        P(nodes, None), P(nodes, None), P(nodes), P(("groups", "space"), "chan"),
        P(("groups", "space"), "pipe"), P(), P(), P(), P(), P(), P(nodes, "chan"),
    )
    out_specs = (
        P(nodes, "chan"), P(nodes, "chan"), P(("groups", "space"), "chan"), P("groups", "chan"),
        P("groups", None, "chan"), P("groups", None, "chan"), P("groups", None, "chan"),
        P("groups", "chan"),
    )
    return jax.shard_map(
        per_device, mesh=mesh, in_specs=in_specs, out_specs=out_specs, check_vma=False
    )
```

```python
import functools

import jax
import jax.numpy as jnp
from jax import lax
from jax.experimental import pallas as pl
from jax.experimental.pallas import tpu as pltpu
from jax.sharding import PartitionSpec as P

F32, BF16 = jnp.float32, jnp.bfloat16
FACE_AXES = ("chan", "pipe")


def shifted(block, axis, distance):
    count = lax.axis_size(axis)
    return lax.ppermute(block, axis, [((i + distance) % count, i) for i in range(count)])


def dot_plain(left, right):
    return jnp.dot(left, right, preferred_element_type=F32)


def dot_back(left, right):
    return lax.dot_general(left, right, (((1,), (1,)), ((), ())), preferred_element_type=F32)


def dot_left(left, right):
    return lax.dot_general(left, right, (((0,), (0,)), ((), ())), preferred_element_type=F32)


def slope_of(values, sigmoid_v):
    return sigmoid_v * (1.0 + values * (1.0 - sigmoid_v))


def one_hot(rows, ids):
    return jnp.where(rows == ids, 1.0, 0.0).astype(BF16)


def pick(values, index, width):
    out = values[:, :width]
    for j in range(1, values.shape[1] // width):
        out = jnp.where(index == j, values[:, j * width : (j + 1) * width], out)
    return out


def in_order(first, mine, other):
    return jnp.where(first, mine, other), jnp.where(first, other, mine)


def widen(parts):
    chan, first = lax.axis_index("chan"), lax.axis_index("pipe") == 0
    count = len(parts) // 2
    pairs = [
        jnp.concatenate(in_order(first, parts[2 * j][...], parts[2 * j + 1][...]), axis=1)
        for j in range(count)
    ]
    out = []
    for place in range(count):
        block = pairs[0]
        for j in range(1, count):
            block = jnp.where(lax.rem(chan + j, count) == place, pairs[j], block)
        out.append(block)
    return jnp.concatenate(out, axis=1)


def own_quarter():
    return lax.axis_index("chan") * lax.axis_size("pipe") + lax.axis_index("pipe")


def run(body, args, outs, scratch=(), flops=0, vmem=17, hbm=(), loads=()):
    args = [
        pltpu.with_memory_space_constraint(a, pltpu.HBM if i in loads else pltpu.VMEM)
        for i, a in enumerate(args)
    ]
    return pl.pallas_call(
        body,
        out_shape=[
            jax.ShapeDtypeStruct(s, d) if i in hbm else pltpu.VMEM(s, d)
            for i, (s, d) in enumerate(outs)
        ],
        in_specs=[pl.BlockSpec(memory_space=pltpu.VMEM)] * len(args),
        out_specs=[pl.BlockSpec(memory_space=pltpu.VMEM)] * len(outs),
        scratch_shapes=list(scratch),
        compiler_params=pltpu.CompilerParams(vmem_limit_bytes=vmem * 1024 * 1024),
        cost_estimate=pl.CostEstimate(flops=flops, bytes_accessed=0, transcendentals=0),
    )(*args)


def rows_at(index, size):
    return pl.ds(pl.multiple_of(index * size, size), size)


def table_rows(mesh_rows, face_ids, node_ids):
    count = lax.axis_size("space")
    turned = face_ids - lax.axis_index("space")
    return jnp.where(turned < 0, turned + count, turned) * mesh_rows + node_ids


def sum_by_node(mesh_rows, face_ids, node_ids, values, keep, give):
    mesh_all, width = keep.shape
    grid_rows = values.shape[0]
    size = 512
    first = lax.axis_index("pipe") == 0
    target = table_rows(mesh_rows, face_ids[...], node_ids[...])

    def step(i, carry):
        ids = lax.broadcasted_iota(jnp.int32, (size, grid_rows), 0) + i * size
        total = dot_plain(one_hot(ids, target), values[...])
        mine, other = in_order(first, total[:, :width], total[:, width:])
        keep[rows_at(i, size), :] = mine.astype(BF16)
        give[rows_at(i, size), :] = other.astype(BF16)
        return carry

    lax.fori_loop(0, mesh_all // size, step, 0)


def encode_body(mesh_rows, x, w, face_ids, node_ids, keep, give, enc):
    size = 512
    columns = pick(w[...], lax.axis_index("chan"), enc.shape[1])

    def step(i, carry):
        z = dot_plain(x[rows_at(i, size), :], columns)
        enc[rows_at(i, size), :] = (z * jax.nn.sigmoid(z)).astype(BF16)
        return carry

    lax.fori_loop(0, x.shape[0] // size, step, 0)
    sum_by_node(mesh_rows, face_ids, node_ids, enc, keep, give)


def join_body(keep, got, *outs):
    rows = outs[0].shape[0]
    for k, out in enumerate(outs):
        at = slice(k * rows, (k + 1) * rows)
        out[...] = (keep[at, :].astype(F32) + got[at, :].astype(F32)).astype(BF16)


def add_all(parts):
    total = parts[0][...].astype(F32)
    for ref in parts[1:]:
        total = total + ref[...].astype(F32)
    return total


def add_body(*refs):
    refs[-1][...] = add_all(refs[:-1]).astype(refs[-1].dtype)


def state_body(mix_scale, mesh, *refs):
    own = pick(mesh[...], lax.axis_index("pipe"), refs[-1].shape[1]).astype(F32)
    refs[-1][...] = (own + mix_scale * add_all(refs[:-1])).astype(BF16)


def project(layer, state_b, w_send, w_recv, send_p, recv_p):
    width, quarter = send_p.shape[1], own_quarter()
    send_p[...] = dot_plain(state_b, pick(w_send[layer], quarter, width)).astype(BF16)
    recv_p[...] = dot_plain(state_b, pick(w_recv[layer], quarter, width))


def first_body(w_send, w_recv, *refs):
    state_0, send_p, recv_p = refs[-3:]
    wide = widen(refs[:-3])
    state_0[...] = wide
    project(0, wide, w_send, w_recv, send_p, recv_p)


def next_body(state, w_node, w_send, w_recv, *refs):
    agg_wide, new_state, send_p, recv_p = refs[-4:]
    wide = widen(refs[:-4])
    agg_wide[...] = wide
    total = state[...].astype(F32) + dot_plain(wide, w_node[0])
    new_state[...] = total
    project(1, total.astype(BF16), w_send, w_recv, send_p, recv_p)


def spot_body(mine, other, spot, spot_row):
    count, mesh_rows = mine.shape
    faces = lax.axis_size("space")
    spare = jnp.zeros((spot.shape[1] - 2 * count, mesh_rows), jnp.int32)
    links = jnp.concatenate([mine[...], other[...], spare], axis=0)
    owner = lax.div(links, mesh_rows)
    local = links - owner * mesh_rows
    step = owner - lax.axis_index("space")
    step = jnp.where(step < 0, step + faces, step)
    place = jnp.where(step == 0, mesh_rows, jnp.where(step == 1, 2 * mesh_rows, 0)) + local
    spot[...] = place.T
    for k in range(2 * count):
        spot_row[:, k * mesh_rows : (k + 1) * mesh_rows] = place[k : k + 1, :]


def stack_body(*refs):
    rows = refs[0].shape[0]
    for k, ref in enumerate(refs[:-1]):
        refs[-1][k * rows : (k + 1) * rows, :] = ref[...]


def pick_body(values, out):
    out[...] = pick(values[...], lax.axis_index("chan"), out.shape[1])


def edge_body(below, own, above, recv_p, spot, agg, slope, halo):
    mesh_rows, width = own.shape
    middle, half = mesh_rows // 2, 3 * mesh_rows // 2
    halo[:mesh_rows, :width] = below[...]
    halo[mesh_rows:, :width] = own[:middle, :]
    halo[:middle, width:] = own[middle:, :]
    halo[middle:, width:] = above[...]
    ids = lax.broadcasted_iota(jnp.int32, (mesh_rows, half), 1)
    count = slope.shape[0]
    total = jnp.zeros(agg.shape, F32)
    for k in range(count):
        place = spot[:, k : k + 1]
        right = place >= half
        both = dot_plain(one_hot(ids, jnp.where(right, place - half, place)), halo[...])
        pre = jnp.where(right, both[:, width:], both[:, :width]) + recv_p[...]
        sigmoid_v = jax.nn.sigmoid(pre)
        total = total + pre * sigmoid_v
        slope[k] = slope_of(pre, sigmoid_v).astype(BF16)
    agg[...] = (total / count).astype(BF16)


def edge_back(grad_b, w_node, slope, spot, spot_row, recv_grad, below, own, above, back):
    mesh_rows, width = recv_grad.shape
    middle, half = mesh_rows // 2, 3 * mesh_rows // 2
    count = slope.shape[0]
    back_agg = dot_back(grad_b, w_node[rows_at(own_quarter(), width), :]) / count
    total = jnp.zeros(recv_grad.shape, F32)
    for k in range(count):
        term = back_agg * slope[k].astype(F32)
        total = total + term
        right = spot[:, k : k + 1] >= half
        rows = slice(k * mesh_rows, (k + 1) * mesh_rows)
        back[rows, :width] = jnp.where(right, 0.0, term).astype(BF16)
        back[rows, width:] = jnp.where(right, term, 0.0).astype(BF16)
    recv_grad[...] = total.astype(BF16)
    place = spot_row[...]
    place = jnp.where(place >= half, place - half, place)
    ids = lax.broadcasted_iota(jnp.int32, (half, count * mesh_rows), 0)
    spread = dot_plain(one_hot(ids, place), back[...])
    below[...] = spread[:mesh_rows, :width].astype(BF16)
    own[:middle, :] = spread[mesh_rows:, :width]
    own[middle:, :] = spread[:middle, width:]
    above[...] = spread[middle:, width:].astype(BF16)


def turn_body(count, state, w_node, w_dec, slope, spot, spot_row, *refs):
    agg, back_dec = refs[:count], refs[count : 2 * count]
    agg_wide, last_b, dec_part, dec_grad, grad = refs[2 * count : 2 * count + 5]
    wide = widen(agg)
    agg_wide[...] = wide
    last = (state[...] + dot_plain(wide, w_node[1])).astype(BF16)
    last_b[...] = last
    z_dec = dot_plain(last, w_dec[...])
    sigmoid_v = jax.nn.sigmoid(z_dec)
    dec_part[...] = pick(z_dec * sigmoid_v, own_quarter(), dec_part.shape[1]).astype(BF16)
    down = (widen(back_dec).astype(F32) * slope_of(z_dec, sigmoid_v)).astype(BF16)
    dec_grad[...] = down
    total = dot_back(down, w_dec[...])
    grad[...] = total
    edge_back(total.astype(BF16), w_node.at[1], slope, spot, spot_row, *refs[2 * count + 5 :])


def through(layer, grad, w_send, w_recv, send_parts, recv_parts, send_wide, recv_wide):
    send, recv = widen(send_parts), widen(recv_parts)
    send_wide[...] = send
    recv_wide[...] = recv
    return grad[...] + dot_back(send, w_send[layer]) + dot_back(recv, w_recv[layer])


def back_body(count, grad, w_send, w_recv, w_node, slope, spot, spot_row, *refs):
    send_parts, recv_parts = refs[:count], refs[count : 2 * count]
    send_wide, recv_wide, new_grad = refs[2 * count : 2 * count + 3]
    total = through(1, grad, w_send, w_recv, send_parts, recv_parts, send_wide, recv_wide)
    new_grad[...] = total
    edge_back(total.astype(BF16), w_node.at[0], slope, spot, spot_row, *refs[2 * count + 3 :])


def last_body(count, mix_scale, grad_1, w_send, w_recv, *refs):
    send_parts, recv_parts = refs[:count], refs[count : 2 * count]
    send_wide, recv_wide, grad, enc_part, enc_all = refs[2 * count :]
    total = through(0, grad_1, w_send, w_recv, send_parts, recv_parts, send_wide, recv_wide)
    grad[...] = total
    scaled = (mix_scale * total).astype(BF16)
    enc_part[...] = pick(scaled, own_quarter(), enc_part.shape[1])
    enc_all[...] = scaled


def put_pair(table, row, column, mine, other):
    rows, width = mine.shape
    low, high = in_order(lax.axis_index("pipe") == 0, mine[...], other[...])
    table[row : row + rows, column : column + width] = low
    table[row : row + rows, column + width : column + 2 * width] = high


def node_values(target, at, table):
    ids = lax.broadcasted_iota(jnp.int32, (table.shape[0], at.size), 0)
    return dot_left(one_hot(ids, target[:, at]), table[...])


def mixed_body(x, w, face_ids, node_ids, mine, other, mixed, slope, table, target):
    put_pair(table, 0, 0, mine, other)
    mesh_rows = mine.shape[0] // lax.axis_size("space")
    target[...] = table_rows(mesh_rows, face_ids[...], node_ids[...])
    size = 512
    chan = lax.axis_index("chan")

    def step(i, carry):
        at = rows_at(i, size)
        got = node_values(target, at, table)
        rows = x[at, :]
        mixed[at, :] = (pick(rows, chan, mixed.shape[1]).astype(F32) + got).astype(BF16)
        z = dot_plain(rows, w[...])
        slope[at, :] = slope_of(z, jax.nn.sigmoid(z)).astype(BF16)
        return carry

    lax.fori_loop(0, x.shape[0] // size, step, 0)


def enc_own_body(
    x, face_ids, node_ids, slope, enc_all, mine, other,
    enc_grad, grad_keep, grad_give, table, target, total,
):
    mesh_rows = enc_all.shape[0]
    chan, pipe = lax.axis_index("chan"), lax.axis_index("pipe")
    table[:mesh_rows, :] = pick(enc_all[...], chan, table.shape[1])
    put_pair(table, mesh_rows, 0, mine, other)
    target[...] = table_rows(mesh_rows, face_ids[...], node_ids[...])
    size = 512
    total[...] = jnp.zeros(total.shape, F32)

    def step(i, carry):
        at = rows_at(i, size)
        own = pick(slope[at, :], chan, enc_grad.shape[1]).astype(F32)
        down = (node_values(target, at, table) * own).astype(BF16)
        enc_grad[at, :] = down
        total[...] += dot_left(x[at, :], down)
        return carry

    lax.fori_loop(0, x.shape[0] // size, step, 0)
    half = grad_keep.shape[0]
    grad_keep[...] = total[rows_at(pipe, half), :]
    grad_give[...] = total[rows_at(1 - pipe, half), :].astype(BF16)


def enc_other_body(count, face_ids, node_ids, cotangent, enc_grad, enc_all, slope, w, *refs):
    blocks = refs[:-3]
    grad_grid, table, target = refs[-3:]
    grid_rows, narrow = cotangent.shape
    mesh_rows = enc_all.shape[0]
    chan = lax.axis_index("chan")
    for j in range(count):
        other = lax.rem(chan + 1 + j, count + 1)
        columns = slice(j * narrow, (j + 1) * narrow)
        table[:mesh_rows, columns] = pick(enc_all[...], other, narrow)
        put_pair(table, mesh_rows, j * narrow, blocks[2 * j], blocks[2 * j + 1])
    target[...] = table_rows(mesh_rows, face_ids[...], node_ids[...])
    size = 512
    w_rows = w[rows_at(chan, narrow), :]
    own_block = pick(w_rows, chan, narrow)

    def step(i, carry):
        at = rows_at(i, size)
        got = node_values(target, at, table)
        total = cotangent[at, :].astype(F32) + dot_back(enc_grad[at, :], own_block)
        for j in range(count):
            other = lax.rem(chan + 1 + j, count + 1)
            part = got[:, j * narrow : (j + 1) * narrow]
            down = (part * pick(slope[at, :], other, narrow).astype(F32)).astype(BF16)
            total = total + dot_back(down, pick(w_rows, other, narrow))
        grad_grid[at, :] = total.astype(BF16)
        return carry

    lax.fori_loop(0, grid_rows // size, step, 0)


def cut_by_face(table, outs):
    count, size = len(outs), outs[0].shape[0]
    face = lax.axis_index("space")
    for k, out in enumerate(outs):
        out[...] = table[rows_at(lax.rem(face + k, count), size), :].astype(out.dtype)


def weight_body(kinds, *refs):
    outs, table = refs[-1 - lax.axis_size("space") : -1], refs[-1]
    rows = table.shape[0] // len(kinds)
    chan, pipe = lax.axis_index("chan"), lax.axis_index("pipe")
    for i, (left, right) in enumerate(kinds):
        one = pick(refs[left][...].astype(BF16), pipe, rows)
        two = pick(refs[right][...].astype(BF16), chan, table.shape[1])
        table[i * rows : (i + 1) * rows, :] = dot_left(one, two).astype(BF16)
    cut_by_face(table, outs)


def cores_body(keep, got, *refs):
    refs[-1][...] = keep[...] + got[...].astype(F32)
    cut_by_face(refs[-1], refs[:-1])


def stack_all_body(*refs):
    row = 0
    for ref in refs[:-1]:
        rows = ref.shape[0]
        refs[-1][row : row + rows, :] = ref[...]
        row += rows


def write_body(places, *refs):
    count = lax.axis_size("space")
    outs, tables = refs[2 * count : -len(places)], refs[-len(places) :]
    pipe, face = lax.axis_index("pipe"), lax.axis_index("space")
    for side in range(2):
        half = pipe if side == 0 else 1 - pipe
        for k in range(count):
            piece = refs[side * count + k]
            block = lax.rem(face + k, count)
            row = 0
            for table in tables:
                size = table.shape[0] // count
                table[rows_at(block, size), :] = piece[row : row + size, :]
                row += size
        for table, items in zip(tables, places):
            rows = table.shape[0] // len(items)
            for j, (out, layer) in enumerate(items):
                to = outs[out] if layer is None else outs[out].at[layer]
                to[rows_at(half, rows), :] = table[j * rows : (j + 1) * rows, :].astype(F32)


def per_device(
    grid_latent, g2m_face, g2m_node, mesh_latent, mesh_links,
    w_enc, w_send, w_recv, w_node, w_dec, cotangent,
):
    tie = lax.optimization_barrier
    faces = lax.axis_size("space")
    pipe_count = lax.axis_size("pipe")
    chan_count = lax.axis_size("chan")
    grid_rows, wide = grid_latent.shape
    mesh_rows, narrow = mesh_latent.shape
    part = narrow // pipe_count
    mesh_all = faces * mesh_rows
    mix_scale = (mesh_rows / (grid_rows * pipe_count)) ** 0.5
    nbrs = mesh_links.shape[1] * pipe_count
    ids = (g2m_face.reshape(1, grid_rows), g2m_node.reshape(1, grid_rows))
    grid_vmem = 14 + mesh_all // 512

    def on(body, *fixed):
        return functools.partial(body, *fixed)

    def over_faces(blocks, step):
        return [shifted(b, "space", step * k) for k, b in enumerate(blocks) if k > 0]

    def face_parts(block):
        out = []
        for j in range(chan_count):
            mine = shifted(block, "chan", j) if j else block
            out += [mine, shifted(mine, "pipe", 1)]
        return out

    def add(parts, kind=BF16):
        return run(add_body, parts, [(parts[0].shape, kind)])[0]

    block = (mesh_rows, part)
    full = (mesh_rows, wide)
    half = wide // pipe_count
    sums = [((mesh_all, part), BF16)] * 2
    sum_flops = 2 * mesh_all * grid_rows * narrow
    edge_flops = 6 * mesh_rows * mesh_rows * nbrs * part
    parts_count = 2 * chan_count

    near = [k for k in range(1, faces) if k in (1, faces - 1)]
    far = [k for k in range(1, faces) if k not in near]

    def join(keep, give):
        return run(join_body, (keep, shifted(give, "pipe", 1)), [(block, BF16)] * faces)

    def neighbours(send_p):
        return shifted(send_p, "space", -1), shifted(send_p, "space", 1)

    def stack(blocks):
        rows, columns = blocks[0].shape
        return run(stack_body, blocks, [((len(blocks) * rows, columns), blocks[0].dtype)])[0]

    keep, give = run(
        on(encode_body, mesh_rows), (grid_latent, w_enc, *ids), sums,
        scratch=[pltpu.VMEM((grid_rows, narrow), BF16)], loads=(0, 1, 2, 3),
        flops=sum_flops + 2 * grid_rows * wide * narrow, vmem=grid_vmem,
    )
    *blocks, cotangent_late, links = tie((*join(keep, give), cotangent, mesh_links.T))
    state_part, = run(
        on(state_body, mix_scale), (mesh_latent, blocks[0], *over_faces(blocks, -1)),
        [(block, BF16)],
    )
    spot, spot_row = run(
        spot_body, (links, shifted(links, "pipe", 1)),
        [((mesh_rows, 8), jnp.int32), ((1, nbrs * mesh_rows), jnp.int32)],
    )
    state_part, spot, spot_row = tie((state_part, spot, spot_row))
    keep, give = run(
        on(sum_by_node, mesh_rows), (*ids, cotangent_late), sums, flops=sum_flops,
        vmem=grid_vmem, loads=(2,),
    )
    back_blocks = join(keep, give)
    parts = face_parts(state_part)

    def edges(send_p, recv_p, below, above):
        return run(
            edge_body, (below, send_p, above, recv_p, spot),
            [(block, BF16), ((nbrs,) + block, BF16)],
            scratch=[pltpu.VMEM((3 * mesh_rows // 2, 2 * part), BF16)], flops=edge_flops,
        )

    state_0, send_p, recv_p = run(
        first_body, (w_send, w_recv, *parts),
        [(full, BF16), (block, BF16), (block, F32)], flops=4 * mesh_rows * wide * part,
    )
    agg, slope_0 = edges(send_p, recv_p, *neighbours(send_p))
    agg, *back_blocks = tie((agg, *back_blocks))
    back_near = [shifted(back_blocks[k], "space", -k) for k in near]
    outs = tie((*face_parts(agg), *back_near))
    agg_parts, back_near = outs[:parts_count], outs[parts_count:]
    agg_0, state_1, send_p, recv_p = run(
        next_body, (state_0, w_node, w_send, w_recv, *agg_parts),
        [(full, BF16), (full, F32), (block, BF16), (block, F32)],
        flops=2 * mesh_rows * wide * wide,
    )
    back_far = [shifted(back_blocks[k], "space", -k) for k in far]
    below, above, *back_far = tie((*neighbours(send_p), *back_far))
    agg, slope_1 = edges(send_p, recv_p, below, above)
    back_parts = face_parts(add([back_blocks[0], *back_near, *back_far]))
    back_outs = [(full, F32), (block, BF16), (block, BF16), (block, F32), (block, BF16)]
    back_scratch = [pltpu.VMEM((nbrs * mesh_rows, 2 * part), BF16)]
    agg_1, last_b, dec_part, dec_grad, grad_2, recv_grad, below, own, above = run(
        on(turn_body, parts_count),
        (state_1, w_node, w_dec, slope_1, spot, spot_row, *face_parts(agg), *back_parts),
        [(full, BF16), (full, BF16), (block, BF16), (full, BF16)] + back_outs,
        scratch=back_scratch, flops=edge_flops + 6 * mesh_rows * wide * wide,
    )

    def weights(args, kinds):
        rows = half * len(kinds)
        return run(
            on(weight_body, kinds), args, [((rows // faces, narrow), BF16)] * faces,
            scratch=[pltpu.VMEM((rows, narrow), BF16)], flops=2 * mesh_rows * rows * narrow,
        )

    def from_owners(piece):
        return [piece] + [shifted(piece, "space", k) for k in range(1, faces)]

    recv_parts = face_parts(recv_grad)
    below, above = shifted(below, "space", 1), shifted(above, "space", -1)
    below, above, dec_part, *recv_parts = tie((below, above, dec_part, *recv_parts))
    dec_near = [shifted(dec_part, "space", k) for k in near]
    outs = tie((*face_parts(add([own, below, above])), *dec_near))
    send_parts, dec_near = outs[:parts_count], outs[parts_count:]
    send_1, recv_1, grad_1, recv_grad, below, own, above = run(
        on(back_body, parts_count),
        (grad_2, w_send, w_recv, w_node, slope_0, spot, spot_row, *send_parts, *recv_parts),
        [(full, BF16), (full, BF16)] + back_outs,
        scratch=back_scratch, flops=edge_flops + 4 * mesh_rows * wide * wide,
    )

    recv_parts = face_parts(recv_grad)
    below, above = shifted(below, "space", 1), shifted(above, "space", -1)
    below, above, dec_last, *recv_parts = tie((below, above, dec_part, *recv_parts))
    dec_far = [shifted(dec_last, "space", k) for k in far]
    outs = tie((*face_parts(add([own, below, above])), *dec_far))
    send_parts, dec_far = outs[:parts_count], outs[parts_count:]
    dec_all = dict(zip(near + far, [*dec_near, *dec_far]))
    dec_mine = stack([dec_part] + [dec_all[k] for k in range(1, faces)])
    dec_other = shifted(dec_mine, "pipe", 1)
    send_0, recv_0, grad_0, enc_part, enc_all = run(
        on(last_body, parts_count, mix_scale), (grad_1, w_send, w_recv, *send_parts, *recv_parts),
        [(full, BF16), (full, BF16), (full, F32), (block, BF16), (full, BF16)],
        flops=4 * mesh_rows * wide * wide,
    )

    enc_got = from_owners(enc_part)[1:]
    pieces_w = weights(
        (state_1, send_1, recv_1, agg_0, grad_1, state_0, send_0, recv_0)
        + (last_b, dec_grad, agg_1, grad_2),
        ((0, 1), (0, 2), (3, 4), (5, 6), (5, 7), (8, 9), (10, 11)),
    )
    grad_mesh, = run(pick_body, (grad_0,), [((mesh_rows, narrow), F32)], hbm=(0,))
    table = [pltpu.VMEM((mesh_all, narrow), BF16), pltpu.VMEM((1, grid_rows), jnp.int32)]
    mixed, slope_enc = run(
        mixed_body, (grid_latent, w_enc, *ids, dec_mine, dec_other),
        [((grid_rows, narrow), BF16), ((grid_rows, wide), BF16)], scratch=table, hbm=(0,),
        flops=sum_flops + 2 * grid_rows * wide * wide, vmem=grid_vmem,
    )
    outs = tie((slope_enc, grad_mesh, *enc_got, *pieces_w))
    slope_enc, grad_mesh = outs[:2]
    enc_got, pieces_w = outs[2 : 1 + faces], outs[1 + faces :]
    sums_b = add([pieces_w[0], *over_faces(pieces_w, -1)])
    enc_mine = stack(enc_got)
    enc_grad, grad_keep, grad_give = run(
        enc_own_body,
        (grid_latent, *ids, slope_enc, enc_all, enc_mine, shifted(enc_mine, "pipe", 1)),
        [((grid_rows, narrow), BF16), ((half, narrow), F32), ((half, narrow), BF16)],
        scratch=table + [pltpu.VMEM((wide, narrow), F32)],
        flops=sum_flops + 2 * grid_rows * wide * narrow, vmem=grid_vmem,
    )
    sums_g = run(
        cores_body, (grad_keep, shifted(grad_give, "pipe", 1)),
        [((half // faces, narrow), BF16)] * faces, scratch=[pltpu.VMEM((half, narrow), F32)],
    )
    *sums_g, sums_b = tie((*sums_g, sums_b))
    sums_g = add([sums_g[0], *over_faces(sums_g, -1)])
    sums_all = (sums_b, sums_g)
    reduced, = run(
        stack_all_body, sums_all, [((sum(a.shape[0] for a in sums_all), narrow), BF16)]
    )
    reduced = from_owners(reduced)
    others = chan_count - 1
    pieces = face_parts(enc_mine)[2:]
    grad_grid, = run(
        on(enc_other_body, others),
        (*ids, cotangent, enc_grad, enc_all, slope_enc, w_enc, *pieces),
        [((grid_rows, narrow), BF16)], loads=(2,),
        scratch=[pltpu.VMEM((mesh_all, narrow * others), BF16), table[1]],
        flops=(sum_flops + 4 * grid_rows * narrow * narrow) * others, vmem=grid_vmem + 4, hbm=(0,),
    )
    *reduced, grad_grid = tie((*reduced, grad_grid))
    reduced_other = [shifted(piece, "pipe", 1) for piece in reduced]
    layer_shape = ((w_send.shape[0], wide, narrow), F32)
    places = (
        ((0, 1), (1, 1), (2, 0), (0, 0), (1, 0), (3, None), (2, 1)), ((4, None),),
    )
    grad_w_send, grad_w_recv, grad_w_node, grad_w_dec, grad_w_enc = run(
        on(write_body, places), (*reduced, *reduced_other),
        [layer_shape] * 3 + [((wide, narrow), F32)] * 2, hbm=(0, 1, 2, 3, 4),
        scratch=[pltpu.VMEM((half * len(items), narrow), BF16) for items in places],
    )
    return (
        mixed,
        grad_grid,
        grad_mesh,
        grad_w_enc,
        grad_w_send,
        grad_w_recv,
        grad_w_node,
        grad_w_dec,
    )


def solution(mesh):
    nodes = ("groups", "space", "pipe")
    in_specs = (
        P(nodes, None), P(nodes, None), P(nodes), P(("groups", "space"), "chan"),
        P(("groups", "space"), "pipe"), P(), P(), P(), P(), P(), P(nodes, "chan"),
    )
    out_specs = (
        P(nodes, "chan"), P(nodes, "chan"), P(("groups", "space"), "chan"), P("groups", "chan"),
        P("groups", None, "chan"), P("groups", None, "chan"), P("groups", None, "chan"),
        P("groups", "chan"),
    )
    return jax.shard_map(
        per_device, mesh=mesh, in_specs=in_specs, out_specs=out_specs, check_vma=False
    )
```

```python
import functools

import jax
import jax.numpy as jnp
from jax import lax
from jax.experimental import pallas as pl
from jax.experimental.pallas import tpu as pltpu
from jax.sharding import PartitionSpec as P

F32, BF16 = jnp.float32, jnp.bfloat16
FACE_AXES = ("chan", "pipe")


def shifted(block, axis, distance):
    count = lax.axis_size(axis)
    return lax.ppermute(block, axis, [((i + distance) % count, i) for i in range(count)])


def dot_plain(left, right):
    return jnp.dot(left, right, preferred_element_type=F32)


def dot_back(left, right):
    return lax.dot_general(left, right, (((1,), (1,)), ((), ())), preferred_element_type=F32)


def dot_left(left, right):
    return lax.dot_general(left, right, (((0,), (0,)), ((), ())), preferred_element_type=F32)


def slope_of(values, sigmoid_v):
    return sigmoid_v * (1.0 + values * (1.0 - sigmoid_v))


def one_hot(rows, ids):
    return jnp.where(rows == ids, 1.0, 0.0).astype(BF16)


def pick(values, index, width):
    out = values[:, :width]
    for j in range(1, values.shape[1] // width):
        out = jnp.where(index == j, values[:, j * width : (j + 1) * width], out)
    return out


def in_order(first, mine, other):
    return jnp.where(first, mine, other), jnp.where(first, other, mine)


def widen(parts):
    chan, first = lax.axis_index("chan"), lax.axis_index("pipe") == 0
    count = len(parts) // 2
    pairs = [
        jnp.concatenate(in_order(first, parts[2 * j][...], parts[2 * j + 1][...]), axis=1)
        for j in range(count)
    ]
    out = []
    for place in range(count):
        block = pairs[0]
        for j in range(1, count):
            block = jnp.where(lax.rem(chan + j, count) == place, pairs[j], block)
        out.append(block)
    return jnp.concatenate(out, axis=1)


def own_quarter():
    return lax.axis_index("chan") * lax.axis_size("pipe") + lax.axis_index("pipe")


def run(body, args, outs, scratch=(), flops=0, vmem=17, hbm=(), loads=()):
    args = [
        pltpu.with_memory_space_constraint(a, pltpu.HBM if i in loads else pltpu.VMEM)
        for i, a in enumerate(args)
    ]
    return pl.pallas_call(
        body,
        out_shape=[
            jax.ShapeDtypeStruct(s, d) if i in hbm else pltpu.VMEM(s, d)
            for i, (s, d) in enumerate(outs)
        ],
        in_specs=[pl.BlockSpec(memory_space=pltpu.VMEM)] * len(args),
        out_specs=[pl.BlockSpec(memory_space=pltpu.VMEM)] * len(outs),
        scratch_shapes=list(scratch),
        compiler_params=pltpu.CompilerParams(vmem_limit_bytes=vmem * 1024 * 1024),
        cost_estimate=pl.CostEstimate(flops=flops, bytes_accessed=0, transcendentals=0),
    )(*args)


def rows_at(index, size):
    return pl.ds(pl.multiple_of(index * size, size), size)


def table_rows(mesh_rows, face_ids, node_ids):
    count = lax.axis_size("space")
    turned = face_ids - lax.axis_index("space")
    return jnp.where(turned < 0, turned + count, turned) * mesh_rows + node_ids


def sum_by_node(mesh_rows, face_ids, node_ids, values, keep, give):
    mesh_all, width = keep.shape
    grid_rows = values.shape[0]
    size = 512
    first = lax.axis_index("pipe") == 0
    target = table_rows(mesh_rows, face_ids[...], node_ids[...])

    def step(i, carry):
        ids = lax.broadcasted_iota(jnp.int32, (size, grid_rows), 0) + i * size
        total = dot_plain(one_hot(ids, target), values[...])
        mine, other = in_order(first, total[:, :width], total[:, width:])
        keep[rows_at(i, size), :] = mine.astype(BF16)
        give[rows_at(i, size), :] = other.astype(BF16)
        return carry

    lax.fori_loop(0, mesh_all // size, step, 0)


def encode_body(mesh_rows, x, w, face_ids, node_ids, keep, give, enc):
    size = 512
    columns = pick(w[...], lax.axis_index("chan"), enc.shape[1])

    def step(i, carry):
        z = dot_plain(x[rows_at(i, size), :], columns)
        enc[rows_at(i, size), :] = (z * jax.nn.sigmoid(z)).astype(BF16)
        return carry

    lax.fori_loop(0, x.shape[0] // size, step, 0)
    sum_by_node(mesh_rows, face_ids, node_ids, enc, keep, give)


def join_body(keep, got, *outs):
    rows = outs[0].shape[0]
    for k, out in enumerate(outs):
        at = slice(k * rows, (k + 1) * rows)
        out[...] = (keep[at, :].astype(F32) + got[at, :].astype(F32)).astype(BF16)


def add_all(parts):
    total = parts[0][...].astype(F32)
    for ref in parts[1:]:
        total = total + ref[...].astype(F32)
    return total


def add_body(*refs):
    refs[-1][...] = add_all(refs[:-1]).astype(refs[-1].dtype)


def state_body(mix_scale, mesh, *refs):
    own = pick(mesh[...], lax.axis_index("pipe"), refs[-1].shape[1]).astype(F32)
    refs[-1][...] = (own + mix_scale * add_all(refs[:-1])).astype(BF16)


def project(layer, state_b, w_send, w_recv, send_p, recv_p):
    width, quarter = send_p.shape[1], own_quarter()
    send_p[...] = dot_plain(state_b, pick(w_send[layer], quarter, width)).astype(BF16)
    recv_p[...] = dot_plain(state_b, pick(w_recv[layer], quarter, width))


def first_body(w_send, w_recv, *refs):
    state_0, send_p, recv_p = refs[-3:]
    wide = widen(refs[:-3])
    state_0[...] = wide
    project(0, wide, w_send, w_recv, send_p, recv_p)


def next_body(state, w_node, w_send, w_recv, *refs):
    agg_wide, new_state, send_p, recv_p = refs[-4:]
    wide = widen(refs[:-4])
    agg_wide[...] = wide
    total = state[...].astype(F32) + dot_plain(wide, w_node[0])
    new_state[...] = total
    project(1, total.astype(BF16), w_send, w_recv, send_p, recv_p)


def spot_body(mine, other, spot, spot_row):
    count, mesh_rows = mine.shape
    faces = lax.axis_size("space")
    spare = jnp.zeros((spot.shape[1] - 2 * count, mesh_rows), jnp.int32)
    links = jnp.concatenate([mine[...], other[...], spare], axis=0)
    owner = lax.div(links, mesh_rows)
    local = links - owner * mesh_rows
    step = owner - lax.axis_index("space")
    step = jnp.where(step < 0, step + faces, step)
    place = jnp.where(step == 0, mesh_rows, jnp.where(step == 1, 2 * mesh_rows, 0)) + local
    spot[...] = place.T
    for k in range(2 * count):
        spot_row[:, k * mesh_rows : (k + 1) * mesh_rows] = place[k : k + 1, :]


def stack_body(*refs):
    rows = refs[0].shape[0]
    for k, ref in enumerate(refs[:-1]):
        refs[-1][k * rows : (k + 1) * rows, :] = ref[...]


def pick_body(values, out):
    out[...] = pick(values[...], lax.axis_index("chan"), out.shape[1])


def edge_body(below, own, above, recv_p, spot, agg, slope, halo):
    mesh_rows, width = own.shape
    middle, half = mesh_rows // 2, 3 * mesh_rows // 2
    halo[:mesh_rows, :width] = below[...]
    halo[mesh_rows:, :width] = own[:middle, :]
    halo[:middle, width:] = own[middle:, :]
    halo[middle:, width:] = above[...]
    ids = lax.broadcasted_iota(jnp.int32, (mesh_rows, half), 1)
    count = slope.shape[0]
    total = jnp.zeros(agg.shape, F32)
    for k in range(count):
        place = spot[:, k : k + 1]
        right = place >= half
        both = dot_plain(one_hot(ids, jnp.where(right, place - half, place)), halo[...])
        pre = jnp.where(right, both[:, width:], both[:, :width]) + recv_p[...]
        sigmoid_v = jax.nn.sigmoid(pre)
        total = total + pre * sigmoid_v
        slope[k] = slope_of(pre, sigmoid_v).astype(BF16)
    agg[...] = (total / count).astype(BF16)


def edge_back(grad_b, w_node, slope, spot, spot_row, recv_grad, below, own, above, back):
    mesh_rows, width = recv_grad.shape
    middle, half = mesh_rows // 2, 3 * mesh_rows // 2
    count = slope.shape[0]
    back_agg = dot_back(grad_b, w_node[rows_at(own_quarter(), width), :]) / count
    total = jnp.zeros(recv_grad.shape, F32)
    for k in range(count):
        term = back_agg * slope[k].astype(F32)
        total = total + term
        right = spot[:, k : k + 1] >= half
        rows = slice(k * mesh_rows, (k + 1) * mesh_rows)
        back[rows, :width] = jnp.where(right, 0.0, term).astype(BF16)
        back[rows, width:] = jnp.where(right, term, 0.0).astype(BF16)
    recv_grad[...] = total.astype(BF16)
    place = spot_row[...]
    place = jnp.where(place >= half, place - half, place)
    ids = lax.broadcasted_iota(jnp.int32, (half, count * mesh_rows), 0)
    spread = dot_plain(one_hot(ids, place), back[...])
    below[...] = spread[:mesh_rows, :width].astype(BF16)
    own[:middle, :] = spread[mesh_rows:, :width]
    own[middle:, :] = spread[:middle, width:]
    above[...] = spread[middle:, width:].astype(BF16)


def turn_body(count, state, w_node, w_dec, slope, spot, spot_row, *refs):
    agg, back_dec = refs[:count], refs[count : 2 * count]
    agg_wide, last_b, dec_part, dec_grad, grad = refs[2 * count : 2 * count + 5]
    wide = widen(agg)
    agg_wide[...] = wide
    last = (state[...] + dot_plain(wide, w_node[1])).astype(BF16)
    last_b[...] = last
    z_dec = dot_plain(last, w_dec[...])
    sigmoid_v = jax.nn.sigmoid(z_dec)
    dec_part[...] = pick(z_dec * sigmoid_v, own_quarter(), dec_part.shape[1]).astype(BF16)
    down = (widen(back_dec).astype(F32) * slope_of(z_dec, sigmoid_v)).astype(BF16)
    dec_grad[...] = down
    total = dot_back(down, w_dec[...])
    grad[...] = total
    edge_back(total.astype(BF16), w_node.at[1], slope, spot, spot_row, *refs[2 * count + 5 :])


def through(layer, grad, w_send, w_recv, send_parts, recv_parts, send_wide, recv_wide):
    send, recv = widen(send_parts), widen(recv_parts)
    send_wide[...] = send
    recv_wide[...] = recv
    return grad[...] + dot_back(send, w_send[layer]) + dot_back(recv, w_recv[layer])


def back_body(count, grad, w_send, w_recv, w_node, slope, spot, spot_row, *refs):
    send_parts, recv_parts = refs[:count], refs[count : 2 * count]
    send_wide, recv_wide, new_grad = refs[2 * count : 2 * count + 3]
    total = through(1, grad, w_send, w_recv, send_parts, recv_parts, send_wide, recv_wide)
    new_grad[...] = total
    edge_back(total.astype(BF16), w_node.at[0], slope, spot, spot_row, *refs[2 * count + 3 :])


def last_body(count, mix_scale, grad_1, w_send, w_recv, *refs):
    send_parts, recv_parts = refs[:count], refs[count : 2 * count]
    send_wide, recv_wide, grad, enc_part, enc_all = refs[2 * count :]
    total = through(0, grad_1, w_send, w_recv, send_parts, recv_parts, send_wide, recv_wide)
    grad[...] = total
    scaled = (mix_scale * total).astype(BF16)
    enc_part[...] = pick(scaled, own_quarter(), enc_part.shape[1])
    enc_all[...] = scaled


def put_pair(table, row, column, mine, other):
    rows, width = mine.shape
    low, high = in_order(lax.axis_index("pipe") == 0, mine[...], other[...])
    table[row : row + rows, column : column + width] = low
    table[row : row + rows, column + width : column + 2 * width] = high


def node_values(target, at, table):
    ids = lax.broadcasted_iota(jnp.int32, (table.shape[0], at.size), 0)
    return dot_left(one_hot(ids, target[:, at]), table[...])


def mixed_body(x, w, face_ids, node_ids, mine, other, mixed, slope, table, target):
    put_pair(table, 0, 0, mine, other)
    mesh_rows = mine.shape[0] // lax.axis_size("space")
    target[...] = table_rows(mesh_rows, face_ids[...], node_ids[...])
    size = 512
    chan = lax.axis_index("chan")

    def step(i, carry):
        at = rows_at(i, size)
        got = node_values(target, at, table)
        rows = x[at, :]
        mixed[at, :] = (pick(rows, chan, mixed.shape[1]).astype(F32) + got).astype(BF16)
        z = dot_plain(rows, w[...])
        slope[at, :] = slope_of(z, jax.nn.sigmoid(z)).astype(BF16)
        return carry

    lax.fori_loop(0, x.shape[0] // size, step, 0)


def enc_own_body(
    x, face_ids, node_ids, slope, enc_all, mine, other,
    enc_grad, grad_keep, grad_give, table, target, total,
):
    mesh_rows = enc_all.shape[0]
    chan, pipe = lax.axis_index("chan"), lax.axis_index("pipe")
    table[:mesh_rows, :] = pick(enc_all[...], chan, table.shape[1])
    put_pair(table, mesh_rows, 0, mine, other)
    target[...] = table_rows(mesh_rows, face_ids[...], node_ids[...])
    size = 512
    total[...] = jnp.zeros(total.shape, F32)

    def step(i, carry):
        at = rows_at(i, size)
        own = pick(slope[at, :], chan, enc_grad.shape[1]).astype(F32)
        down = (node_values(target, at, table) * own).astype(BF16)
        enc_grad[at, :] = down
        total[...] += dot_left(x[at, :], down)
        return carry

    lax.fori_loop(0, x.shape[0] // size, step, 0)
    half = grad_keep.shape[0]
    grad_keep[...] = total[rows_at(pipe, half), :]
    grad_give[...] = total[rows_at(1 - pipe, half), :].astype(BF16)


def enc_other_body(count, face_ids, node_ids, cotangent, enc_grad, enc_all, slope, w, *refs):
    blocks = refs[:-3]
    grad_grid, table, target = refs[-3:]
    grid_rows, narrow = cotangent.shape
    mesh_rows = enc_all.shape[0]
    chan = lax.axis_index("chan")
    for j in range(count):
        other = lax.rem(chan + 1 + j, count + 1)
        columns = slice(j * narrow, (j + 1) * narrow)
        table[:mesh_rows, columns] = pick(enc_all[...], other, narrow)
        put_pair(table, mesh_rows, j * narrow, blocks[2 * j], blocks[2 * j + 1])
    target[...] = table_rows(mesh_rows, face_ids[...], node_ids[...])
    size = 512
    w_rows = w[rows_at(chan, narrow), :]
    own_block = pick(w_rows, chan, narrow)

    def step(i, carry):
        at = rows_at(i, size)
        got = node_values(target, at, table)
        total = cotangent[at, :].astype(F32) + dot_back(enc_grad[at, :], own_block)
        for j in range(count):
            other = lax.rem(chan + 1 + j, count + 1)
            part = got[:, j * narrow : (j + 1) * narrow]
            down = (part * pick(slope[at, :], other, narrow).astype(F32)).astype(BF16)
            total = total + dot_back(down, pick(w_rows, other, narrow))
        grad_grid[at, :] = total.astype(BF16)
        return carry

    lax.fori_loop(0, grid_rows // size, step, 0)


def cut_by_face(table, outs):
    count, size = len(outs), outs[0].shape[0]
    face = lax.axis_index("space")
    for k, out in enumerate(outs):
        out[...] = table[rows_at(lax.rem(face + k, count), size), :].astype(out.dtype)


def weight_body(kinds, *refs):
    outs, table = refs[-1 - lax.axis_size("space") : -1], refs[-1]
    rows = table.shape[0] // len(kinds)
    chan, pipe = lax.axis_index("chan"), lax.axis_index("pipe")
    for i, (left, right) in enumerate(kinds):
        one = pick(refs[left][...].astype(BF16), pipe, rows)
        two = pick(refs[right][...].astype(BF16), chan, table.shape[1])
        table[i * rows : (i + 1) * rows, :] = dot_left(one, two).astype(BF16)
    cut_by_face(table, outs)


def cores_body(keep, got, *refs):
    count, table = len(refs) // 2, refs[-1]
    face, size = lax.axis_index("space"), table.shape[0] // count
    table[...] = keep[...] + got[...].astype(F32)
    for k in range(count):
        piece, out = refs[k], refs[count + k]
        rows = piece.shape[0]
        out[:rows, :] = piece[...]
        out[rows:, :] = table[rows_at(lax.rem(face + k, count), size), :].astype(BF16)


def stack_all_body(*refs):
    row = 0
    for ref in refs[:-1]:
        rows = ref.shape[0]
        refs[-1][row : row + rows, :] = ref[...]
        row += rows


def write_body(places, *refs):
    count = lax.axis_size("space")
    outs, tables = refs[2 * count : -len(places)], refs[-len(places) :]
    pipe, face = lax.axis_index("pipe"), lax.axis_index("space")
    for side in range(2):
        half = pipe if side == 0 else 1 - pipe
        for k in range(count):
            piece = refs[side * count + k]
            block = lax.rem(face + k, count)
            row = 0
            for table in tables:
                size = table.shape[0] // count
                table[rows_at(block, size), :] = piece[row : row + size, :]
                row += size
        for table, items in zip(tables, places):
            rows = table.shape[0] // len(items)
            for j, (out, layer) in enumerate(items):
                to = outs[out] if layer is None else outs[out].at[layer]
                to[rows_at(half, rows), :] = table[j * rows : (j + 1) * rows, :].astype(F32)


def per_device(
    grid_latent, g2m_face, g2m_node, mesh_latent, mesh_links,
    w_enc, w_send, w_recv, w_node, w_dec, cotangent,
):
    tie = lax.optimization_barrier
    faces = lax.axis_size("space")
    pipe_count = lax.axis_size("pipe")
    chan_count = lax.axis_size("chan")
    grid_rows, wide = grid_latent.shape
    mesh_rows, narrow = mesh_latent.shape
    part = narrow // pipe_count
    mesh_all = faces * mesh_rows
    mix_scale = (mesh_rows / (grid_rows * pipe_count)) ** 0.5
    nbrs = mesh_links.shape[1] * pipe_count
    ids = (g2m_face.reshape(1, grid_rows), g2m_node.reshape(1, grid_rows))
    grid_vmem = 14 + mesh_all // 512

    def on(body, *fixed):
        return functools.partial(body, *fixed)

    def over_faces(blocks, step):
        return [shifted(b, "space", step * k) for k, b in enumerate(blocks) if k > 0]

    def face_parts(block):
        out = []
        for j in range(chan_count):
            mine = shifted(block, "chan", j) if j else block
            out += [mine, shifted(mine, "pipe", 1)]
        return out

    def other_chans(block):
        out = []
        for j in range(1, chan_count):
            for t in range(pipe_count):
                route = [
                    ((c + j) % chan_count * pipe_count + (p + t) % pipe_count, c * pipe_count + p)
                    for c in range(chan_count)
                    for p in range(pipe_count)
                ]
                out.append(lax.ppermute(block, FACE_AXES, route))
        return out

    def add(parts, kind=BF16):
        return run(add_body, parts, [(parts[0].shape, kind)])[0]

    block = (mesh_rows, part)
    full = (mesh_rows, wide)
    half = wide // pipe_count
    sums = [((mesh_all, part), BF16)] * 2
    sum_flops = 2 * mesh_all * grid_rows * narrow
    edge_flops = 6 * mesh_rows * mesh_rows * nbrs * part
    parts_count = 2 * chan_count

    near = [k for k in range(1, faces) if k in (1, faces - 1)]
    far = [k for k in range(1, faces) if k not in near]

    def join(keep, give):
        return run(join_body, (keep, shifted(give, "pipe", 1)), [(block, BF16)] * faces)

    def neighbours(send_p):
        return shifted(send_p, "space", -1), shifted(send_p, "space", 1)

    def stack(blocks):
        rows, columns = blocks[0].shape
        return run(stack_body, blocks, [((len(blocks) * rows, columns), blocks[0].dtype)])[0]

    keep, give = run(
        on(encode_body, mesh_rows), (grid_latent, w_enc, *ids), sums,
        scratch=[pltpu.VMEM((grid_rows, narrow), BF16)], loads=(0, 1, 2, 3),
        flops=sum_flops + 2 * grid_rows * wide * narrow, vmem=grid_vmem,
    )
    *blocks, cotangent_late, links = tie((*join(keep, give), cotangent, mesh_links.T))
    state_part, = run(
        on(state_body, mix_scale), (mesh_latent, blocks[0], *over_faces(blocks, -1)),
        [(block, BF16)],
    )
    spot, spot_row = run(
        spot_body, (links, shifted(links, "pipe", 1)),
        [((mesh_rows, 8), jnp.int32), ((1, nbrs * mesh_rows), jnp.int32)],
    )
    state_part, spot, spot_row = tie((state_part, spot, spot_row))
    keep, give = run(
        on(sum_by_node, mesh_rows), (*ids, cotangent_late), sums, flops=sum_flops,
        vmem=grid_vmem, loads=(2,),
    )
    back_blocks = join(keep, give)
    parts = face_parts(state_part)

    def edges(send_p, recv_p, below, above):
        return run(
            edge_body, (below, send_p, above, recv_p, spot),
            [(block, BF16), ((nbrs,) + block, BF16)],
            scratch=[pltpu.VMEM((3 * mesh_rows // 2, 2 * part), BF16)], flops=edge_flops,
        )

    state_0, send_p, recv_p = run(
        first_body, (w_send, w_recv, *parts),
        [(full, BF16), (block, BF16), (block, F32)], flops=4 * mesh_rows * wide * part,
    )
    agg, slope_0 = edges(send_p, recv_p, *neighbours(send_p))
    agg, *back_blocks = tie((agg, *back_blocks))
    back_near = [shifted(back_blocks[k], "space", -k) for k in near]
    outs = tie((*face_parts(agg), *back_near))
    agg_parts, back_near = outs[:parts_count], outs[parts_count:]
    agg_0, state_1, send_p, recv_p = run(
        next_body, (state_0, w_node, w_send, w_recv, *agg_parts),
        [(full, BF16), (full, F32), (block, BF16), (block, F32)],
        flops=2 * mesh_rows * wide * wide,
    )
    back_far = [shifted(back_blocks[k], "space", -k) for k in far]
    below, above, *back_far = tie((*neighbours(send_p), *back_far))
    agg, slope_1 = edges(send_p, recv_p, below, above)
    back_parts = face_parts(add([back_blocks[0], *back_near, *back_far]))
    back_outs = [(full, F32), (block, BF16), (block, BF16), (block, F32), (block, BF16)]
    back_scratch = [pltpu.VMEM((nbrs * mesh_rows, 2 * part), BF16)]
    agg_1, last_b, dec_part, dec_grad, grad_2, recv_grad, below, own, above = run(
        on(turn_body, parts_count),
        (state_1, w_node, w_dec, slope_1, spot, spot_row, *face_parts(agg), *back_parts),
        [(full, BF16), (full, BF16), (block, BF16), (full, BF16)] + back_outs,
        scratch=back_scratch, flops=edge_flops + 6 * mesh_rows * wide * wide,
    )

    def weights(args, kinds):
        rows = half * len(kinds)
        return run(
            on(weight_body, kinds), args, [((rows // faces, narrow), BF16)] * faces,
            scratch=[pltpu.VMEM((rows, narrow), BF16)], flops=2 * mesh_rows * rows * narrow,
        )

    def from_owners(piece):
        return [piece] + [shifted(piece, "space", k) for k in range(1, faces)]

    recv_parts = face_parts(recv_grad)
    below, above = shifted(below, "space", 1), shifted(above, "space", -1)
    below, above, dec_part, *recv_parts = tie((below, above, dec_part, *recv_parts))
    dec_near = [shifted(dec_part, "space", k) for k in near]
    outs = tie((*face_parts(add([own, below, above])), *dec_near))
    send_parts, dec_near = outs[:parts_count], outs[parts_count:]
    send_1, recv_1, grad_1, recv_grad, below, own, above = run(
        on(back_body, parts_count),
        (grad_2, w_send, w_recv, w_node, slope_0, spot, spot_row, *send_parts, *recv_parts),
        [(full, BF16), (full, BF16)] + back_outs,
        scratch=back_scratch, flops=edge_flops + 4 * mesh_rows * wide * wide,
    )

    recv_parts = face_parts(recv_grad)
    below, above = shifted(below, "space", 1), shifted(above, "space", -1)
    below, above, dec_last, *recv_parts = tie((below, above, dec_part, *recv_parts))
    dec_far = [shifted(dec_last, "space", k) for k in far]
    outs = tie((*face_parts(add([own, below, above])), *dec_far))
    send_parts, dec_far = outs[:parts_count], outs[parts_count:]
    dec_all = dict(zip(near + far, [*dec_near, *dec_far]))
    dec_mine = stack([dec_part] + [dec_all[k] for k in range(1, faces)])
    dec_other = shifted(dec_mine, "pipe", 1)
    send_0, recv_0, grad_0, enc_part, enc_all = run(
        on(last_body, parts_count, mix_scale), (grad_1, w_send, w_recv, *send_parts, *recv_parts),
        [(full, BF16), (full, BF16), (full, F32), (block, BF16), (full, BF16)],
        flops=4 * mesh_rows * wide * wide,
    )

    enc_got = from_owners(enc_part)[1:]
    pieces_w = weights(
        (state_1, send_1, recv_1, agg_0, grad_1, last_b, dec_grad),
        ((0, 1), (0, 2), (3, 4), (5, 6)),
    )
    pieces_c = weights((state_0, send_0, recv_0, agg_1, grad_2), ((0, 1), (0, 2), (3, 4)))
    grad_mesh, = run(pick_body, (grad_0,), [((mesh_rows, narrow), F32)], hbm=(0,))
    table = [pltpu.VMEM((mesh_all, narrow), BF16), pltpu.VMEM((1, grid_rows), jnp.int32)]
    mixed, slope_enc = run(
        mixed_body, (grid_latent, w_enc, *ids, dec_mine, dec_other),
        [((grid_rows, narrow), BF16), ((grid_rows, wide), BF16)], scratch=table, hbm=(0,),
        flops=sum_flops + 2 * grid_rows * wide * wide, vmem=grid_vmem,
    )
    outs = tie((slope_enc, grad_mesh, *enc_got, *pieces_w, *pieces_c))
    slope_enc, grad_mesh = outs[:2]
    enc_got, pieces_w = outs[2 : 1 + faces], outs[1 + faces : 1 + 2 * faces]
    pieces_c = outs[1 + 2 * faces :]
    sums_b = add([pieces_w[0], *over_faces(pieces_w, -1)])
    enc_mine = stack(enc_got)
    enc_grad, grad_keep, grad_give = run(
        enc_own_body,
        (grid_latent, *ids, slope_enc, enc_all, enc_mine, shifted(enc_mine, "pipe", 1)),
        [((grid_rows, narrow), BF16), ((half, narrow), F32), ((half, narrow), BF16)],
        scratch=table + [pltpu.VMEM((wide, narrow), F32)],
        flops=sum_flops + 2 * grid_rows * wide * narrow, vmem=grid_vmem,
    )
    sums_g = run(
        cores_body, (grad_keep, shifted(grad_give, "pipe", 1), *pieces_c),
        [((pieces_c[0].shape[0] + half // faces, narrow), BF16)] * faces, scratch=[pltpu.VMEM((half, narrow), F32)],
    )
    *sums_g, sums_b = tie((*sums_g, sums_b))
    sums_g = add([sums_g[0], *over_faces(sums_g, -1)])
    sums_all = (sums_b, sums_g)
    reduced, = run(
        stack_all_body, sums_all, [((sum(a.shape[0] for a in sums_all), narrow), BF16)]
    )
    reduced = from_owners(reduced)
    others = chan_count - 1
    pieces = other_chans(enc_mine)
    grad_grid, = run(
        on(enc_other_body, others),
        (*ids, cotangent, enc_grad, enc_all, slope_enc, w_enc, *pieces),
        [((grid_rows, narrow), BF16)], loads=(2,),
        scratch=[pltpu.VMEM((mesh_all, narrow * others), BF16), table[1]],
        flops=(sum_flops + 4 * grid_rows * narrow * narrow) * others, vmem=grid_vmem + 4, hbm=(0,),
    )
    *reduced_far, grad_grid = tie((*(reduced[k] for k in far), grad_grid))
    for k, piece in zip(far, reduced_far):
        reduced[k] = piece
    reduced_other = [shifted(piece, "pipe", 1) for piece in reduced]
    layer_shape = ((w_send.shape[0], wide, narrow), F32)
    places = (
        ((0, 1), (1, 1), (2, 0), (3, None)), ((0, 0), (1, 0), (2, 1)), ((4, None),),
    )
    grad_w_send, grad_w_recv, grad_w_node, grad_w_dec, grad_w_enc = run(
        on(write_body, places), (*reduced, *reduced_other),
        [layer_shape] * 3 + [((wide, narrow), F32)] * 2, hbm=(0, 1, 2, 3, 4),
        scratch=[pltpu.VMEM((half * len(items), narrow), BF16) for items in places],
    )
    return (
        mixed,
        grad_grid,
        grad_mesh,
        grad_w_enc,
        grad_w_send,
        grad_w_recv,
        grad_w_node,
        grad_w_dec,
    )


def solution(mesh):
    nodes = ("groups", "space", "pipe")
    in_specs = (
        P(nodes, None), P(nodes, None), P(nodes), P(("groups", "space"), "chan"),
        P(("groups", "space"), "pipe"), P(), P(), P(), P(), P(), P(nodes, "chan"),
    )
    out_specs = (
        P(nodes, "chan"), P(nodes, "chan"), P(("groups", "space"), "chan"), P("groups", "chan"),
        P("groups", None, "chan"), P("groups", None, "chan"), P("groups", None, "chan"),
        P("groups", "chan"),
    )
    return jax.shard_map(
        per_device, mesh=mesh, in_specs=in_specs, out_specs=out_specs, check_vma=False
    )
```
